128 devices in a mesh: seq: 4 (over x), fsdp: 32 (over z, y, core).
Axes of the slice: x: 4, y: 4, z: 4, core: 2. Of those that a mesh axis runs over, the one named last changes fastest.
Arguments:
- hidden: bfloat16 [32, 1536, 768], P('fsdp', 'seq'), may hold values from -6 to 6
- lengths: int32 [32, 4], P('fsdp'), may hold values from 1 to 1344, 1536 in all within a row
- attn_gain: bfloat16 [768], P('fsdp'), may hold values from 0.5 to 1.5
- w_qkv: bfloat16 [768, 2304], P('fsdp'), may hold values from -0.21875 to 0.21875
- w_attn_out: bfloat16 [768, 768], P('fsdp'), may hold values from -1.75 to 1.75
- mlp_gain: bfloat16 [768], P('fsdp'), may hold values from 0.5 to 1.5
- w_in: bfloat16 [768, 2304], P('fsdp'), may hold values from -0.21875 to 0.21875
- w_mlp_out: bfloat16 [1152, 768], P('fsdp'), may hold values from -0.1875 to 0.1875
- cotangent: bfloat16 [32, 1536, 768], P('fsdp', 'seq'), may hold values from -6 to 6
Outputs:
- output: bfloat16 [32, 1536, 768], P('fsdp', 'seq')
- input_grad: float32 [32, 1536, 768], P('fsdp', 'seq')
- grad_attn_gain: float32 [768], P('fsdp')
- grad_qkv_weight: float32 [768, 2304], P('fsdp', 'seq')
- grad_attn_out: float32 [768, 768], P('fsdp', 'seq')
- grad_mlp_gain: float32 [768], P('fsdp')
- grad_w_in: float32 [768, 2304], P('fsdp', 'seq')
- grad_mlp_out: float32 [1152, 768], P('fsdp', 'seq')
The draws below stay inside these ranges and needn't reach their ends.
Inputs may be any that keep to these rules, and one draw needn't show every extreme that they name: `lengths`: each row sums to 1536; its largest entry is exactly 1344.
All inputs are finite; a program needn't handle non-finite values.
Results may differ from the reference program's by a relative error of at most 0.017.
Values may be sent and summed in bfloat16 or wider, within the bound.
A program may use at most 128 MiB of HBM per device.

```python
import math
import jax
import jax.numpy as jnp
import numpy as np
from jax import lax

D = 768
HEADS = 12
HEAD_DIM = 64
FF = 1152
DOCS = 4
GROUPS = 32
PACK = 1536
LONGEST = 1344


def raised(values, rng, source, target, blocks, factor):
    owner, partner = [(jnp.arange(values.shape[dim]) // (values.shape[dim] // blocks)).reshape([-1 if axis == dim else 1 for axis in range(values.ndim)]) for dim in (source, target)]
    chosen = jax.random.permutation(rng, blocks)[partner]
    strong = (owner == chosen) | (owner == (partner + blocks // 2) % blocks)
    return jnp.where(strong, factor * values, values)


def level_of(key, dims, shards, smallest, high):
    def one(dim, blocks):
        heights = jax.random.uniform(jax.random.fold_in(jax.random.fold_in(key, 6), dim), (blocks,), jnp.float32, smallest / len(shards), high / len(shards))
        return jnp.repeat(jnp.exp(heights), dims[dim] // blocks).reshape((-1,) + (1,) * (len(dims) - dim - 1))

    level = one(*shards[0])
    for cut in shards[1:]:
        level = level * one(*cut)
    return level


def split_up(amount, total, limit, slope):
    loads = [(1 << 20) // math.isqrt(standing ** slope) + 1 for standing in range(2, amount + 1)]
    surplus, counts = total - limit - (amount - 1), [1] * (amount - 1)
    while surplus > 0:
        free = [i for i in range(amount - 1) if counts[i] < limit]
        mass, remaining = sum([loads[i] for i in free]), surplus
        for i in free:
            more = min(limit - counts[i], max(1, remaining * loads[i] // mass), surplus)
            counts[i] = counts[i] + more
            surplus = surplus - more
    return np.array([limit] + counts)


def uneven_parts(rng, number_of, total, most, skew):
    if number_of == 2:
        one = jax.random.randint(rng, (), max(1, total - most), min(most, total - 1) + 1)
        return jnp.stack([one, total - one])
    sizes = jnp.asarray(split_up(number_of, total, most, skew), jnp.int32)
    twos = (number_of - 1) // 2
    source_of, sink = sizes[1:1 + 2 * twos:2], sizes[2:2 + 2 * twos:2]
    room = jnp.minimum(source_of - 1, most - sink)
    passed = jax.random.randint(jax.random.fold_in(rng, 1), (twos,), 0, 1 << 20) % (room + 1)
    sizes = sizes.at[1:1 + 2 * twos:2].set(source_of - passed).at[2:2 + 2 * twos:2].set(sink + passed)
    return sizes[jax.random.permutation(jax.random.fold_in(rng, 2), number_of)]


def scatter_about(key, shape, width, limit, cuts=(), kind=jnp.bfloat16):
    level = level_of(key, shape, cuts, -0.22, 0.18) if cuts else 1.0
    drawn = jax.random.normal(key, shape, jnp.float32) * width * level
    return jnp.minimum(jnp.maximum(drawn, -limit), limit).astype(kind)


def heavy_noise(own_key, shape, width, bound, split, heavy, kind=jnp.bfloat16):
    entries = width * jax.random.normal(own_key, shape, jnp.float32)
    if split:
        entries = entries * level_of(own_key, shape, split, -0.22, 0.18)
    return jnp.clip(raised(entries, jax.random.fold_in(own_key, 3), *heavy), -bound, bound).astype(kind)


def setup_inputs(seed: int = 0) -> dict:
    splits = jax.random.split(jax.random.key(seed), 10)
    return {
        "hidden": heavy_noise(splits[0], (GROUPS, PACK, D), 1.0, 6.0, ((0, 32), (1, 4)), (0, 2, 32, 2.75)),
        "lengths": jax.vmap(lambda own: uneven_parts(own, DOCS, PACK, LONGEST, 2))(jax.random.split(splits[1], GROUPS)).reshape((GROUPS, DOCS)).astype(jnp.int32),
        "attn_gain": jnp.clip(1.0 + 0.1 * jax.random.normal(splits[2], (D,), jnp.float32), 0.5, 1.5).astype(jnp.bfloat16),
        "w_qkv": scatter_about(splits[3], (D, 3 * D), D ** -0.5, 0.21875, ((0, 32),)),
        "w_attn_out": scatter_about(splits[4], (D, D), (max(D // 64, 1)) ** -0.5, 1.75, ((0, 32),)),
        "mlp_gain": jnp.clip(1.0 + 0.1 * jax.random.normal(splits[5], (D,), jnp.float32), 0.5, 1.5).astype(jnp.bfloat16),
        "w_in": scatter_about(splits[6], (D, 2 * FF), D ** -0.5, 0.21875, ((0, 32),)),
        "w_mlp_out": scatter_about(splits[7], (FF, D), FF ** -0.5, 0.1875, ((0, 32),)),
        "cotangent": scatter_about(splits[8], (GROUPS, PACK, D), 1.0, 6.0, ((0, 32), (1, 4))),
    }


@jax.custom_vjp
def low(v):
    return lax.optimization_barrier(v.astype(jnp.bfloat16)).astype(jnp.float32)

@jax.custom_vjp
def low_back(v):
    return v

def low_keep(v):
    return (low(v), None)

def low_pass(kept, grad):
    return (grad,)

def back_keep(v):
    return (v, None)

def back_low(kept, grad):
    return (low(grad),)
low.defvjp(low_keep, low_pass)
low_back.defvjp(back_keep, back_low)
precise = lax.Precision.HIGHEST

def norm_stats(values):
    average = lax.optimization_barrier(jnp.mean(values, axis=-1, keepdims=True))
    centred = values - average
    variance = lax.optimization_barrier(jnp.mean(centred * centred, axis=-1, keepdims=True))
    return centred * lax.rsqrt(variance + 1e-05)

def doc_tables(lengths, places, head_dim):
    doc_ends = jnp.cumsum(lengths).astype(jnp.int32)
    starts = (doc_ends - lengths).astype(jnp.int32)
    member = (places[:, None] >= starts[None, :]) & (places[:, None] < doc_ends[None, :])
    numbers = jnp.arange(lengths.shape[0], dtype=jnp.int32)
    segment = lax.optimization_barrier(jnp.sum(jnp.where(member, numbers[None, :], 0), axis=1)).astype(jnp.int32)
    offset = lax.optimization_barrier(jnp.sum(jnp.where(member, starts[None, :], 0), axis=1)).astype(jnp.int32)
    position = (places - offset).astype(jnp.float32)
    halfway = head_dim // 2
    inverse = jnp.exp(jnp.arange(halfway, dtype=jnp.float32) * (-2.0 * math.log(160000.0) / head_dim))
    angles = position[:, None] * inverse[None, :]
    angles = jnp.concatenate([angles, angles], axis=-1)
    return (segment, jnp.cos(angles), jnp.sin(angles))

def rotate(values, cosine, sine_table):
    halfway = values.shape[-1] // 2
    turned = jnp.concatenate([-values[..., halfway:], values[..., :halfway]], axis=-1)
    return values * cosine[:, None, :] + turned * sine_table[:, None, :]

def attend(query_rot, key_rot, value_low, segment):
    score_scale = HEAD_DIM ** (-0.5)
    raw_scores = jnp.einsum('qhd,khd->hqk', query_rot, key_rot, precision=precise) * score_scale
    scores = low_back(raw_scores)
    same_doc = segment[:, None] == segment[None, :]
    scores = jnp.where(same_doc[None], scores, -1000000000.0)
    highest = lax.optimization_barrier(jnp.max(scores, axis=-1, keepdims=True))
    weights = jnp.exp(scores - highest)
    shares = low(weights / lax.optimization_barrier(jnp.sum(weights, axis=-1, keepdims=True)))
    return jnp.einsum('hqk,khd->qhd', shares, value_low, precision=precise)

def pack_forward(params, pack_rows, pack_lengths):
    attn_gain, w_qkv, w_attn_out, mlp_gain, w_in, w_mlp_out = params
    places = jnp.arange(PACK, dtype=jnp.int32)
    segment, cosine, sine_table = doc_tables(pack_lengths, places, HEAD_DIM)
    attn_in = low(norm_stats(pack_rows) * attn_gain)
    qkv = low_back(jnp.dot(attn_in, w_qkv, precision=precise))
    query = qkv[:, :D].reshape(PACK, HEADS, HEAD_DIM)
    key_part = qkv[:, D:2 * D].reshape(PACK, HEADS, HEAD_DIM)
    value_part = qkv[:, 2 * D:].reshape(PACK, HEADS, HEAD_DIM)
    query_rot = low(low_back(rotate(query, cosine, sine_table)))
    key_rot = low(low_back(rotate(key_part, cosine, sine_table)))
    value_low = low(value_part)

    def attention(query_in, key_in, value_in):
        return attend(query_in, key_in, value_in, segment)
    mixed = jax.checkpoint(attention)(query_rot, key_rot, value_low)
    attn_mix = low(low_back(mixed.reshape(PACK, D)))
    residual = pack_rows + low_back(jnp.dot(attn_mix, w_attn_out, precision=precise))
    mlp_in = low(norm_stats(residual) * mlp_gain)
    projected = low_back(jnp.dot(mlp_in, w_in, precision=precise))
    activated = low(jax.nn.gelu(projected[:, :FF], approximate=False) * projected[:, FF:])
    return residual + low_back(jnp.dot(activated, w_mlp_out, precision=precise))

def reference(hidden, lengths, attn_gain, w_qkv, w_attn_out, mlp_gain, w_in, w_mlp_out, cotangent):
    weights_in = tuple((item.astype(jnp.float32) for item in (attn_gain, w_qkv, w_attn_out, mlp_gain, w_in, w_mlp_out)))

    def forward(inputs, *params):

        def advance(carried, pair):
            return (carried, pack_forward(params, pair[0], pair[1]))
        unused, result = lax.scan(advance, jnp.zeros((), jnp.float32), (inputs, lengths))
        return result
    result, pullback = jax.vjp(forward, hidden.astype(jnp.float32), *weights_in)
    gradients = pullback(cotangent.astype(jnp.float32))
    return (result.astype(jnp.bfloat16), gradients[0], gradients[1], gradients[2], gradients[3], gradients[4], gradients[5], gradients[6])
```

```python
import math

import jax
import jax.numpy as jnp
from jax import lax
from jax.experimental import pallas as pl
from jax.experimental.pallas import tpu as pltpu
from jax.sharding import PartitionSpec as P

HEADS = 12
HEAD_DIM = 64
LONGEST = 1344
SEQ = 4
LOCAL = 3
TOK = 384
HALF = 192
PACK = 1536
F32 = jnp.float32
BF16 = jnp.bfloat16
VMEM_LIMIT = 60 * 1024 * 1024


def mm(left, right):
    return jnp.dot(left, right, preferred_element_type=F32)


def mm_nt(left, right):
    return lax.dot_general(left, right, (((1,), (1,)), ((), ())), preferred_element_type=F32)


def mm_tn(left, right):
    return lax.dot_general(left, right, (((0,), (0,)), ((), ())), preferred_element_type=F32)


def iota(shape, dim):
    return lax.broadcasted_iota(jnp.int32, shape, dim)


def roll(x, shift):
    return pltpu.roll(x, shift, 1)


def low_lanes(rows):
    return iota((rows, 128), 1) < 64


def turned(x):
    lane = iota(x.shape, 1)
    first = (lane & 32) == 0
    return jnp.where(first, roll(x, 96), roll(x, 32))


def norm_parts(values):
    average = jnp.mean(values, axis=-1, keepdims=True)
    centred = values - average
    variance = jnp.mean(centred * centred, axis=-1, keepdims=True)
    scale = lax.rsqrt(variance + 1e-05)
    return centred * scale, scale


def doc_bounds(len_ref):
    first = len_ref[0]
    second = first + len_ref[1]
    third = second + len_ref[2]
    start = jnp.where(
        len_ref[0] == LONGEST,
        0,
        jnp.where(len_ref[1] == LONGEST, first, jnp.where(len_ref[2] == LONGEST, second, third)),
    )
    return first, second, third, start


def edge_order(start, transposed):
    stored = iota((2 * HALF, 2 * HALF), 1 if transposed else 0)
    edge = iota((2 * HALF, 2 * HALF), 0 if transposed else 1)
    source = stored + (HALF + start)
    source = jnp.where(source >= 2 * HALF, source - 2 * HALF, source)
    return jnp.where(edge == source, 1.0, 0.0).astype(BF16)


def short_mask(bounds):
    first, second, third, start = bounds

    def numbers(dim):
        row = iota((HALF, HALF), dim) + (HALF + start)
        row = jnp.where(row >= 2 * HALF, row - 2 * HALF, row)
        place = jnp.where(row >= HALF, row + (PACK - 2 * HALF), row)
        return (
            jnp.where(place >= first, 1, 0)
            + jnp.where(place >= second, 1, 0)
            + jnp.where(place >= third, 1, 0)
        )

    return numbers(0) == numbers(1)


def extra_lanes(base, column):
    lane = iota(base.shape, 1)
    rest = -column
    top = rest.astype(BF16).astype(F32)
    rest = rest - top
    middle = rest.astype(BF16).astype(F32)
    rest = rest - middle
    return jnp.where(
        lane < 64,
        base,
        jnp.where(lane == 64, top, jnp.where(lane == 65, middle, jnp.where(lane == 66, rest, 0.0))),
    )


def permute_edge(order, ref, head):
    edge = jnp.concatenate([ref[head, 0:HALF, :], ref[head, PACK - HALF : PACK, :]], axis=0)
    moved = mm(order, edge).astype(BF16)
    return moved[0:HALF], moved[HALF : 2 * HALF]


def pack_halves(top, bottom):
    return jnp.where(low_lanes(top.shape[0]), top, roll(bottom, 64))


def project_block(block, hid_ref, w_ref, cos_ref, sin_ref, q_ref, k_ref, v_ref, xt_ref):
    rows = pl.ds(pl.multiple_of(block * TOK, TOK), TOK)
    xhat = norm_parts(hid_ref[block].astype(F32))[0].astype(BF16)
    xt_ref[block] = jnp.transpose(xhat)
    qkv = mm(xhat, w_ref[...])
    cosine, sine = cos_ref[rows, :], sin_ref[rows, :]
    lane = iota((TOK, 128), 1)
    low = lane < 64
    ones = jnp.where(lane < 67, 1.0, 0.0)
    for chunk in range(5):
        part = qkv[:, 128 * chunk : min(128 * chunk + 128, 576)]
        if chunk == 4:
            part = jnp.concatenate([part, part], axis=1)
        if chunk < 3:
            part = part * cosine + turned(part) * sine
        for odd in range(2):
            index = 2 * chunk + odd
            if index == 9:
                continue
            piece = roll(part, 64) if odd else part
            kind, head = index // 3, index % 3
            if kind == 0:
                q_ref[head, rows, :] = (jnp.where(low, piece, 0.0).astype(BF16).astype(F32) * 0.125).astype(BF16)
            elif kind == 1:
                k_ref[head, rows, :] = jnp.where(low, piece, ones).astype(BF16)
            else:
                v_ref[head, rows, :] = jnp.where(low, piece, ones).astype(BF16)


def attend_rows(head, rows, keys, mask, q_ref, k_ref, v_ref, o_ref):
    query = q_ref[head, rows, :]
    scores = mm_nt(query, k_ref[head, keys, :])
    if mask is not None:
        scores = jnp.where(mask, scores, -1e9)
    highest = jnp.max(scores, axis=1, keepdims=True)
    weights = jnp.exp(scores - highest).astype(BF16)
    mixed = mm(weights, v_ref[head, keys, :])
    total = mixed[:, 64:65]
    lane = iota(mixed.shape, 1)
    o_ref[head, rows, :] = jnp.where(lane < 64, mixed * (1.0 / total), 0.0).astype(BF16)
    q_ref[head, rows, :] = extra_lanes(query.astype(F32), highest + jnp.log(total)).astype(BF16)


def forward_kernel(len_ref, hid_ref, w_ref, cos_ref, sin_ref, q_ref, k_ref, v_ref, o_ref, mix_ref, xt_ref):
    bounds = doc_bounds(len_ref)

    @pl.loop(0, SEQ)
    def _(block):
        project_block(block, hid_ref, w_ref, cos_ref, sin_ref, q_ref, k_ref, v_ref, xt_ref)

    order = edge_order(bounds[3], False)
    back = edge_order(bounds[3], True)
    for ref in (q_ref, k_ref, v_ref):
        for head in range(LOCAL):
            short, long = permute_edge(order, ref, head)
            ref[head, 0:HALF, :] = short
            ref[head, PACK - HALF : PACK, :] = long
    mask = short_mask(bounds)
    for head in range(LOCAL):
        attend_rows(head, pl.ds(0, HALF), pl.ds(0, HALF), mask, q_ref, k_ref, v_ref, o_ref)

    @pl.loop(1, PACK // HALF)
    def _(block):
        rows = pl.ds(pl.multiple_of(block * HALF, HALF), HALF)
        for head in range(LOCAL):
            attend_rows(head, rows, pl.ds(HALF, PACK - HALF), None, q_ref, k_ref, v_ref, o_ref)

    for head in range(LOCAL):
        top, bottom = permute_edge(back, o_ref, head)
        for dest in range(SEQ):
            first = top if dest == 0 else o_ref[head, TOK * dest : TOK * dest + HALF, :]
            second = bottom if dest == SEQ - 1 else o_ref[head, TOK * dest + HALF : TOK * dest + TOK, :]
            mix_ref[dest, head] = pack_halves(first.astype(F32), second.astype(F32)).astype(BF16)


def backward_rows(head, rows, queries, mask, q_ref, k_ref, v_ref, d_ref, dk_ref, dv_ref):
    query, grad = q_ref[head, queries, :], d_ref[head, queries, :]
    key = k_ref[head, rows, :]
    shares = jnp.exp(mm_nt(key, query))
    if mask is not None:
        shares = jnp.where(mask, shares, 0.0)
    grad_scores = (shares * mm_nt(v_ref[head, rows, :], grad)).astype(BF16)
    dv_ref[head, rows, :] = mm(shares.astype(BF16), grad).astype(BF16)
    dk_ref[head, rows, :] = mm(grad_scores, query).astype(BF16)
    return mm_tn(grad_scores, key)


def backward_kernel(
    len_ref, g_ref, q_ref, k_ref, v_ref, o_ref, xt_ref, cos_ref, sin_ref,
    out_ref, gw_ref, d_ref, dq_ref, dk_ref, dv_ref, acc_ref, gq_ref,
):
    bounds = doc_bounds(len_ref)
    order = edge_order(bounds[3], False)
    back = edge_order(bounds[3], True)
    low = low_lanes(HALF)
    for head in range(LOCAL):
        for source in range(SEQ):
            packed = g_ref[source, head].astype(F32)
            d_ref[head, TOK * source : TOK * source + HALF, :] = jnp.where(low, packed, 0.0).astype(BF16)
            d_ref[head, TOK * source + HALF : TOK * source + TOK, :] = jnp.where(
                low, roll(packed, 64), 0.0
            ).astype(BF16)
        short, long = permute_edge(order, d_ref, head)
        d_ref[head, 0:HALF, :] = short
        d_ref[head, PACK - HALF : PACK, :] = long

    @pl.loop(0, PACK // HALF)
    def _(block):
        rows = pl.ds(pl.multiple_of(block * HALF, HALF), HALF)
        for head in range(LOCAL):
            grad = d_ref[head, rows, :].astype(F32)
            inner = jnp.sum(grad * o_ref[head, rows, :].astype(F32), axis=1, keepdims=True)
            d_ref[head, rows, :] = extra_lanes(grad, inner).astype(BF16)

    mask = short_mask(bounds)
    for head in range(LOCAL):
        acc_ref[head, 0:HALF, :] = backward_rows(
            head, pl.ds(0, HALF), pl.ds(0, HALF), mask, q_ref, k_ref, v_ref, d_ref, dk_ref, dv_ref
        )
        acc_ref[head, HALF:PACK, :] = jnp.zeros((LONGEST, 128), F32)

    @pl.loop(1, PACK // HALF)
    def _(block):
        rows = pl.ds(pl.multiple_of(block * HALF, HALF), HALF)
        for head in range(LOCAL):
            acc_ref[head, HALF:PACK, :] += backward_rows(
                head, rows, pl.ds(HALF, LONGEST), None, q_ref, k_ref, v_ref, d_ref, dk_ref, dv_ref
            )

    for head in range(LOCAL):
        dq_ref[head] = (acc_ref[head] * 0.125).astype(BF16)
        for ref in (dq_ref, dk_ref, dv_ref):
            top, bottom = permute_edge(back, ref, head)
            ref[head, 0:HALF, :] = top
            ref[head, PACK - HALF : PACK, :] = bottom

    @pl.loop(0, SEQ)
    def _(dest):
        top = pl.ds(pl.multiple_of(dest * TOK, TOK), HALF)
        bottom = pl.ds(pl.multiple_of(dest * TOK + HALF, HALF), HALF)
        cosine = pack_halves(cos_ref[top, :], cos_ref[bottom, :])
        sine = pack_halves(sin_ref[top, :], sin_ref[bottom, :])
        blocks = []
        for kind, ref in enumerate((dq_ref, dk_ref, dv_ref)):
            for head in range(LOCAL):
                packed = pack_halves(ref[head, top, :].astype(F32), ref[head, bottom, :].astype(F32))
                if kind < 2:
                    packed = packed * cosine - turned(packed) * sine
                out_ref[dest, head, kind] = packed.astype(BF16)
                blocks.append(packed)
        for chunk in range(5):
            one = blocks[2 * chunk]
            two = blocks[2 * chunk + 1] if chunk < 4 else jnp.zeros_like(one)
            gq_ref[top, 128 * chunk : 128 * chunk + 128] = pack_halves(one, two).astype(BF16)
            gq_ref[bottom, 128 * chunk : 128 * chunk + 128] = jnp.where(low, roll(one, 64), two).astype(BF16)

    total = mm(xt_ref[0], gq_ref[0:TOK, :])
    for block in range(1, SEQ):
        total += mm(xt_ref[block], gq_ref[TOK * block : TOK * block + TOK, :])
    gw_ref[...] = total[:, :576].astype(BF16)


def middle_kernel(
    hid_ref, mix_ref, wo_ref, wi_ref, wd_ref, cot_ref,
    out_ref, gres_ref, gmix_ref, go_ref, gi_ref, gd_ref,
    attn_ref, x_ref, proj_ref, act_ref, gp_ref,
):
    low = low_lanes(HALF)
    for chunk in range(6):
        pair = []
        for index in (2 * chunk, 2 * chunk + 1):
            pair.append(mix_ref[index // 3, index % 3].astype(F32))
        one, two = pair
        lanes = slice(128 * chunk, 128 * chunk + 128)
        attn_ref[0:HALF, lanes] = pack_halves(one, two).astype(BF16)
        attn_ref[HALF:TOK, lanes] = jnp.where(low, roll(one, 64), two).astype(BF16)
    residual = hid_ref[...].astype(F32) + mm(attn_ref[...], wo_ref[...])
    xhat, scale = norm_parts(residual)
    x_ref[...] = xhat.astype(BF16)
    ff = wd_ref.shape[0]
    step = 384
    for chunk in range(2 * ff // step):
        lanes = slice(step * chunk, step * chunk + step)
        proj_ref[:, lanes] = mm(x_ref[...], wi_ref[:, lanes])
    output = residual
    branch = cot_ref[...]
    for chunk in range(ff // step):
        lanes = slice(step * chunk, step * chunk + step)
        inner = proj_ref[:, lanes]
        gate = proj_ref[:, ff + step * chunk : ff + step * chunk + step]
        phi = 0.5 * (1.0 + lax.erf(inner * math.sqrt(0.5)))
        gelu = inner * phi
        act = (gelu * gate).astype(BF16)
        act_ref[:, lanes] = act
        output = output + mm(act, wd_ref[lanes, :])
        grad_act = mm_nt(branch, wd_ref[lanes, :])
        density = jnp.exp(inner * inner * -0.5) * (1.0 / math.sqrt(2.0 * math.pi))
        gp_ref[:, lanes] = (grad_act * gate * (phi + inner * density)).astype(BF16)
        gp_ref[:, ff + step * chunk : ff + step * chunk + step] = (grad_act * gelu).astype(BF16)
    out_ref[...] = output.astype(BF16)
    grad = mm_nt(gp_ref[...], wi_ref[...])
    grad = scale * (
        grad
        - jnp.mean(grad, axis=-1, keepdims=True)
        - xhat * jnp.mean(grad * xhat, axis=-1, keepdims=True)
    )
    grad_res = branch.astype(F32) + grad
    gres_ref[...] = grad_res
    grad_attn = grad_res.astype(BF16)
    grad_mix = mm_nt(grad_attn, wo_ref[...]).astype(BF16).astype(F32)
    for chunk in range(6):
        lanes = slice(128 * chunk, 128 * chunk + 128)
        top, bottom = grad_mix[0:HALF, lanes], grad_mix[HALF:TOK, lanes]
        one = pack_halves(top, bottom)
        two = jnp.where(low, roll(top, 64), bottom)
        gmix_ref[2 * chunk // 3, 2 * chunk % 3] = one.astype(BF16)
        gmix_ref[(2 * chunk + 1) // 3, (2 * chunk + 1) % 3] = two.astype(BF16)
    go_ref[...] = mm_tn(attn_ref[...], grad_attn).astype(BF16)
    for chunk in range(2 * ff // step):
        lanes = slice(step * chunk, step * chunk + step)
        gi_ref[:, lanes] = mm_tn(x_ref[...], gp_ref[:, lanes]).astype(BF16)
    for chunk in range(ff // step):
        lanes = slice(step * chunk, step * chunk + step)
        gd_ref[lanes, :] = mm_tn(act_ref[:, lanes], branch).astype(BF16)


def last_kernel(g_ref, w_ref, hid_ref, gres_ref, out_ref, full_ref):
    low = low_lanes(HALF)
    for chunk in range(18):
        pair = []
        for index in (2 * chunk, 2 * chunk + 1):
            kind, head = index // HEADS, index % HEADS
            pair.append(g_ref[head // 3, head % 3, kind].astype(F32))
        one, two = pair
        lanes = slice(128 * chunk, 128 * chunk + 128)
        full_ref[0:HALF, lanes] = pack_halves(one, two).astype(BF16)
        full_ref[HALF:TOK, lanes] = jnp.where(low, roll(one, 64), two).astype(BF16)
    grad = mm_nt(full_ref[...], w_ref[...])
    xhat, scale = norm_parts(hid_ref[...].astype(F32))
    grad = scale * (
        grad
        - jnp.mean(grad, axis=-1, keepdims=True)
        - xhat * jnp.mean(grad * xhat, axis=-1, keepdims=True)
    )
    out_ref[...] = gres_ref[...] + grad


SMEM = pl.BlockSpec(memory_space=pltpu.SMEM)
VMEM = pl.BlockSpec(memory_space=pltpu.VMEM)


def shape(*dims, dtype=BF16):
    return jax.ShapeDtypeStruct(dims, dtype)


def call(kernel, args, outs, scratch=(), smem=False):
    specs = [VMEM] * len(args)
    if smem:
        specs[0] = SMEM
    return pl.pallas_call(
        kernel,
        out_shape=outs,
        in_specs=specs,
        out_specs=jax.tree.map(lambda _: VMEM, outs),
        scratch_shapes=list(scratch),
        compiler_params=pltpu.CompilerParams(vmem_limit_bytes=VMEM_LIMIT),
    )(*args)


def rope_tables(lengths):
    ends = jnp.cumsum(lengths)
    places = jnp.arange(PACK, dtype=jnp.int32)
    started = jnp.where(places[:, None] >= ends[None, :3], lengths[None, :3], 0)
    position = (places - jnp.sum(started, axis=1)).astype(F32)
    lane = jnp.arange(128, dtype=jnp.int32)
    inverse = jnp.exp((lane % 32).astype(F32) * (-2.0 * math.log(160000.0) / HEAD_DIM))
    angles = position[:, None] * inverse[None, :]
    sign = jnp.where((lane & 32) == 0, -1.0, 1.0)
    return jnp.cos(angles), jnp.sin(angles) * sign


def body(hidden, lengths, attn_gain, w_qkv, w_attn_out, mlp_gain, w_in, w_mlp_out, cotangent):
    rank = lax.axis_index("seq")
    lengths = lengths[0]
    gain_one = attn_gain.astype(F32)[:, None]
    gain_two = mlp_gain.astype(F32)[:, None]
    w_one = (w_qkv.astype(F32) * gain_one).astype(BF16)
    w_two = (w_in.astype(F32) * gain_two).astype(BF16)
    own = lax.dynamic_index_in_dim(w_one.reshape(-1, 3, SEQ, 192), rank, 2, keepdims=False).reshape(-1, 576)

    def gather(x):
        return lax.all_gather(x, "fsdp", axis=0, tiled=True)

    own_full, one_full, out_full = gather(own), gather(w_one), gather(w_attn_out)
    two_full, down_full = gather(w_two), gather(w_mlp_out)
    hidden_full = lax.all_gather(hidden[0], "seq", axis=0)
    cosine, sine = rope_tables(lengths)
    head_shape = shape(LOCAL, PACK, 128)
    q, k, v, o, mix, xt = call(
        forward_kernel,
        (lengths, hidden_full, own_full, cosine, sine),
        (head_shape, head_shape, head_shape, head_shape, shape(SEQ, LOCAL, HALF, 128), shape(SEQ, 768, TOK)),
        smem=True,
    )
    mix = lax.all_to_all(mix, "seq", 0, 0)
    ff = down_full.shape[0]
    output, grad_res, grad_mix, grad_out, grad_in, grad_down = call(
        middle_kernel,
        (hidden[0], mix, out_full, two_full, down_full, cotangent[0]),
        (
            shape(TOK, 768),
            shape(TOK, 768, dtype=F32),
            shape(SEQ, LOCAL, HALF, 128),
            shape(768, 768),
            shape(768, 2 * ff),
            shape(ff, 768),
        ),
        (
            pltpu.VMEM((TOK, 768), BF16),
            pltpu.VMEM((TOK, 768), BF16),
            pltpu.VMEM((TOK, 2 * ff), F32),
            pltpu.VMEM((TOK, ff), BF16),
            pltpu.VMEM((TOK, 2 * ff), BF16),
        ),
    )
    grad_mix = lax.all_to_all(grad_mix, "seq", 0, 0)
    grads, grad_own = call(
        backward_kernel,
        (lengths, grad_mix, q, k, v, o, xt, cosine, sine),
        (shape(SEQ, LOCAL, 3, HALF, 128), shape(768, 576)),
        (
            pltpu.VMEM((LOCAL, PACK, 128), BF16),
            pltpu.VMEM((LOCAL, PACK, 128), BF16),
            pltpu.VMEM((LOCAL, PACK, 128), BF16),
            pltpu.VMEM((LOCAL, PACK, 128), BF16),
            pltpu.VMEM((LOCAL, PACK, 128), F32),
            pltpu.VMEM((PACK, 640), BF16),
        ),
        smem=True,
    )
    grads = lax.all_to_all(grads, "seq", 0, 0)
    input_grad = call(
        last_kernel,
        (grads, one_full, hidden[0], grad_res),
        shape(TOK, 768, dtype=F32),
        (pltpu.VMEM((TOK, 2304), BF16),),
    )

    def scatter(x):
        return lax.psum_scatter(x, "fsdp", scatter_dimension=0, tiled=True)

    def columns(x):
        return lax.psum_scatter(x, "seq", scatter_dimension=1, tiled=True).astype(F32)

    rows_in = scatter(grad_in)
    rows_own = scatter(grad_own).astype(F32)
    gain_part_two = jnp.sum(rows_in.astype(F32) * w_in.astype(F32), axis=1)
    own_raw = lax.dynamic_index_in_dim(w_qkv.reshape(-1, 3, SEQ, 192), rank, 2, keepdims=False).reshape(-1, 576)
    gain_part_one = jnp.sum(rows_own * own_raw.astype(F32), axis=1)
    grad_gain_one, grad_gain_two = lax.psum((gain_part_one, gain_part_two), "seq")
    spread = lax.all_gather((rows_own * gain_one).reshape(-1, 3, 192), "seq", axis=2)
    grad_qkv = lax.dynamic_slice_in_dim(spread.reshape(-1, 2304), rank * 576, 576, axis=1)
    return (
        output[None],
        input_grad[None],
        grad_gain_one,
        grad_qkv,
        columns(scatter(grad_out)),
        grad_gain_two,
        columns(rows_in) * gain_two,
        columns(scatter(grad_down)),
    )


def solution(mesh):
    in_specs = (
        P("fsdp", "seq", None),
        P("fsdp", None),
        P("fsdp"),
        P("fsdp", None),
        P("fsdp", None),
        P("fsdp"),
        P("fsdp", None),
        P("fsdp", None),
        P("fsdp", "seq", None),
    )
    out_specs = (
        P("fsdp", "seq", None),
        P("fsdp", "seq", None),
        P("fsdp"),
        P("fsdp", "seq"),
        P("fsdp", "seq"),
        P("fsdp"),
        P("fsdp", "seq"),
        P("fsdp", "seq"),
    )
    return jax.shard_map(body, mesh=mesh, in_specs=in_specs, out_specs=out_specs, check_vma=False)
```

```python
import math

import jax
import jax.numpy as jnp
from jax import lax
from jax.experimental import pallas as pl
from jax.experimental.pallas import tpu as pltpu
from jax.sharding import PartitionSpec as P

HEADS = 12
HEAD_DIM = 64
LONGEST = 1344
SEQ = 4
LOCAL = 3
TOK = 384
HALF = 192
PACK = 1536
F32 = jnp.float32
BF16 = jnp.bfloat16
VMEM_LIMIT = 60 * 1024 * 1024


def mm(left, right):
    return jnp.dot(left, right, preferred_element_type=F32)


def mm_nt(left, right):
    return lax.dot_general(left, right, (((1,), (1,)), ((), ())), preferred_element_type=F32)


def mm_tn(left, right):
    return lax.dot_general(left, right, (((0,), (0,)), ((), ())), preferred_element_type=F32)


def iota(shape, dim):
    return lax.broadcasted_iota(jnp.int32, shape, dim)


def roll(x, shift):
    return pltpu.roll(x, shift, 1)


def low_lanes(rows):
    return iota((rows, 128), 1) < 64


def turned(x):
    lane = iota(x.shape, 1)
    first = (lane & 32) == 0
    return jnp.where(first, roll(x, 96), roll(x, 32))


def norm_parts(values):
    average = jnp.mean(values, axis=-1, keepdims=True)
    centred = values - average
    variance = jnp.mean(centred * centred, axis=-1, keepdims=True)
    scale = lax.rsqrt(variance + 1e-05)
    return centred * scale, scale


def doc_bounds(len_ref):
    first = len_ref[0]
    second = first + len_ref[1]
    third = second + len_ref[2]
    start = jnp.where(
        len_ref[0] == LONGEST,
        0,
        jnp.where(len_ref[1] == LONGEST, first, jnp.where(len_ref[2] == LONGEST, second, third)),
    )
    return first, second, third, start


def edge_order(start, transposed):
    stored = iota((2 * HALF, 2 * HALF), 1 if transposed else 0)
    edge = iota((2 * HALF, 2 * HALF), 0 if transposed else 1)
    source = stored + (HALF + start)
    source = jnp.where(source >= 2 * HALF, source - 2 * HALF, source)
    return jnp.where(edge == source, 1.0, 0.0).astype(BF16)


def short_mask(bounds):
    first, second, third, start = bounds

    def numbers(dim):
        row = iota((HALF, HALF), dim) + (HALF + start)
        row = jnp.where(row >= 2 * HALF, row - 2 * HALF, row)
        place = jnp.where(row >= HALF, row + (PACK - 2 * HALF), row)
        return (
            jnp.where(place >= first, 1, 0)
            + jnp.where(place >= second, 1, 0)
            + jnp.where(place >= third, 1, 0)
        )

    return numbers(0) == numbers(1)


def extra_lanes(base, column):
    lane = iota(base.shape, 1)
    rest = -column
    top = rest.astype(BF16).astype(F32)
    rest = rest - top
    middle = rest.astype(BF16).astype(F32)
    rest = rest - middle
    return jnp.where(
        lane < 64,
        base,
        jnp.where(lane == 64, top, jnp.where(lane == 65, middle, jnp.where(lane == 66, rest, 0.0))),
    )


def permute_edge(order, ref, head):
    edge = jnp.concatenate([ref[head, 0:HALF, :], ref[head, PACK - HALF : PACK, :]], axis=0)
    moved = mm(order, edge).astype(BF16)
    return moved[0:HALF], moved[HALF : 2 * HALF]


def pack_halves(top, bottom):
    return jnp.where(low_lanes(top.shape[0]), top, roll(bottom, 64))


def rope_rows(len_ref, inv_ref, block, cos_ref, sin_ref):
    rows = pl.ds(pl.multiple_of(block * TOK, TOK), TOK)
    place = iota((TOK, 128), 0) + block * TOK
    first = len_ref[0]
    second = first + len_ref[1]
    third = second + len_ref[2]
    started = (
        jnp.where(place >= first, len_ref[0], 0)
        + jnp.where(place >= second, len_ref[1], 0)
        + jnp.where(place >= third, len_ref[2], 0)
    )
    angles = (place - started).astype(F32) * inv_ref[0:1, :]
    sine = jnp.sin(angles)
    cos_ref[rows, :] = jnp.cos(angles)
    sin_ref[rows, :] = jnp.where((iota((TOK, 128), 1) & 32) == 0, -sine, sine)


def project_block(block, hid_ref, w_ref, cos_ref, sin_ref, q_ref, k_ref, v_ref, xt_ref):
    rows = pl.ds(pl.multiple_of(block * TOK, TOK), TOK)
    xhat = norm_parts(hid_ref[block].astype(F32))[0].astype(BF16)
    xt_ref[block] = jnp.transpose(xhat)
    qkv = mm(xhat, w_ref[...])
    cosine, sine = cos_ref[rows, :], sin_ref[rows, :]
    lane = iota((TOK, 128), 1)
    low = lane < 64
    ones = jnp.where(lane < 67, 1.0, 0.0)
    for chunk in range(5):
        part = qkv[:, 128 * chunk : min(128 * chunk + 128, 576)]
        if chunk == 4:
            part = jnp.concatenate([part, part], axis=1)
        if chunk < 3:
            part = part * cosine + turned(part) * sine
        for odd in range(2):
            index = 2 * chunk + odd
            if index == 9:
                continue
            piece = roll(part, 64) if odd else part
            kind, head = index // 3, index % 3
            if kind == 0:
                q_ref[head, rows, :] = (jnp.where(low, piece, 0.0).astype(BF16).astype(F32) * 0.125).astype(BF16)
            elif kind == 1:
                k_ref[head, rows, :] = jnp.where(low, piece, ones).astype(BF16)
            else:
                v_ref[head, rows, :] = jnp.where(low, piece, ones).astype(BF16)


def attend_rows(head, rows, keys, mask, q_ref, k_ref, v_ref, o_ref):
    query = q_ref[head, rows, :]
    scores = mm_nt(query, k_ref[head, keys, :])
    if mask is not None:
        scores = jnp.where(mask, scores, -1e9)
    highest = jnp.max(scores, axis=1, keepdims=True)
    weights = jnp.exp(scores - highest).astype(BF16)
    mixed = mm(weights, v_ref[head, keys, :])
    total = mixed[:, 64:65]
    lane = iota(mixed.shape, 1)
    o_ref[head, rows, :] = jnp.where(lane < 64, mixed * (1.0 / total), 0.0).astype(BF16)
    q_ref[head, rows, :] = extra_lanes(query.astype(F32), highest + jnp.log(total)).astype(BF16)


def places():
    seq, fsdp = lax.axis_index("seq"), lax.axis_index("fsdp")
    return seq, fsdp, fsdp // 8, (fsdp // 2) % 4, fsdp % 2


def peer(axis, step):
    seq, fsdp, z, y, core = places()
    if axis == "x":
        return ((seq + step) % SEQ, fsdp)
    if axis == "y":
        return (seq, z * 8 + ((y + step) % 4) * 2 + core)
    if axis == "z":
        return (seq, ((z + step) % 4) * 8 + y * 2 + core)
    return (seq, fsdp + 1 - 2 * core)


def remote(source, target, send_sem, recv_sem, device):
    return pltpu.make_async_remote_copy(
        src_ref=source,
        dst_ref=target,
        send_sem=send_sem,
        recv_sem=recv_sem,
        device_id=device,
        device_id_type=pl.DeviceIdType.MESH,
    )


ALL_PEERS = [(axis, step) for axis in "xyz" for step in (1, 2, 3)] + [("c", 1)]


def greet():
    barrier = pltpu.get_barrier_semaphore()
    for axis, step in ALL_PEERS:
        pl.semaphore_signal(barrier, inc=1, device_id=peer(axis, step), device_id_type=pl.DeviceIdType.MESH)
    pl.semaphore_wait(barrier, len(ALL_PEERS))


class Gather:
    def __init__(self, shard, full, send, recv, index, first):
        _, _, z, y, core = places()
        self.shard, self.mine = shard, full.at[z, y, core]
        self.send, self.recv, self.index = send, recv, index
        line = full.at[z, :, core] if first == "y" else full.at[:, y, core]
        self.hops = (
            [(shard, self.mine, first, step) for step in (1, 2, 3)],
            [(line, line, "z" if first == "y" else "y", step) for step in (1, 2, 3)],
            [(full.at[:, :, core], full.at[:, :, core], "c", 1)],
        )
        self.local = pltpu.make_async_copy(shard, self.mine, send.at[index, 7])

    def copies(self, hop):
        return [
            remote(src, dst, self.send.at[self.index, 3 * hop + n], self.recv.at[self.index, 3 * hop + n], peer(axis, step))
            for n, (src, dst, axis, step) in enumerate(self.hops[hop])
        ]

    def start(self, hop):
        if hop == 0:
            self.local.start()
        for copy in self.copies(hop):
            copy.start()

    def arrive(self, hop):
        if hop == 0:
            self.local.wait()
        for copy in self.copies(hop):
            copy.wait_recv()

    def finish(self):
        for hop in range(3):
            for copy in self.copies(hop):
                copy.wait_send()


def forward_kernel(
    len_ref, inv_ref, own_ref, hid_in, two_ref, out_ref, down_ref,
    q_ref, k_ref, v_ref, o_ref, mix_ref, xt_ref, cos_ref, sin_ref, two_full, out_full, down_full,
    hid_ref, own_full, w_ref, stage_ref, gather_send, gather_recv, hid_send, hid_recv, mix_send, mix_recv,
):
    seq, fsdp, _, _, _ = places()
    bounds = doc_bounds(len_ref)
    right, left = (seq + 1) % SEQ, (seq + 3) % SEQ
    greet()
    own = Gather(own_ref, own_full, gather_send, gather_recv, 0, "y")
    two = Gather(two_ref, two_full, gather_send, gather_recv, 1, "y")
    out = Gather(out_ref, out_full, gather_send, gather_recv, 2, "z")
    down = Gather(down_ref, down_full, gather_send, gather_recv, 3, "z")
    own.start(0)
    to_right = remote(hid_in, hid_ref.at[seq], hid_send.at[0], hid_recv.at[0], peer("x", 1))
    to_left = remote(hid_in, hid_ref.at[seq], hid_send.at[1], hid_recv.at[1], peer("x", 3))
    to_right.start()
    to_left.start()
    hid_ref[seq] = hid_in[...]
    for weight in (out, two, down):
        weight.start(0)

    rope_rows(len_ref, inv_ref, seq, cos_ref, sin_ref)
    own.arrive(0)
    own.start(1)
    rope_rows(len_ref, inv_ref, right, cos_ref, sin_ref)
    own.arrive(1)
    own.start(2)
    rope_rows(len_ref, inv_ref, left, cos_ref, sin_ref)
    rope_rows(len_ref, inv_ref, (seq + 2) % SEQ, cos_ref, sin_ref)
    own.arrive(2)
    for pair in range(16):
        z, y = pair // 4, pair % 4
        rows = jnp.concatenate([own_full[z, y, 0].astype(F32), own_full[z, y, 1].astype(F32)], axis=0)
        w_ref[48 * pair : 48 * pair + 48, :] = rows.astype(BF16)

    def project(block):
        project_block(block, hid_ref, w_ref, cos_ref, sin_ref, q_ref, k_ref, v_ref, xt_ref)

    project(seq)
    to_right.wait_recv()
    on_right = remote(
        hid_ref.at[left, pl.ds(0, HALF)], hid_ref.at[left, pl.ds(0, HALF)],
        hid_send.at[2], hid_recv.at[2], peer("x", 1),
    )
    on_right.start()
    to_left.wait_recv()
    on_left = remote(
        hid_ref.at[right, pl.ds(HALF, HALF)], hid_ref.at[right, pl.ds(HALF, HALF)],
        hid_send.at[3], hid_recv.at[3], peer("x", 3),
    )
    on_left.start()
    for weight in (out, two, down):
        weight.arrive(0)
        weight.start(1)
    project(left)
    project(right)
    on_right.wait_recv()
    on_left.wait_recv()
    project((seq + 2) % SEQ)

    order = edge_order(bounds[3], False)
    back = edge_order(bounds[3], True)
    for ref in (q_ref, k_ref, v_ref):
        for head in range(LOCAL):
            short, long = permute_edge(order, ref, head)
            ref[head, 0:HALF, :] = short
            ref[head, PACK - HALF : PACK, :] = long

    def attend(block):
        rows = pl.ds(pl.multiple_of(block * HALF, HALF), HALF)
        for head in range(LOCAL):
            attend_rows(head, rows, pl.ds(HALF, PACK - HALF), None, q_ref, k_ref, v_ref, o_ref)

    def mix_copy(dest):
        return remote(stage_ref.at[dest], mix_ref.at[seq], mix_send.at[dest], mix_recv.at[seq], (dest, fsdp))

    def give(dest, head, top, bottom):
        stage_ref[dest, head] = pack_halves(top.astype(F32), bottom.astype(F32)).astype(BF16)

    def hand_over(dest):
        @pl.when(seq != dest)
        def _():
            mix_copy(dest).start()

    def inner_dest(dest):
        pl.loop(2 * dest, 2 * dest + 2)(attend)
        for head in range(LOCAL):
            first = TOK * dest
            give(dest, head, o_ref[head, first : first + HALF, :], o_ref[head, first + HALF : first + TOK, :])
        hand_over(dest)

    inner_dest(1)
    for weight in (out, two, down):
        weight.arrive(1)
        weight.start(2)
    inner_dest(2)
    mask = short_mask(bounds)
    for head in range(LOCAL):
        attend_rows(head, pl.ds(0, HALF), pl.ds(0, HALF), mask, q_ref, k_ref, v_ref, o_ref)

    @pl.loop(0, 3)
    def _(index):
        attend(1 + 5 * jnp.minimum(index, 1) + jnp.maximum(index - 1, 0))

    for head in range(LOCAL):
        top, bottom = permute_edge(back, o_ref, head)
        give(0, head, top, o_ref[head, HALF:TOK, :])
        give(3, head, o_ref[head, 3 * TOK : 3 * TOK + HALF, :], bottom)
    hand_over(0)
    hand_over(3)
    mix_ref[seq] = stage_ref[seq]
    for weight in (out, two, down):
        weight.arrive(2)
    for weight in (own, out, two, down):
        weight.finish()
    for copy in (to_right, to_left, on_right, on_left):
        copy.wait_send()
    for step in (1, 2, 3):
        source = (seq + step) % SEQ
        remote(stage_ref.at[0], mix_ref.at[source], mix_send.at[0], mix_recv.at[source], peer("x", step)).wait_recv()
    for dest in range(SEQ):
        @pl.when(seq != dest)
        def _(dest=dest):
            mix_copy(dest).wait_send()


def backward_rows(head, rows, queries, mask, q_ref, k_ref, v_ref, d_ref, dk_ref, dv_ref):
    query, grad = q_ref[head, queries, :], d_ref[head, queries, :]
    key = k_ref[head, rows, :]
    shares = jnp.exp(mm_nt(key, query))
    if mask is not None:
        shares = jnp.where(mask, shares, 0.0)
    grad_scores = (shares * mm_nt(v_ref[head, rows, :], grad)).astype(BF16)
    dv_ref[head, rows, :] = mm(shares.astype(BF16), grad).astype(BF16)
    dk_ref[head, rows, :] = mm(grad_scores, query).astype(BF16)
    return mm_tn(grad_scores, key)


def backward_kernel(
    len_ref, g_ref, q_ref, k_ref, v_ref, o_ref, xt_ref, cos_ref, sin_ref,
    out_ref, gw_ref, d_ref, dq_ref, dk_ref, dv_ref, acc_ref, gq_ref,
):
    bounds = doc_bounds(len_ref)
    order = edge_order(bounds[3], False)
    back = edge_order(bounds[3], True)
    low = low_lanes(HALF)
    for head in range(LOCAL):
        for source in range(SEQ):
            packed = g_ref[source, head].astype(F32)
            d_ref[head, TOK * source : TOK * source + HALF, :] = jnp.where(low, packed, 0.0).astype(BF16)
            d_ref[head, TOK * source + HALF : TOK * source + TOK, :] = jnp.where(
                low, roll(packed, 64), 0.0
            ).astype(BF16)
        short, long = permute_edge(order, d_ref, head)
        d_ref[head, 0:HALF, :] = short
        d_ref[head, PACK - HALF : PACK, :] = long

    @pl.loop(0, PACK // HALF)
    def _(block):
        rows = pl.ds(pl.multiple_of(block * HALF, HALF), HALF)
        for head in range(LOCAL):
            grad = d_ref[head, rows, :].astype(F32)
            inner = jnp.sum(grad * o_ref[head, rows, :].astype(F32), axis=1, keepdims=True)
            d_ref[head, rows, :] = extra_lanes(grad, inner).astype(BF16)

    mask = short_mask(bounds)
    for head in range(LOCAL):
        acc_ref[head, 0:HALF, :] = backward_rows(
            head, pl.ds(0, HALF), pl.ds(0, HALF), mask, q_ref, k_ref, v_ref, d_ref, dk_ref, dv_ref
        )
        acc_ref[head, HALF:PACK, :] = jnp.zeros((LONGEST, 128), F32)

    @pl.loop(1, PACK // HALF)
    def _(block):
        rows = pl.ds(pl.multiple_of(block * HALF, HALF), HALF)
        for head in range(LOCAL):
            acc_ref[head, HALF:PACK, :] += backward_rows(
                head, rows, pl.ds(HALF, LONGEST), None, q_ref, k_ref, v_ref, d_ref, dk_ref, dv_ref
            )

    for head in range(LOCAL):
        dq_ref[head] = (acc_ref[head] * 0.125).astype(BF16)
        for ref in (dq_ref, dk_ref, dv_ref):
            top, bottom = permute_edge(back, ref, head)
            ref[head, 0:HALF, :] = top
            ref[head, PACK - HALF : PACK, :] = bottom

    @pl.loop(0, SEQ)
    def _(dest):
        top = pl.ds(pl.multiple_of(dest * TOK, TOK), HALF)
        bottom = pl.ds(pl.multiple_of(dest * TOK + HALF, HALF), HALF)
        cosine = pack_halves(cos_ref[top, :], cos_ref[bottom, :])
        sine = pack_halves(sin_ref[top, :], sin_ref[bottom, :])
        blocks = []
        for kind, ref in enumerate((dq_ref, dk_ref, dv_ref)):
            for head in range(LOCAL):
                packed = pack_halves(ref[head, top, :].astype(F32), ref[head, bottom, :].astype(F32))
                if kind < 2:
                    packed = packed * cosine - turned(packed) * sine
                out_ref[dest, head, kind] = packed.astype(BF16)
                blocks.append(packed)
        for chunk in range(5):
            one = blocks[2 * chunk]
            two = blocks[2 * chunk + 1] if chunk < 4 else jnp.zeros_like(one)
            gq_ref[top, 128 * chunk : 128 * chunk + 128] = pack_halves(one, two).astype(BF16)
            gq_ref[bottom, 128 * chunk : 128 * chunk + 128] = jnp.where(low, roll(one, 64), two).astype(BF16)

    total = mm(xt_ref[0], gq_ref[0:TOK, :])
    for block in range(1, SEQ):
        total += mm(xt_ref[block], gq_ref[TOK * block : TOK * block + TOK, :])
    gw_ref[...] = total[:, :576].astype(BF16)


def middle_kernel(
    hid_ref, mix_ref, wo_ref, wi_ref, wd_ref, cot_ref,
    out_ref, gres_ref, gmix_ref, go_ref, gi_ref, gd_ref,
    attn_ref, x_ref, proj_ref, act_ref, gp_ref,
):
    low = low_lanes(HALF)
    for chunk in range(6):
        pair = []
        for index in (2 * chunk, 2 * chunk + 1):
            pair.append(mix_ref[index // 3, index % 3].astype(F32))
        one, two = pair
        lanes = slice(128 * chunk, 128 * chunk + 128)
        attn_ref[0:HALF, lanes] = pack_halves(one, two).astype(BF16)
        attn_ref[HALF:TOK, lanes] = jnp.where(low, roll(one, 64), two).astype(BF16)
    residual = hid_ref[...].astype(F32) + mm(attn_ref[...], wo_ref[...])
    xhat, scale = norm_parts(residual)
    x_ref[...] = xhat.astype(BF16)
    ff = wd_ref.shape[0]
    step = 384
    for chunk in range(2 * ff // step):
        lanes = slice(step * chunk, step * chunk + step)
        proj_ref[:, lanes] = mm(x_ref[...], wi_ref[:, lanes])
    output = residual
    branch = cot_ref[...]
    for chunk in range(ff // step):
        lanes = slice(step * chunk, step * chunk + step)
        inner = proj_ref[:, lanes]
        gate = proj_ref[:, ff + step * chunk : ff + step * chunk + step]
        phi = 0.5 * (1.0 + lax.erf(inner * math.sqrt(0.5)))
        gelu = inner * phi
        act = (gelu * gate).astype(BF16)
        act_ref[:, lanes] = act
        output = output + mm(act, wd_ref[lanes, :])
        grad_act = mm_nt(branch, wd_ref[lanes, :])
        density = jnp.exp(inner * inner * -0.5) * (1.0 / math.sqrt(2.0 * math.pi))
        gp_ref[:, lanes] = (grad_act * gate * (phi + inner * density)).astype(BF16)
        gp_ref[:, ff + step * chunk : ff + step * chunk + step] = (grad_act * gelu).astype(BF16)
    out_ref[...] = output.astype(BF16)
    grad = mm_nt(gp_ref[...], wi_ref[...])
    grad = scale * (
        grad
        - jnp.mean(grad, axis=-1, keepdims=True)
        - xhat * jnp.mean(grad * xhat, axis=-1, keepdims=True)
    )
    grad_res = branch.astype(F32) + grad
    gres_ref[...] = grad_res
    grad_attn = grad_res.astype(BF16)
    grad_mix = mm_nt(grad_attn, wo_ref[...]).astype(BF16).astype(F32)
    for chunk in range(6):
        lanes = slice(128 * chunk, 128 * chunk + 128)
        top, bottom = grad_mix[0:HALF, lanes], grad_mix[HALF:TOK, lanes]
        one = pack_halves(top, bottom)
        two = jnp.where(low, roll(top, 64), bottom)
        gmix_ref[2 * chunk // 3, 2 * chunk % 3] = one.astype(BF16)
        gmix_ref[(2 * chunk + 1) // 3, (2 * chunk + 1) % 3] = two.astype(BF16)
    go_ref[...] = mm_tn(attn_ref[...], grad_attn).astype(BF16)
    for chunk in range(2 * ff // step):
        lanes = slice(step * chunk, step * chunk + step)
        gi_ref[:, lanes] = mm_tn(x_ref[...], gp_ref[:, lanes]).astype(BF16)
    for chunk in range(ff // step):
        lanes = slice(step * chunk, step * chunk + step)
        gd_ref[lanes, :] = mm_tn(act_ref[:, lanes], branch).astype(BF16)


def last_kernel(g_ref, w_ref, hid_ref, gres_ref, out_ref, full_ref):
    low = low_lanes(HALF)
    for chunk in range(18):
        pair = []
        for index in (2 * chunk, 2 * chunk + 1):
            kind, head = index // HEADS, index % HEADS
            pair.append(g_ref[head // 3, head % 3, kind].astype(F32))
        one, two = pair
        lanes = slice(128 * chunk, 128 * chunk + 128)
        full_ref[0:HALF, lanes] = pack_halves(one, two).astype(BF16)
        full_ref[HALF:TOK, lanes] = jnp.where(low, roll(one, 64), two).astype(BF16)
    grad = mm_nt(full_ref[...], w_ref[...])
    xhat, scale = norm_parts(hid_ref[...].astype(F32))
    grad = scale * (
        grad
        - jnp.mean(grad, axis=-1, keepdims=True)
        - xhat * jnp.mean(grad * xhat, axis=-1, keepdims=True)
    )
    out_ref[...] = gres_ref[...] + grad


SMEM = pl.BlockSpec(memory_space=pltpu.SMEM)
VMEM = pl.BlockSpec(memory_space=pltpu.VMEM)
ANY = pl.BlockSpec(memory_space=pl.ANY)


def shape(*dims, dtype=BF16):
    return jax.ShapeDtypeStruct(dims, dtype)


def call(kernel, args, outs, scratch=(), arg_specs=None, out_specs=None, collective=None):
    return pl.pallas_call(
        kernel,
        out_shape=outs,
        in_specs=arg_specs or [VMEM] * len(args),
        out_specs=out_specs or jax.tree.map(lambda _: VMEM, outs),
        scratch_shapes=list(scratch),
        compiler_params=pltpu.CompilerParams(
            vmem_limit_bytes=VMEM_LIMIT,
            collective_id=collective,
            has_side_effects=collective is not None,
        ),
    )(*args)


def body(hidden, lengths, attn_gain, w_qkv, w_attn_out, mlp_gain, w_in, w_mlp_out, cotangent):
    rank = lax.axis_index("seq")
    lengths = lengths[0]
    gain_one = attn_gain.astype(F32)[:, None]
    gain_two = mlp_gain.astype(F32)[:, None]
    w_one = (w_qkv.astype(F32) * gain_one).astype(BF16)
    w_two = (w_in.astype(F32) * gain_two).astype(BF16)
    own = lax.dynamic_index_in_dim(w_one.reshape(-1, 3, SEQ, 192), rank, 2, keepdims=False).reshape(-1, 576)

    def gather(x):
        return lax.all_gather(x, "fsdp", axis=0, tiled=True)

    one_full = gather(w_one)
    lane = jnp.arange(128, dtype=jnp.int32) % 32
    inverse = jnp.exp(lane.astype(F32) * (-2.0 * math.log(160000.0) / HEAD_DIM))
    inverse = jnp.broadcast_to(inverse, (8, 128))
    head_shape = shape(LOCAL, PACK, 128)
    ff = w_mlp_out.shape[0] * 32

    def spread(x):
        return shape(4, 4, 2, *x.shape)

    q, k, v, o, mix, xt, cosine, sine, two_full, out_full, down_full = call(
        forward_kernel,
        (lengths, inverse, own, hidden[0], w_two, w_attn_out, w_mlp_out),
        (
            head_shape, head_shape, head_shape, head_shape,
            shape(SEQ, LOCAL, HALF, 128), shape(SEQ, 768, TOK),
            shape(PACK, 128, dtype=F32), shape(PACK, 128, dtype=F32),
            spread(w_two), spread(w_attn_out), spread(w_mlp_out),
        ),
        (
            pltpu.VMEM((SEQ, TOK, 768), BF16),
            pltpu.VMEM((4, 4, 2, 24, 576), BF16),
            pltpu.VMEM((768, 576), BF16),
            pltpu.VMEM((SEQ, LOCAL, HALF, 128), BF16),
            pltpu.SemaphoreType.DMA((4, 8)),
            pltpu.SemaphoreType.DMA((4, 8)),
            pltpu.SemaphoreType.DMA((4,)),
            pltpu.SemaphoreType.DMA((4,)),
            pltpu.SemaphoreType.DMA((4,)),
            pltpu.SemaphoreType.DMA((4,)),
        ),
        [SMEM, VMEM, VMEM, VMEM, ANY, ANY, ANY],
        (VMEM,) * 8 + (ANY,) * 3,
        collective=1,
    )
    two_full, out_full, down_full = (x.reshape(-1, x.shape[-1]) for x in (two_full, out_full, down_full))
    output, grad_res, grad_mix, grad_out, grad_in, grad_down = call(
        middle_kernel,
        (hidden[0], mix, out_full, two_full, down_full, cotangent[0]),
        (
            shape(TOK, 768),
            shape(TOK, 768, dtype=F32),
            shape(SEQ, LOCAL, HALF, 128),
            shape(768, 768),
            shape(768, 2 * ff),
            shape(ff, 768),
        ),
        (
            pltpu.VMEM((TOK, 768), BF16),
            pltpu.VMEM((TOK, 768), BF16),
            pltpu.VMEM((TOK, 2 * ff), F32),
            pltpu.VMEM((TOK, ff), BF16),
            pltpu.VMEM((TOK, 2 * ff), BF16),
        ),
    )
    grad_mix = lax.all_to_all(grad_mix, "seq", 0, 0)
    grads, grad_own = call(
        backward_kernel,
        (lengths, grad_mix, q, k, v, o, xt, cosine, sine),
        (shape(SEQ, LOCAL, 3, HALF, 128), shape(768, 576)),
        (
            pltpu.VMEM((LOCAL, PACK, 128), BF16),
            pltpu.VMEM((LOCAL, PACK, 128), BF16),
            pltpu.VMEM((LOCAL, PACK, 128), BF16),
            pltpu.VMEM((LOCAL, PACK, 128), BF16),
            pltpu.VMEM((LOCAL, PACK, 128), F32),
            pltpu.VMEM((PACK, 640), BF16),
        ),
        [SMEM] + [VMEM] * 8,
    )
    grads = lax.all_to_all(grads, "seq", 0, 0)
    input_grad = call(
        last_kernel,
        (grads, one_full, hidden[0], grad_res),
        shape(TOK, 768, dtype=F32),
        (pltpu.VMEM((TOK, 2304), BF16),),
    )

    def scatter(x):
        return lax.psum_scatter(x, "fsdp", scatter_dimension=0, tiled=True)

    def columns(x):
        return lax.psum_scatter(x, "seq", scatter_dimension=1, tiled=True).astype(F32)

    rows_in = scatter(grad_in)
    rows_own = scatter(grad_own).astype(F32)
    gain_part_two = jnp.sum(rows_in.astype(F32) * w_in.astype(F32), axis=1)
    own_raw = lax.dynamic_index_in_dim(w_qkv.reshape(-1, 3, SEQ, 192), rank, 2, keepdims=False).reshape(-1, 576)
    gain_part_one = jnp.sum(rows_own * own_raw.astype(F32), axis=1)
    grad_gain_one, grad_gain_two = lax.psum((gain_part_one, gain_part_two), "seq")
    spread = lax.all_gather((rows_own * gain_one).reshape(-1, 3, 192), "seq", axis=2)
    grad_qkv = lax.dynamic_slice_in_dim(spread.reshape(-1, 2304), rank * 576, 576, axis=1)
    return (
        output[None],
        input_grad[None],
        grad_gain_one,
        grad_qkv,
        columns(scatter(grad_out)),
        grad_gain_two,
        columns(rows_in) * gain_two,
        columns(scatter(grad_down)),
    )


def solution(mesh):
    in_specs = (
        P("fsdp", "seq", None),
        P("fsdp", None),
        P("fsdp"),
        P("fsdp", None),
        P("fsdp", None),
        P("fsdp"),
        P("fsdp", None),
        P("fsdp", None),
        P("fsdp", "seq", None),
    )
    out_specs = (
        P("fsdp", "seq", None),
        P("fsdp", "seq", None),
        P("fsdp"),
        P("fsdp", "seq"),
        P("fsdp", "seq"),
        P("fsdp"),
        P("fsdp", "seq"),
        P("fsdp", "seq"),
    )
    return jax.shard_map(body, mesh=mesh, in_specs=in_specs, out_specs=out_specs, check_vma=False)
```

```python
import math

import jax
import jax.numpy as jnp
from jax import lax
from jax.experimental import pallas as pl
from jax.experimental.pallas import tpu as pltpu
from jax.sharding import PartitionSpec as P

HEADS = 12
HEAD_DIM = 64
LONGEST = 1344
SEQ = 4
LOCAL = 3
TOK = 384
HALF = 192
PACK = 1536
F32 = jnp.float32
BF16 = jnp.bfloat16
VMEM_LIMIT = 60 * 1024 * 1024


def mm(left, right):
    return jnp.dot(left, right, preferred_element_type=F32)


def mm_nt(left, right):
    return lax.dot_general(left, right, (((1,), (1,)), ((), ())), preferred_element_type=F32)


def mm_tn(left, right):
    return lax.dot_general(left, right, (((0,), (0,)), ((), ())), preferred_element_type=F32)


def iota(shape, dim):
    return lax.broadcasted_iota(jnp.int32, shape, dim)


def roll(x, shift):
    return pltpu.roll(x, shift, 1)


def low_lanes(rows):
    return iota((rows, 128), 1) < 64


def turned(x):
    lane = iota(x.shape, 1)
    first = (lane & 32) == 0
    return jnp.where(first, roll(x, 96), roll(x, 32))


def norm_parts(values):
    average = jnp.mean(values, axis=-1, keepdims=True)
    centred = values - average
    variance = jnp.mean(centred * centred, axis=-1, keepdims=True)
    scale = lax.rsqrt(variance + 1e-05)
    return centred * scale, scale


def doc_bounds(len_ref):
    first = len_ref[0]
    second = first + len_ref[1]
    third = second + len_ref[2]
    start = jnp.where(
        len_ref[0] == LONGEST,
        0,
        jnp.where(len_ref[1] == LONGEST, first, jnp.where(len_ref[2] == LONGEST, second, third)),
    )
    return first, second, third, start


def edge_order(start, transposed):
    stored = iota((2 * HALF, 2 * HALF), 1 if transposed else 0)
    edge = iota((2 * HALF, 2 * HALF), 0 if transposed else 1)
    source = stored + (HALF + start)
    source = jnp.where(source >= 2 * HALF, source - 2 * HALF, source)
    return jnp.where(edge == source, 1.0, 0.0).astype(BF16)


def short_mask(bounds):
    first, second, third, start = bounds

    def numbers(dim):
        row = iota((HALF, HALF), dim) + (HALF + start)
        row = jnp.where(row >= 2 * HALF, row - 2 * HALF, row)
        place = jnp.where(row >= HALF, row + (PACK - 2 * HALF), row)
        return (
            jnp.where(place >= first, 1, 0)
            + jnp.where(place >= second, 1, 0)
            + jnp.where(place >= third, 1, 0)
        )

    return numbers(0) == numbers(1)


def extra_lanes(base, column):
    lane = iota(base.shape, 1)
    rest = -column
    top = rest.astype(BF16).astype(F32)
    rest = rest - top
    middle = rest.astype(BF16).astype(F32)
    rest = rest - middle
    return jnp.where(
        lane < 64,
        base,
        jnp.where(lane == 64, top, jnp.where(lane == 65, middle, jnp.where(lane == 66, rest, 0.0))),
    )


def permute_edge(order, ref, head):
    edge = jnp.concatenate([ref[head, 0:HALF, :], ref[head, PACK - HALF : PACK, :]], axis=0)
    moved = mm(order, edge).astype(BF16)
    return moved[0:HALF], moved[HALF : 2 * HALF]


def pack_halves(top, bottom):
    return jnp.where(low_lanes(top.shape[0]), top, roll(bottom, 64))


def rope_rows(len_ref, inv_ref, block, cos_ref, sin_ref):
    rows = pl.ds(pl.multiple_of(block * TOK, TOK), TOK)
    place = iota((TOK, 128), 0) + block * TOK
    first = len_ref[0]
    second = first + len_ref[1]
    third = second + len_ref[2]
    started = (
        jnp.where(place >= first, len_ref[0], 0)
        + jnp.where(place >= second, len_ref[1], 0)
        + jnp.where(place >= third, len_ref[2], 0)
    )
    angles = (place - started).astype(F32) * inv_ref[0:1, :]
    sine = jnp.sin(angles)
    cos_ref[rows, :] = jnp.cos(angles)
    sin_ref[rows, :] = jnp.where((iota((TOK, 128), 1) & 32) == 0, -sine, sine)


def project_block(block, hid_ref, w_ref, cos_ref, sin_ref, q_ref, k_ref, v_ref, xt_ref):
    rows = pl.ds(pl.multiple_of(block * TOK, TOK), TOK)
    xhat = norm_parts(hid_ref[block].astype(F32))[0].astype(BF16)
    xt_ref[block] = jnp.transpose(xhat)
    qkv = mm(xhat, w_ref[...])
    cosine, sine = cos_ref[rows, :], sin_ref[rows, :]
    lane = iota((TOK, 128), 1)
    low = lane < 64
    ones = jnp.where(lane < 67, 1.0, 0.0)
    for chunk in range(5):
        part = qkv[:, 128 * chunk : min(128 * chunk + 128, 576)]
        if chunk == 4:
            part = jnp.concatenate([part, part], axis=1)
        if chunk < 3:
            part = part * cosine + turned(part) * sine
        for odd in range(2):
            index = 2 * chunk + odd
            if index == 9:
                continue
            piece = roll(part, 64) if odd else part
            kind, head = index // 3, index % 3
            if kind == 0:
                q_ref[head, rows, :] = (jnp.where(low, piece, 0.0).astype(BF16).astype(F32) * 0.125).astype(BF16)
            elif kind == 1:
                k_ref[head, rows, :] = jnp.where(low, piece, ones).astype(BF16)
            else:
                v_ref[head, rows, :] = jnp.where(low, piece, ones).astype(BF16)


def attend_rows(head, rows, keys, mask, q_ref, k_ref, v_ref, o_ref):
    query = q_ref[head, rows, :]
    scores = mm_nt(query, k_ref[head, keys, :])
    if mask is not None:
        scores = jnp.where(mask, scores, -1e9)
    highest = jnp.max(scores, axis=1, keepdims=True)
    weights = jnp.exp(scores - highest).astype(BF16)
    mixed = mm(weights, v_ref[head, keys, :])
    total = mixed[:, 64:65]
    lane = iota(mixed.shape, 1)
    o_ref[head, rows, :] = jnp.where(lane < 64, mixed * (1.0 / total), 0.0).astype(BF16)
    q_ref[head, rows, :] = extra_lanes(query.astype(F32), highest + jnp.log(total)).astype(BF16)


def places():
    seq, fsdp = lax.axis_index("seq"), lax.axis_index("fsdp")
    return seq, fsdp, fsdp // 8, (fsdp // 2) % 4, fsdp % 2


def peer(axis, step):
    seq, fsdp, z, y, core = places()
    if axis == "x":
        return ((seq + step) % SEQ, fsdp)
    if axis == "y":
        return (seq, z * 8 + ((y + step) % 4) * 2 + core)
    if axis == "z":
        return (seq, ((z + step) % 4) * 8 + y * 2 + core)
    return (seq, fsdp + 1 - 2 * core)


def remote(source, target, send_sem, recv_sem, device):
    return pltpu.make_async_remote_copy(
        src_ref=source,
        dst_ref=target,
        send_sem=send_sem,
        recv_sem=recv_sem,
        device_id=device,
        device_id_type=pl.DeviceIdType.MESH,
    )


ALL_PEERS = [(axis, step) for axis in "xyz" for step in (1, 2, 3)] + [("c", 1)]


def greet():
    barrier = pltpu.get_barrier_semaphore()
    for axis, step in ALL_PEERS:
        pl.semaphore_signal(barrier, inc=1, device_id=peer(axis, step), device_id_type=pl.DeviceIdType.MESH)
    pl.semaphore_wait(barrier, len(ALL_PEERS))


class Gather:
    def __init__(self, shard, full, send, recv, index, first):
        _, _, z, y, core = places()
        self.shard, self.mine = shard, full.at[z, y, core]
        self.send, self.recv, self.index = send, recv, index
        line = full.at[z, :, core] if first == "y" else full.at[:, y, core]
        self.hops = (
            [(shard, self.mine, first, step) for step in (1, 2, 3)],
            [(line, line, "z" if first == "y" else "y", step) for step in (1, 2, 3)],
            [(full.at[:, :, core], full.at[:, :, core], "c", 1)],
        )
        self.local = pltpu.make_async_copy(shard, self.mine, send.at[index, 7])

    def copies(self, hop):
        return [
            remote(src, dst, self.send.at[self.index, 3 * hop + n], self.recv.at[self.index, 3 * hop + n], peer(axis, step))
            for n, (src, dst, axis, step) in enumerate(self.hops[hop])
        ]

    def start(self, hop):
        if hop == 0:
            self.local.start()
        for copy in self.copies(hop):
            copy.start()

    def arrive(self, hop):
        if hop == 0:
            self.local.wait()
        for copy in self.copies(hop):
            copy.wait_recv()

    def finish(self):
        for hop in range(3):
            for copy in self.copies(hop):
                copy.wait_send()


def forward_kernel(
    len_ref, inv_ref, own_ref, hid_in, two_ref, out_ref, down_ref,
    q_ref, k_ref, v_ref, o_ref, mix_ref, xt_ref, cos_ref, sin_ref, two_full, out_full, down_full,
    hid_ref, own_full, w_ref, stage_ref, gather_send, gather_recv, hid_send, hid_recv, mix_send, mix_recv,
):
    seq, fsdp, _, _, _ = places()
    bounds = doc_bounds(len_ref)
    right, left = (seq + 1) % SEQ, (seq + 3) % SEQ
    greet()
    own = Gather(own_ref, own_full, gather_send, gather_recv, 0, "y")
    two = Gather(two_ref, two_full, gather_send, gather_recv, 1, "y")
    out = Gather(out_ref, out_full, gather_send, gather_recv, 2, "z")
    down = Gather(down_ref, down_full, gather_send, gather_recv, 3, "z")
    own.start(0)
    to_right = remote(hid_in, hid_ref.at[seq], hid_send.at[0], hid_recv.at[0], peer("x", 1))
    to_left = remote(hid_in, hid_ref.at[seq], hid_send.at[1], hid_recv.at[1], peer("x", 3))
    to_right.start()
    to_left.start()
    hid_ref[seq] = hid_in[...]
    for weight in (out, two, down):
        weight.start(0)

    rope_rows(len_ref, inv_ref, seq, cos_ref, sin_ref)
    own.arrive(0)
    own.start(1)
    rope_rows(len_ref, inv_ref, right, cos_ref, sin_ref)
    own.arrive(1)
    own.start(2)
    rope_rows(len_ref, inv_ref, left, cos_ref, sin_ref)
    rope_rows(len_ref, inv_ref, (seq + 2) % SEQ, cos_ref, sin_ref)
    own.arrive(2)
    for pair in range(16):
        z, y = pair // 4, pair % 4
        rows = jnp.concatenate([own_full[z, y, 0].astype(F32), own_full[z, y, 1].astype(F32)], axis=0)
        w_ref[48 * pair : 48 * pair + 48, :] = rows.astype(BF16)

    def project(block):
        project_block(block, hid_ref, w_ref, cos_ref, sin_ref, q_ref, k_ref, v_ref, xt_ref)

    project(seq)
    to_right.wait_recv()
    on_right = remote(
        hid_ref.at[left, pl.ds(0, HALF)], hid_ref.at[left, pl.ds(0, HALF)],
        hid_send.at[2], hid_recv.at[2], peer("x", 1),
    )
    on_right.start()
    to_left.wait_recv()
    on_left = remote(
        hid_ref.at[right, pl.ds(HALF, HALF)], hid_ref.at[right, pl.ds(HALF, HALF)],
        hid_send.at[3], hid_recv.at[3], peer("x", 3),
    )
    on_left.start()
    for weight in (out, two, down):
        weight.arrive(0)
        weight.start(1)
    project(left)
    project(right)
    on_right.wait_recv()
    on_left.wait_recv()
    project((seq + 2) % SEQ)

    order = edge_order(bounds[3], False)
    back = edge_order(bounds[3], True)
    for ref in (q_ref, k_ref, v_ref):
        for head in range(LOCAL):
            short, long = permute_edge(order, ref, head)
            ref[head, 0:HALF, :] = short
            ref[head, PACK - HALF : PACK, :] = long

    def attend(block):
        rows = pl.ds(pl.multiple_of(block * HALF, HALF), HALF)
        for head in range(LOCAL):
            attend_rows(head, rows, pl.ds(HALF, PACK - HALF), None, q_ref, k_ref, v_ref, o_ref)

    def mix_copy(dest):
        return remote(stage_ref.at[dest], mix_ref.at[seq], mix_send.at[dest], mix_recv.at[seq], (dest, fsdp))

    def give(dest, head, top, bottom):
        stage_ref[dest, head] = pack_halves(top.astype(F32), bottom.astype(F32)).astype(BF16)

    def hand_over(dest):
        @pl.when(seq != dest)
        def _():
            mix_copy(dest).start()

    def inner_dest(dest):
        pl.loop(2 * dest, 2 * dest + 2)(attend)
        for head in range(LOCAL):
            first = TOK * dest
            give(dest, head, o_ref[head, first : first + HALF, :], o_ref[head, first + HALF : first + TOK, :])
        hand_over(dest)

    inner_dest(1)
    for weight in (out, two, down):
        weight.arrive(1)
        weight.start(2)
    inner_dest(2)
    mask = short_mask(bounds)
    for head in range(LOCAL):
        attend_rows(head, pl.ds(0, HALF), pl.ds(0, HALF), mask, q_ref, k_ref, v_ref, o_ref)

    @pl.loop(0, 3)
    def _(index):
        attend(1 + 5 * jnp.minimum(index, 1) + jnp.maximum(index - 1, 0))

    for head in range(LOCAL):
        top, bottom = permute_edge(back, o_ref, head)
        give(0, head, top, o_ref[head, HALF:TOK, :])
        give(3, head, o_ref[head, 3 * TOK : 3 * TOK + HALF, :], bottom)
    hand_over(0)
    hand_over(3)
    mix_ref[seq] = stage_ref[seq]
    for weight in (out, two, down):
        weight.arrive(2)
    for weight in (own, out, two, down):
        weight.finish()
    for copy in (to_right, to_left, on_right, on_left):
        copy.wait_send()
    for step in (1, 2, 3):
        source = (seq + step) % SEQ
        remote(stage_ref.at[0], mix_ref.at[source], mix_send.at[0], mix_recv.at[source], peer("x", step)).wait_recv()
    for dest in range(SEQ):
        @pl.when(seq != dest)
        def _(dest=dest):
            mix_copy(dest).wait_send()


def backward_rows(head, rows, queries, mask, q_ref, k_ref, v_ref, d_ref, dk_ref, dv_ref):
    query, grad = q_ref[head, queries, :], d_ref[head, queries, :]
    key = k_ref[head, rows, :]
    shares = jnp.exp(mm_nt(key, query))
    if mask is not None:
        shares = jnp.where(mask, shares, 0.0)
    grad_scores = (shares * mm_nt(v_ref[head, rows, :], grad)).astype(BF16)
    dv_ref[head, rows, :] = mm(shares.astype(BF16), grad).astype(BF16)
    dk_ref[head, rows, :] = mm(grad_scores, query).astype(BF16)
    return mm_tn(grad_scores, key)


def middle_kernel(
    hid_ref, mix_ref, wo_ref, wi_ref, wd_ref, cot_ref,
    out_ref, gres_ref, gmix_ref, go_ref, gi_ref, gd_ref,
    attn_ref, x_ref, proj_ref, act_ref, gp_ref, wide_ref,
):
    low = low_lanes(HALF)
    for chunk in range(6):
        pair = []
        for index in (2 * chunk, 2 * chunk + 1):
            pair.append(mix_ref[index // 3, index % 3].astype(F32))
        one, two = pair
        lanes = slice(128 * chunk, 128 * chunk + 128)
        attn_ref[0:HALF, lanes] = pack_halves(one, two).astype(BF16)
        attn_ref[HALF:TOK, lanes] = jnp.where(low, roll(one, 64), two).astype(BF16)
    residual = hid_ref[...].astype(F32) + mm(attn_ref[...], wo_ref[...])
    xhat, scale = norm_parts(residual)
    x_ref[...] = xhat.astype(BF16)
    ff = wd_ref.shape[0]
    step = 384
    for chunk in range(2 * ff // step):
        lanes = slice(step * chunk, step * chunk + step)
        proj_ref[:, lanes] = mm(x_ref[...], wi_ref[:, lanes])
    output = residual
    branch = cot_ref[...]
    for chunk in range(ff // step):
        lanes = slice(step * chunk, step * chunk + step)
        inner = proj_ref[:, lanes]
        gate = proj_ref[:, ff + step * chunk : ff + step * chunk + step]
        phi = 0.5 * (1.0 + lax.erf(inner * math.sqrt(0.5)))
        gelu = inner * phi
        act = (gelu * gate).astype(BF16)
        act_ref[:, lanes] = act
        output = output + mm(act, wd_ref[lanes, :])
        grad_act = mm_nt(branch, wd_ref[lanes, :])
        density = jnp.exp(inner * inner * -0.5) * (1.0 / math.sqrt(2.0 * math.pi))
        gp_ref[:, lanes] = (grad_act * gate * (phi + inner * density)).astype(BF16)
        gp_ref[:, ff + step * chunk : ff + step * chunk + step] = (grad_act * gelu).astype(BF16)
    out_ref[...] = output.astype(BF16)
    grad = mm_nt(gp_ref[...], wi_ref[...])
    grad = scale * (
        grad
        - jnp.mean(grad, axis=-1, keepdims=True)
        - xhat * jnp.mean(grad * xhat, axis=-1, keepdims=True)
    )
    grad_res = branch.astype(F32) + grad
    gres_ref[...] = grad_res
    grad_attn = grad_res.astype(BF16)
    grad_mix = mm_nt(grad_attn, wo_ref[...]).astype(BF16).astype(F32)
    for chunk in range(6):
        lanes = slice(128 * chunk, 128 * chunk + 128)
        top, bottom = grad_mix[0:HALF, lanes], grad_mix[HALF:TOK, lanes]
        one = pack_halves(top, bottom)
        two = jnp.where(low, roll(top, 64), bottom)
        gmix_ref[2 * chunk // 3, 2 * chunk % 3] = one.astype(BF16)
        gmix_ref[(2 * chunk + 1) // 3, (2 * chunk + 1) % 3] = two.astype(BF16)
    def lay(ref, lanes, value):
        for owner in range(32):
            ref[owner % 2, owner // 8, owner // 2 % 4, :, lanes] = value[24 * owner : 24 * owner + 24].astype(BF16)

    for chunk in range(768 // step):
        lanes = slice(step * chunk, step * chunk + step)
        lay(go_ref, lanes, mm_tn(attn_ref[...], grad_attn[:, lanes]))
    for chunk in range(2 * ff // step):
        lanes = slice(step * chunk, step * chunk + step)
        lay(gi_ref, lanes, mm_tn(x_ref[...], gp_ref[:, lanes]))
    for chunk in range(ff // step):
        lanes = slice(step * chunk, step * chunk + step)
        wide_ref[lanes, :] = mm_tn(act_ref[:, lanes], branch)
    part = ff // 32
    for owner in range(32):
        gd_ref[owner % 2, owner // 8, owner // 2 % 4] = wide_ref[part * owner : part * owner + part, :].astype(BF16)


class Reduce:
    def __init__(self, part, bufs, send, recv, index, first):
        _, _, self.z, self.y, core = places()
        self.core_recv, self.acc, self.recv1, self.acc1, self.recv2 = bufs
        self.send, self.recv, self.index, self.first = send, recv, index, first
        self.second = "z" if first == "y" else "y"
        self.local = pltpu.make_async_copy(part.at[core], self.acc, send.at[index, 7])
        self.hops = [[(part.at[1 - core], self.core_recv, "c", 1)], [], []]
        for step in (1, 2, 3):
            one = (self.y + step) % 4
            two = (self.z + step) % 4
            if first == "y":
                lines, rest = self.acc.at[:, one], two
            else:
                lines, rest = self.acc.at[two], one
            self.hops[1].append((lines, self.recv1.at[step - 1], first, step))
            self.hops[2].append((self.acc1.at[rest], self.recv2.at[step - 1], self.second, step))

    def copies(self, hop):
        base = (0, 1, 4)[hop]
        return [
            remote(src, dst, self.send.at[self.index, base + n], self.recv.at[self.index, base + n], peer(axis, step))
            for n, (src, dst, axis, step) in enumerate(self.hops[hop])
        ]

    def start(self, hop):
        if hop == 0:
            self.local.start()
        for copy in self.copies(hop):
            copy.start()

    def arrive(self, hop):
        if hop == 0:
            self.local.wait()
        for copy in self.copies(hop):
            copy.wait_recv()
        if hop == 0:

            @pl.loop(0, 16)
            def _(index):
                z, y = index // 4, index % 4
                total = self.acc[z, y].astype(F32) + self.core_recv[z, y].astype(F32)
                self.acc[z, y] = total.astype(BF16)

        elif hop == 1:

            @pl.loop(0, 4)
            def _(index):
                own = self.acc[index, self.y] if self.first == "y" else self.acc[self.z, index]
                total = own.astype(F32)
                for step in range(3):
                    total += self.recv1[step, index].astype(F32)
                self.acc1[index] = total.astype(BF16)

        else:
            total = self.acc1[self.z if self.first == "y" else self.y].astype(F32)
            for step in range(3):
                total += self.recv2[step].astype(F32)
            return total

    def finish(self):
        for hop in range(3):
            for copy in self.copies(hop):
                copy.wait_send()


def reduce_scratch(rows, width):
    return [
        pltpu.VMEM((4, 4, rows, width), BF16),
        pltpu.VMEM((4, 4, rows, width), BF16),
        pltpu.VMEM((3, 4, rows, width), BF16),
        pltpu.VMEM((4, rows, width), BF16),
        pltpu.VMEM((3, rows, width), BF16),
    ]


class Cross:
    def __init__(self, sources, targets, send, recv, index):
        self.list = [
            remote(src, dst, send.at[index, n], recv.at[index, n], peer("x", n + 1))
            for n, (src, dst) in enumerate(zip(sources, targets))
        ]

    def start(self):
        for copy in self.list:
            copy.start()

    def arrive(self):
        for copy in self.list:
            copy.wait_recv()

    def finish(self):
        for copy in self.list:
            copy.wait_send()


def column_block(value, start, width):
    total = value.shape[1]
    if start:
        value = roll(value, total - start)
    return value[:, :width]


def backward_kernel(
    len_ref, gmix_ref, q_ref, k_ref, v_ref, o_ref, xt_ref, cos_ref, sin_ref, hid_ref, gres_ref,
    wi_ref, wq_ref, gain1_ref, gain2_ref, one_ref, gi_ref, go_ref, gd_ref,
    in_ref, gq_out, go_out, gi_out, gd_out, gain1_out, gain2_out,
    g_ref, d_ref, dq_ref, dk_ref, dv_ref, acc_ref, stage_ref, got_ref, gq_ref, full_ref,
    one_full, w_ref, m_ref, xi_ref, xo_ref, xd_ref, xg_ref, xm_ref, ri_ref, ro_ref, rd_ref, rg_ref, rm_ref,
    gather_send, gather_recv, red_send, red_recv, x_send, x_recv,
    *bufs,
):
    seq, _, _, _, _ = places()
    bounds = doc_bounds(len_ref)
    greet()

    def by_rank(ref):
        return [ref.at[(seq + step) % SEQ] for step in (1, 2, 3)]

    def by_step(ref):
        return [ref.at[step] for step in range(3)]

    gmix = Cross(by_rank(gmix_ref), [g_ref.at[seq]] * 3, x_send, x_recv, 0)
    gmix.start()
    red_in = Reduce(gi_ref, bufs[0:5], red_send, red_recv, 0, "y")
    red_out = Reduce(go_ref, bufs[5:10], red_send, red_recv, 1, "z")
    red_down = Reduce(gd_ref, bufs[10:15], red_send, red_recv, 2, "z")
    red_own = Reduce(m_ref, bufs[15:20], red_send, red_recv, 3, "y")
    early = (red_in, red_out, red_down)
    for red in early:
        red.start(0)
    one = Gather(one_ref, one_full, gather_send, gather_recv, 0, "z")
    one.start(0)
    g_ref[seq] = gmix_ref[seq]
    order = edge_order(bounds[3], False)
    back = edge_order(bounds[3], True)
    low = low_lanes(HALF)
    gmix.arrive()
    for head in range(LOCAL):
        for source in range(SEQ):
            packed = g_ref[source, head].astype(F32)
            d_ref[head, TOK * source : TOK * source + HALF, :] = jnp.where(low, packed, 0.0).astype(BF16)
            d_ref[head, TOK * source + HALF : TOK * source + TOK, :] = jnp.where(
                low, roll(packed, 64), 0.0
            ).astype(BF16)
        short, long = permute_edge(order, d_ref, head)
        d_ref[head, 0:HALF, :] = short
        d_ref[head, PACK - HALF : PACK, :] = long

    @pl.loop(0, PACK // HALF)
    def _(block):
        rows = pl.ds(pl.multiple_of(block * HALF, HALF), HALF)
        for head in range(LOCAL):
            grad = d_ref[head, rows, :].astype(F32)
            inner = jnp.sum(grad * o_ref[head, rows, :].astype(F32), axis=1, keepdims=True)
            d_ref[head, rows, :] = extra_lanes(grad, inner).astype(BF16)

    mask = short_mask(bounds)
    step_rows = 224

    def attend_back(head):
        acc_ref[0:HALF, :] = backward_rows(
            head, pl.ds(0, HALF), pl.ds(0, HALF), mask, q_ref, k_ref, v_ref, d_ref, dk_ref, dv_ref
        )
        acc_ref[HALF:PACK, :] = jnp.zeros((LONGEST, 128), F32)

        @pl.loop(0, LONGEST // (2 * step_rows))
        def _(block):
            terms = []
            for part in range(2):
                start = HALF + block * (2 * step_rows) + part * step_rows
                rows = pl.ds(pl.multiple_of(start, 32), step_rows)
                terms.append(
                    backward_rows(
                        head, rows, pl.ds(HALF, LONGEST), None, q_ref, k_ref, v_ref, d_ref, dk_ref, dv_ref
                    )
                )
            acc_ref[HALF:PACK, :] += terms[0] + terms[1]

        dq_ref[head] = (acc_ref[...] * 0.125).astype(BF16)
        for ref in (dq_ref, dk_ref, dv_ref):
            top, bottom = permute_edge(back, ref, head)
            ref[head, 0:HALF, :] = top
            ref[head, PACK - HALF : PACK, :] = bottom

        @pl.loop(0, SEQ)
        def _(dest):
            top = pl.ds(pl.multiple_of(dest * TOK, TOK), HALF)
            bottom = pl.ds(pl.multiple_of(dest * TOK + HALF, HALF), HALF)
            cosine = pack_halves(cos_ref[top, :], cos_ref[bottom, :])
            sine = pack_halves(sin_ref[top, :], sin_ref[bottom, :])
            for kind, ref in enumerate((dq_ref, dk_ref, dv_ref)):
                packed = pack_halves(ref[head, top, :].astype(F32), ref[head, bottom, :].astype(F32))
                if kind < 2:
                    packed = packed * cosine - turned(packed) * sine
                stage_ref[dest, head, kind] = packed.astype(BF16)

        got_ref[seq, head] = stage_ref[seq, head]
        sources = [stage_ref.at[(seq + step) % SEQ, head] for step in (1, 2, 3)]
        cross = Cross(sources, [got_ref.at[seq, head]] * 3, x_send, x_recv, 1 + head)
        cross.start()
        return cross

    for red in early:
        red.arrive(0)
        red.start(1)
    one.arrive(0)
    one.start(1)
    crosses = [attend_back(0)]
    for red in early:
        red.arrive(1)
        red.start(2)
    one.arrive(1)
    one.start(2)
    crosses.append(attend_back(1))
    ff = wi_ref.shape[1] // 2
    rows_in = red_in.arrive(2)
    rows_out = red_out.arrive(2)
    rows_down = red_down.arrive(2)

    def share(value, ref, width):
        for dest in range(SEQ):
            ref[dest] = column_block(value, width * dest, width).astype(BF16)

    share(rows_in, xi_ref, ff // 2)
    share(rows_out, xo_ref, HALF)
    share(rows_down, xd_ref, HALF)
    gain = jnp.sum(rows_in * wi_ref[...].astype(F32), axis=1, keepdims=True)
    xg_ref[0] = jnp.broadcast_to(gain, (24, 128))
    late = [
        Cross(by_rank(xi_ref), by_step(ri_ref), x_send, x_recv, 4),
        Cross(by_rank(xo_ref), by_step(ro_ref), x_send, x_recv, 5),
        Cross(by_rank(xd_ref), by_step(rd_ref), x_send, x_recv, 6),
        Cross([xg_ref.at[0]] * 3, by_step(rg_ref.at[0]), x_send, x_recv, 7),
    ]
    for cross in late:
        cross.start()
    crosses.append(attend_back(2))

    for dest in range(SEQ):
        top = slice(TOK * dest, TOK * dest + HALF)
        bottom = slice(TOK * dest + HALF, TOK * dest + TOK)
        for chunk in range(5):
            lanes = slice(128 * chunk, 128 * chunk + 128)
            index = 2 * chunk
            first = stage_ref[dest, index % 3, index // 3].astype(F32)
            index = min(index + 1, 8)
            second = stage_ref[dest, index % 3, index // 3].astype(F32)
            gq_ref[top, lanes] = pack_halves(first, second).astype(BF16)
            gq_ref[bottom, lanes] = jnp.where(low, roll(first, 64), second).astype(BF16)
    total = mm(xt_ref[0], gq_ref[0:TOK, :])
    for block in range(1, SEQ):
        total += mm(xt_ref[block], gq_ref[TOK * block : TOK * block + TOK, :])
    for owner in range(32):
        m_ref[owner % 2, owner // 8, owner // 2 % 4] = total[24 * owner : 24 * owner + 24, :576].astype(BF16)
    red_own.start(0)

    one.arrive(2)
    for pair in range(16):
        z, y = pair // 4, pair % 4
        rows = jnp.concatenate([one_full[z, y, 0].astype(F32), one_full[z, y, 1].astype(F32)], axis=0)
        w_ref[48 * pair : 48 * pair + 48, :] = rows.astype(BF16)
    red_own.arrive(0)
    red_own.start(1)

    for cross in late:
        cross.arrive()

    def collect(own, ref):
        return own.astype(F32) + ref[0].astype(F32) + ref[1].astype(F32) + ref[2].astype(F32)

    gi_out[...] = collect(xi_ref[seq], ri_ref) * gain2_ref[...]
    go_out[...] = collect(xo_ref[seq], ro_ref)
    gd_out[...] = collect(xd_ref[seq], rd_ref)
    gain2_out[...] = collect(xg_ref[0], rg_ref.at[0])

    for cross in crosses:
        cross.arrive()
    red_own.arrive(1)
    red_own.start(2)
    for chunk in range(18):
        pair = []
        for index in (2 * chunk, 2 * chunk + 1):
            kind, head = index // HEADS, index % HEADS
            pair.append(got_ref[head // 3, head % 3, kind].astype(F32))
        first, second = pair
        lanes = slice(128 * chunk, 128 * chunk + 128)
        full_ref[0:HALF, lanes] = pack_halves(first, second).astype(BF16)
        full_ref[HALF:TOK, lanes] = jnp.where(low, roll(first, 64), second).astype(BF16)
    rows_own = red_own.arrive(2)
    gain = jnp.sum(rows_own * wq_ref[...].astype(F32), axis=1, keepdims=True)
    xg_ref[1] = jnp.broadcast_to(gain, (24, 128))
    wide = jnp.concatenate([rows_own, jnp.zeros((24, 64), F32)], axis=1)
    for kind in range(3):
        xm_ref[kind] = column_block(wide, HALF * kind, HALF).astype(BF16)
    rm_ref[seq] = xm_ref[...]
    last = [
        Cross([xm_ref] * 3, [rm_ref.at[seq]] * 3, x_send, x_recv, 8),
        Cross([xg_ref.at[1]] * 3, by_step(rg_ref.at[1]), x_send, x_recv, 9),
    ]
    for cross in last:
        cross.start()
    grad = mm_nt(full_ref[...], w_ref[...])
    xhat, scale = norm_parts(hid_ref[...].astype(F32))
    grad = scale * (
        grad
        - jnp.mean(grad, axis=-1, keepdims=True)
        - xhat * jnp.mean(grad * xhat, axis=-1, keepdims=True)
    )
    in_ref[...] = gres_ref[...] + grad
    for cross in last:
        cross.arrive()
    for place in range(3):
        index = 3 * seq + place
        gq_out[place] = rm_ref[index % 4, index // 4].astype(F32) * gain1_ref[...]
    gain1_out[...] = collect(xg_ref[1], rg_ref.at[1])
    one.finish()
    for item in (*early, red_own, gmix, *crosses, *late, *last):
        item.finish()


SMEM = pl.BlockSpec(memory_space=pltpu.SMEM)
VMEM = pl.BlockSpec(memory_space=pltpu.VMEM)
ANY = pl.BlockSpec(memory_space=pl.ANY)


def shape(*dims, dtype=BF16):
    return jax.ShapeDtypeStruct(dims, dtype)


def call(kernel, args, outs, scratch=(), arg_specs=None, out_specs=None, collective=None):
    return pl.pallas_call(
        kernel,
        out_shape=outs,
        in_specs=arg_specs or [VMEM] * len(args),
        out_specs=out_specs or jax.tree.map(lambda _: VMEM, outs),
        scratch_shapes=list(scratch),
        compiler_params=pltpu.CompilerParams(
            vmem_limit_bytes=VMEM_LIMIT,
            collective_id=collective,
            has_side_effects=collective is not None,
        ),
    )(*args)


def body(hidden, lengths, attn_gain, w_qkv, w_attn_out, mlp_gain, w_in, w_mlp_out, cotangent):
    rank = lax.axis_index("seq")
    lengths = lengths[0]
    gain_one = attn_gain.astype(F32)[:, None]
    gain_two = mlp_gain.astype(F32)[:, None]
    w_one = (w_qkv.astype(F32) * gain_one).astype(BF16)
    w_two = (w_in.astype(F32) * gain_two).astype(BF16)
    own = lax.dynamic_index_in_dim(w_one.reshape(-1, 3, SEQ, 192), rank, 2, keepdims=False).reshape(-1, 576)

    lane = jnp.arange(128, dtype=jnp.int32) % 32
    inverse = jnp.exp(lane.astype(F32) * (-2.0 * math.log(160000.0) / HEAD_DIM))
    inverse = jnp.broadcast_to(inverse, (8, 128))
    head_shape = shape(LOCAL, PACK, 128)
    ff = w_mlp_out.shape[0] * 32

    def spread(x):
        return shape(4, 4, 2, *x.shape)

    q, k, v, o, mix, xt, cosine, sine, two_full, out_full, down_full = call(
        forward_kernel,
        (lengths, inverse, own, hidden[0], w_two, w_attn_out, w_mlp_out),
        (
            head_shape, head_shape, head_shape, head_shape,
            shape(SEQ, LOCAL, HALF, 128), shape(SEQ, 768, TOK),
            shape(PACK, 128, dtype=F32), shape(PACK, 128, dtype=F32),
            spread(w_two), spread(w_attn_out), spread(w_mlp_out),
        ),
        (
            pltpu.VMEM((SEQ, TOK, 768), BF16),
            pltpu.VMEM((4, 4, 2, 24, 576), BF16),
            pltpu.VMEM((768, 576), BF16),
            pltpu.VMEM((SEQ, LOCAL, HALF, 128), BF16),
            pltpu.SemaphoreType.DMA((4, 8)),
            pltpu.SemaphoreType.DMA((4, 8)),
            pltpu.SemaphoreType.DMA((4,)),
            pltpu.SemaphoreType.DMA((4,)),
            pltpu.SemaphoreType.DMA((4,)),
            pltpu.SemaphoreType.DMA((4,)),
        ),
        [SMEM, VMEM, VMEM, VMEM, ANY, ANY, ANY],
        (VMEM,) * 8 + (ANY,) * 3,
        collective=1,
    )
    two_full, out_full, down_full = (x.reshape(-1, x.shape[-1]) for x in (two_full, out_full, down_full))
    output, grad_res, grad_mix, grad_out, grad_in, grad_down = call(
        middle_kernel,
        (hidden[0], mix, out_full, two_full, down_full, cotangent[0]),
        (
            shape(TOK, 768),
            shape(TOK, 768, dtype=F32),
            shape(SEQ, LOCAL, HALF, 128),
            shape(2, 4, 4, 24, 768),
            shape(2, 4, 4, 24, 2 * ff),
            shape(2, 4, 4, ff // 32, 768),
        ),
        (
            pltpu.VMEM((TOK, 768), BF16),
            pltpu.VMEM((TOK, 768), BF16),
            pltpu.VMEM((TOK, 2 * ff), F32),
            pltpu.VMEM((TOK, ff), BF16),
            pltpu.VMEM((TOK, 2 * ff), BF16),
            pltpu.VMEM((ff, 768), F32),
        ),
    )
    heads = pltpu.VMEM((LOCAL, PACK, 128), BF16)
    stage = pltpu.VMEM((SEQ, LOCAL, 3, HALF, 128), BF16)
    own_raw = lax.dynamic_index_in_dim(w_qkv.reshape(-1, 3, SEQ, 192), rank, 2, keepdims=False).reshape(-1, 576)
    input_grad, grad_qkv, grad_out, grad_in, grad_down, grad_gain_one, grad_gain_two = call(
        backward_kernel,
        (
            lengths, grad_mix, q, k, v, o, xt, cosine, sine, hidden[0], grad_res,
            w_in, own_raw, gain_one, gain_two, w_one, grad_in, grad_out, grad_down,
        ),
        (
            shape(TOK, 768, dtype=F32),
            shape(3, 24, 192, dtype=F32),
            shape(24, 192, dtype=F32),
            shape(24, ff // 2, dtype=F32),
            shape(ff // 32, 192, dtype=F32),
            shape(24, 128, dtype=F32),
            shape(24, 128, dtype=F32),
        ),
        (
            pltpu.VMEM((SEQ, LOCAL, HALF, 128), BF16),
            heads, heads, heads, heads,
            pltpu.VMEM((PACK, 128), F32),
            stage, stage,
            pltpu.VMEM((PACK, 640), BF16),
            pltpu.VMEM((TOK, 2304), BF16),
            pltpu.VMEM((4, 4, 2, 24, 2304), BF16),
            pltpu.VMEM((768, 2304), BF16),
            pltpu.VMEM((2, 4, 4, 24, 576), BF16),
            pltpu.VMEM((SEQ, 24, ff // 2), BF16),
            pltpu.VMEM((SEQ, 24, HALF), BF16),
            pltpu.VMEM((SEQ, ff // 32, HALF), BF16),
            pltpu.VMEM((2, 24, 128), F32),
            pltpu.VMEM((3, 24, HALF), BF16),
            pltpu.VMEM((3, 24, ff // 2), BF16),
            pltpu.VMEM((3, 24, HALF), BF16),
            pltpu.VMEM((3, ff // 32, HALF), BF16),
            pltpu.VMEM((2, 3, 24, 128), F32),
            pltpu.VMEM((SEQ, 3, 24, HALF), BF16),
            pltpu.SemaphoreType.DMA((1, 8)),
            pltpu.SemaphoreType.DMA((1, 8)),
            pltpu.SemaphoreType.DMA((4, 8)),
            pltpu.SemaphoreType.DMA((4, 8)),
            pltpu.SemaphoreType.DMA((10, 3)),
            pltpu.SemaphoreType.DMA((10, 3)),
            *reduce_scratch(24, 2 * ff),
            *reduce_scratch(24, 768),
            *reduce_scratch(ff // 32, 768),
            *reduce_scratch(24, 576),
        ),
        [SMEM] + [VMEM] * 14 + [ANY] * 4,
        collective=2,
    )
    return (
        output[None],
        input_grad[None],
        grad_gain_one[:, 0],
        grad_qkv.transpose(1, 0, 2).reshape(-1, 576),
        grad_out,
        grad_gain_two[:, 0],
        grad_in,
        grad_down,
    )


def solution(mesh):
    in_specs = (
        P("fsdp", "seq", None),
        P("fsdp", None),
        P("fsdp"),
        P("fsdp", None),
        P("fsdp", None),
        P("fsdp"),
        P("fsdp", None),
        P("fsdp", None),
        P("fsdp", "seq", None),
    )
    out_specs = (
        P("fsdp", "seq", None),
        P("fsdp", "seq", None),
        P("fsdp"),
        P("fsdp", "seq"),
        P("fsdp", "seq"),
        P("fsdp"),
        P("fsdp", "seq"),
        P("fsdp", "seq"),
    )
    return jax.shard_map(body, mesh=mesh, in_specs=in_specs, out_specs=out_specs, check_vma=False)
```

```python
import math

import jax
import jax.numpy as jnp
import numpy as np
from jax import lax
from jax.experimental import pallas as pl
from jax.experimental.pallas import tpu as pltpu
from jax.sharding import PartitionSpec as P

HEADS = 12
HEAD_DIM = 64
LONGEST = 1344
SEQ = 4
LOCAL = 3
TOK = 384
HALF = 192
PACK = 1536
F32 = jnp.float32
BF16 = jnp.bfloat16
VMEM_LIMIT = 60 * 1024 * 1024


def mm(left, right):
    return jnp.dot(left, right, preferred_element_type=F32)


def mm_nt(left, right):
    return lax.dot_general(left, right, (((1,), (1,)), ((), ())), preferred_element_type=F32)


def mm_tn(left, right):
    return lax.dot_general(left, right, (((0,), (0,)), ((), ())), preferred_element_type=F32)


def iota(shape, dim):
    return lax.broadcasted_iota(jnp.int32, shape, dim)


def roll(x, shift):
    return pltpu.roll(x, shift, 1)


def low_lanes(rows):
    return iota((rows, 128), 1) < 64


def turned(x):
    lane = iota(x.shape, 1)
    first = (lane & 32) == 0
    return jnp.where(first, roll(x, 96), roll(x, 32))


def norm_parts(values):
    average = jnp.mean(values, axis=-1, keepdims=True)
    centred = values - average
    variance = jnp.mean(centred * centred, axis=-1, keepdims=True)
    scale = lax.rsqrt(variance + 1e-05)
    return centred * scale, scale


def doc_bounds(len_ref):
    first = len_ref[0]
    second = first + len_ref[1]
    third = second + len_ref[2]
    start = jnp.where(
        len_ref[0] == LONGEST,
        0,
        jnp.where(len_ref[1] == LONGEST, first, jnp.where(len_ref[2] == LONGEST, second, third)),
    )
    return first, second, third, start


def edge_order(start, transposed):
    stored = iota((2 * HALF, 2 * HALF), 1 if transposed else 0)
    edge = iota((2 * HALF, 2 * HALF), 0 if transposed else 1)
    source = stored + (HALF + start)
    source = jnp.where(source >= 2 * HALF, source - 2 * HALF, source)
    return jnp.where(edge == source, 1.0, 0.0).astype(BF16)


def short_mask(bounds):
    first, second, third, start = bounds

    def numbers(dim):
        row = iota((HALF, HALF), dim) + (HALF + start)
        row = jnp.where(row >= 2 * HALF, row - 2 * HALF, row)
        place = jnp.where(row >= HALF, row + (PACK - 2 * HALF), row)
        return (
            jnp.where(place >= first, 1, 0)
            + jnp.where(place >= second, 1, 0)
            + jnp.where(place >= third, 1, 0)
        )

    return numbers(0) == numbers(1)


def extra_lanes(base, column):
    lane = iota(base.shape, 1)
    rest = -column
    top = rest.astype(BF16).astype(F32)
    rest = rest - top
    middle = rest.astype(BF16).astype(F32)
    rest = rest - middle
    return jnp.where(
        lane < 64,
        base,
        jnp.where(lane == 64, top, jnp.where(lane == 65, middle, jnp.where(lane == 66, rest, 0.0))),
    )


def permute_edge(order, ref, head):
    edge = jnp.concatenate([ref[head, 0:HALF, :], ref[head, PACK - HALF : PACK, :]], axis=0)
    moved = mm(order, edge).astype(BF16)
    return moved[0:HALF], moved[HALF : 2 * HALF]


def pack_halves(top, bottom):
    return jnp.where(low_lanes(top.shape[0]), top, roll(bottom, 64))


def rope_rows(len_ref, inv_ref, block, cos_ref, sin_ref):
    rows = pl.ds(pl.multiple_of(block * TOK, TOK), TOK)
    place = iota((TOK, 128), 0) + block * TOK
    first = len_ref[0]
    second = first + len_ref[1]
    third = second + len_ref[2]
    starts = (
        jnp.where(iota((8, 128), 0) == 1, first, 0)
        + jnp.where(iota((8, 128), 0) == 2, second, 0)
        + jnp.where(iota((8, 128), 0) == 3, third, 0)
    )
    shift = starts.astype(F32) * inv_ref[...]
    shift_cos, shift_sin = jnp.cos(shift), jnp.sin(shift)

    def pick(table):
        return jnp.where(
            place >= third,
            table[3:4],
            jnp.where(place >= second, table[2:3], jnp.where(place >= first, table[1:2], table[0:1])),
        )

    back_cos, back_sin = pick(shift_cos), pick(shift_sin)
    cosine, sine = cos_ref[rows, :], sin_ref[rows, :]
    cos_ref[rows, :] = cosine * back_cos + sine * back_sin
    sine = sine * back_cos - cosine * back_sin
    sin_ref[rows, :] = jnp.where((iota((TOK, 128), 1) & 32) == 0, -sine, sine)


def project_block(block, hid_ref, w_ref, cos_ref, sin_ref, q_ref, k_ref, v_ref, xt_ref):
    rows = pl.ds(pl.multiple_of(block * TOK, TOK), TOK)
    xhat = norm_parts(hid_ref[block].astype(F32))[0].astype(BF16)
    xt_ref[block] = jnp.transpose(xhat)
    qkv = mm(xhat, w_ref[...])
    cosine, sine = cos_ref[rows, :], sin_ref[rows, :]
    lane = iota((TOK, 128), 1)
    low = lane < 64
    ones = jnp.where(lane < 67, 1.0, 0.0)
    for chunk in range(5):
        part = qkv[:, 128 * chunk : min(128 * chunk + 128, 576)]
        if chunk == 4:
            part = jnp.concatenate([part, part], axis=1)
        if chunk < 3:
            part = part * cosine + turned(part) * sine
        for odd in range(2):
            index = 2 * chunk + odd
            if index == 9:
                continue
            piece = roll(part, 64) if odd else part
            kind, head = index // 3, index % 3
            if kind == 0:
                q_ref[head, rows, :] = (jnp.where(low, piece, 0.0).astype(BF16).astype(F32) * 0.125).astype(BF16)
            elif kind == 1:
                k_ref[head, rows, :] = jnp.where(low, piece, ones).astype(BF16)
            else:
                v_ref[head, rows, :] = jnp.where(low, piece, ones).astype(BF16)


def attend_rows(head, rows, keys, mask, q_ref, k_ref, v_ref, o_ref):
    query = q_ref[head, rows, :]
    scores = mm_nt(query, k_ref[head, keys, :])
    if mask is not None:
        scores = jnp.where(mask, scores, -1e9)
    highest = jnp.max(scores, axis=1, keepdims=True)
    weights = jnp.exp(scores - highest).astype(BF16)
    mixed = mm(weights, v_ref[head, keys, :])
    total = mixed[:, 64:65]
    lane = iota(mixed.shape, 1)
    o_ref[head, rows, :] = jnp.where(lane < 64, mixed * (1.0 / total), 0.0).astype(BF16)
    q_ref[head, rows, :] = extra_lanes(query.astype(F32), highest + jnp.log(total)).astype(BF16)


def places():
    seq, fsdp = lax.axis_index("seq"), lax.axis_index("fsdp")
    return seq, fsdp, fsdp // 8, (fsdp // 2) % 4, fsdp % 2


def peer(axis, step):
    seq, fsdp, z, y, core = places()
    if axis == "x":
        return ((seq + step) % SEQ, fsdp)
    if axis == "y":
        return (seq, z * 8 + ((y + step) % 4) * 2 + core)
    if axis == "z":
        return (seq, ((z + step) % 4) * 8 + y * 2 + core)
    return (seq, fsdp + 1 - 2 * core)


def remote(source, target, send_sem, recv_sem, device):
    return pltpu.make_async_remote_copy(
        src_ref=source,
        dst_ref=target,
        send_sem=send_sem,
        recv_sem=recv_sem,
        device_id=device,
        device_id_type=pl.DeviceIdType.MESH,
    )


ALL_PEERS = [(axis, step) for axis in "xyz" for step in (1, 2, 3)] + [("c", 1)]


def greet():
    barrier = pltpu.get_barrier_semaphore()
    for axis, step in ALL_PEERS:
        pl.semaphore_signal(barrier, inc=1, device_id=peer(axis, step), device_id_type=pl.DeviceIdType.MESH)
    pl.semaphore_wait(barrier, len(ALL_PEERS))


class Gather:
    def __init__(self, shard, full, send, recv, index, first):
        _, _, z, y, core = places()
        self.send, self.recv, self.index = send, recv, index
        mine = full.at[z, y, core]
        if first == "y":
            second, at = "z", z

            def line(k, half):
                return full.at[k % 4, half, core]

        else:
            second, at = "y", y

            def line(k, half):
                return full.at[half, k % 4, core]

        whole, low, high = pl.ds(0, 4), pl.ds(0, 2), pl.ds(2, 2)
        self.hops = (
            [(shard, mine, first, step) for step in (1, 2, 3)],
            [(line(at, whole), line(at, whole), second, step) for step in (1, 3)],
            [
                (line(at + 3, low), line(at + 3, low), second, 1),
                (line(at + 1, high), line(at + 1, high), second, 3),
            ],
            [(full.at[:, :, core], full.at[:, :, core], "c", 1)],
        )
        self.local = pltpu.make_async_copy(shard, mine, send.at[index, 8])

    def copies(self, hop):
        base = (0, 3, 5, 7)[hop]
        return [
            remote(src, dst, self.send.at[self.index, base + n], self.recv.at[self.index, base + n], peer(axis, step))
            for n, (src, dst, axis, step) in enumerate(self.hops[hop])
        ]

    def start(self, hop):
        if hop == 0:
            self.local.start()
        for copy in self.copies(hop):
            copy.start()

    def arrive(self, hop):
        if hop == 0:
            self.local.wait()
        for copy in self.copies(hop):
            copy.wait_recv()

    def advance(self, hop):
        self.arrive(hop)
        self.start(hop + 1)

    def finish(self):
        for hop in range(4):
            for copy in self.copies(hop):
                copy.wait_send()


def forward_kernel(
    len_ref, inv_ref, cos_in, sin_in, own_ref, hid_in, two_ref, out_ref, down_ref, one_ref,
    q_ref, k_ref, v_ref, o_ref, mix_ref, xt_ref, cos_ref, sin_ref, two_full, out_full, down_full, one_full,
    hid_ref, own_full, w_ref, stage_ref, gather_send, gather_recv, hid_send, hid_recv, mix_send, mix_recv, table_sem,
):
    seq, fsdp, _, _, _ = places()
    bounds = doc_bounds(len_ref)
    right, left = (seq + 1) % SEQ, (seq + 3) % SEQ
    tables = (
        pltpu.make_async_copy(cos_in, cos_ref, table_sem.at[0]),
        pltpu.make_async_copy(sin_in, sin_ref, table_sem.at[1]),
    )
    for copy in tables:
        copy.start()
    greet()
    own = Gather(own_ref, own_full, gather_send, gather_recv, 0, "y")
    two = Gather(two_ref, two_full, gather_send, gather_recv, 1, "y")
    out = Gather(out_ref, out_full, gather_send, gather_recv, 2, "y")
    down = Gather(down_ref, down_full, gather_send, gather_recv, 3, "z")
    one = Gather(one_ref, one_full, gather_send, gather_recv, 4, "z")
    weights = (out, two, down, one)
    own.start(0)
    to_right = remote(hid_in, hid_ref.at[seq], hid_send.at[0], hid_recv.at[0], peer("x", 1))
    to_left = remote(hid_in, hid_ref.at[seq], hid_send.at[1], hid_recv.at[1], peer("x", 3))
    to_right.start()
    to_left.start()
    hid_ref[seq] = hid_in[...]
    for weight in weights:
        weight.start(0)
    for copy in tables:
        copy.wait()
    own.advance(0)
    for block in range(SEQ):
        rope_rows(len_ref, inv_ref, block, cos_ref, sin_ref)
    own.advance(1)
    for weight in weights:
        weight.advance(0)
    own.advance(2)
    own.arrive(3)
    for pair in range(16):
        z, y = pair // 4, pair % 4
        rows = jnp.concatenate([own_full[z, y, 0].astype(F32), own_full[z, y, 1].astype(F32)], axis=0)
        w_ref[48 * pair : 48 * pair + 48, :] = rows.astype(BF16)

    def project(block):
        project_block(block, hid_ref, w_ref, cos_ref, sin_ref, q_ref, k_ref, v_ref, xt_ref)

    project(seq)
    to_right.wait_recv()
    on_right = remote(
        hid_ref.at[left, pl.ds(0, HALF)], hid_ref.at[left, pl.ds(0, HALF)],
        hid_send.at[2], hid_recv.at[2], peer("x", 1),
    )
    on_right.start()
    to_left.wait_recv()
    on_left = remote(
        hid_ref.at[right, pl.ds(HALF, HALF)], hid_ref.at[right, pl.ds(HALF, HALF)],
        hid_send.at[3], hid_recv.at[3], peer("x", 3),
    )
    on_left.start()
    project(left)
    project(right)
    on_right.wait_recv()
    on_left.wait_recv()
    project((seq + 2) % SEQ)

    order = edge_order(bounds[3], False)
    back = edge_order(bounds[3], True)
    for ref in (q_ref, k_ref, v_ref):
        for head in range(LOCAL):
            short, long = permute_edge(order, ref, head)
            ref[head, 0:HALF, :] = short
            ref[head, PACK - HALF : PACK, :] = long

    def attend(block):
        rows = pl.ds(pl.multiple_of(block * HALF, HALF), HALF)
        for head in range(LOCAL):
            attend_rows(head, rows, pl.ds(HALF, PACK - HALF), None, q_ref, k_ref, v_ref, o_ref)

    def mix_copy(dest):
        return remote(stage_ref.at[dest], mix_ref.at[seq], mix_send.at[dest], mix_recv.at[seq], (dest, fsdp))

    def give(dest, head, top, bottom):
        stage_ref[dest, head] = pack_halves(top.astype(F32), bottom.astype(F32)).astype(BF16)

    def hand_over(dest):
        @pl.when(seq != dest)
        def _():
            mix_copy(dest).start()

    def inner_dest(dest):
        pl.loop(2 * dest, 2 * dest + 2)(attend)
        for head in range(LOCAL):
            first = TOK * dest
            give(dest, head, o_ref[head, first : first + HALF, :], o_ref[head, first + HALF : first + TOK, :])
        hand_over(dest)

    inner_dest(1)
    inner_dest(2)
    for weight in weights:
        weight.advance(1)
    mask = short_mask(bounds)
    for head in range(LOCAL):
        attend_rows(head, pl.ds(0, HALF), pl.ds(0, HALF), mask, q_ref, k_ref, v_ref, o_ref)

    @pl.loop(0, 3)
    def _(index):
        attend(1 + 5 * jnp.minimum(index, 1) + jnp.maximum(index - 1, 0))

    for weight in weights:
        weight.advance(2)
    for head in range(LOCAL):
        top, bottom = permute_edge(back, o_ref, head)
        give(0, head, top, o_ref[head, HALF:TOK, :])
        give(3, head, o_ref[head, 3 * TOK : 3 * TOK + HALF, :], bottom)
    hand_over(0)
    hand_over(3)
    mix_ref[seq] = stage_ref[seq]
    for weight in weights:
        weight.arrive(3)
    for weight in (own, *weights):
        weight.finish()
    for copy in (to_right, to_left, on_right, on_left):
        copy.wait_send()
    for step in (1, 2, 3):
        source = (seq + step) % SEQ
        remote(stage_ref.at[0], mix_ref.at[source], mix_send.at[0], mix_recv.at[source], peer("x", step)).wait_recv()
    for dest in range(SEQ):
        @pl.when(seq != dest)
        def _(dest=dest):
            mix_copy(dest).wait_send()


def backward_rows(head, rows, queries, mask, q_ref, k_ref, v_ref, d_ref, dk_ref, dv_ref):
    query, grad = q_ref[head, queries, :], d_ref[head, queries, :]
    key = k_ref[head, rows, :]
    shares = jnp.exp(mm_nt(key, query))
    if mask is not None:
        shares = jnp.where(mask, shares, 0.0)
    grad_scores = (shares * mm_nt(v_ref[head, rows, :], grad)).astype(BF16)
    dv_ref[head, rows, :] = mm(shares.astype(BF16), grad).astype(BF16)
    dk_ref[head, rows, :] = mm(grad_scores, query).astype(BF16)
    return mm_tn(grad_scores, key)


def middle_kernel(
    hid_ref, mix_ref, wo_ref, wi_ref, wd_full, cot_ref,
    out_ref, gres_ref, gmix_ref, go_ref, gi_ref, gd_ref,
    attn_ref, x_ref, proj_ref, act_ref, gp_ref, wide_ref, wd_ref,
):
    part = wd_full.shape[3]
    for group in range(8):
        shards = [wd_full[k // 8, k // 2 % 4, k % 2].astype(F32) for k in range(4 * group, 4 * group + 4)]
        wd_ref[4 * part * group : 4 * part * (group + 1), :] = jnp.concatenate(shards, axis=0).astype(BF16)
    low = low_lanes(HALF)
    for chunk in range(6):
        pair = []
        for index in (2 * chunk, 2 * chunk + 1):
            pair.append(mix_ref[index // 3, index % 3].astype(F32))
        one, two = pair
        lanes = slice(128 * chunk, 128 * chunk + 128)
        attn_ref[0:HALF, lanes] = pack_halves(one, two).astype(BF16)
        attn_ref[HALF:TOK, lanes] = jnp.where(low, roll(one, 64), two).astype(BF16)
    residual = hid_ref[...].astype(F32) + mm(attn_ref[...], wo_ref[...])
    xhat, scale = norm_parts(residual)
    x_ref[...] = xhat.astype(BF16)
    ff = wd_ref.shape[0]
    step = 384
    for chunk in range(2 * ff // step):
        lanes = slice(step * chunk, step * chunk + step)
        proj_ref[:, lanes] = mm(x_ref[...], wi_ref[:, lanes])
    output = residual
    branch = cot_ref[...]
    for chunk in range(ff // step):
        lanes = slice(step * chunk, step * chunk + step)
        inner = proj_ref[:, lanes]
        gate = proj_ref[:, ff + step * chunk : ff + step * chunk + step]
        phi = 0.5 * (1.0 + lax.erf(inner * math.sqrt(0.5)))
        gelu = inner * phi
        act = (gelu * gate).astype(BF16)
        act_ref[:, lanes] = act
        output = output + mm(act, wd_ref[lanes, :])
        grad_act = mm_nt(branch, wd_ref[lanes, :])
        density = jnp.exp(inner * inner * -0.5) * (1.0 / math.sqrt(2.0 * math.pi))
        gp_ref[:, lanes] = (grad_act * gate * (phi + inner * density)).astype(BF16)
        gp_ref[:, ff + step * chunk : ff + step * chunk + step] = (grad_act * gelu).astype(BF16)
    out_ref[...] = output.astype(BF16)
    grad = mm_nt(gp_ref[...], wi_ref[...])
    grad = scale * (
        grad
        - jnp.mean(grad, axis=-1, keepdims=True)
        - xhat * jnp.mean(grad * xhat, axis=-1, keepdims=True)
    )
    grad_res = branch.astype(F32) + grad
    gres_ref[...] = grad_res
    grad_attn = grad_res.astype(BF16)
    grad_mix = mm_nt(grad_attn, wo_ref[...]).astype(BF16).astype(F32)
    for chunk in range(6):
        lanes = slice(128 * chunk, 128 * chunk + 128)
        top, bottom = grad_mix[0:HALF, lanes], grad_mix[HALF:TOK, lanes]
        one = pack_halves(top, bottom)
        two = jnp.where(low, roll(top, 64), bottom)
        gmix_ref[2 * chunk // 3, 2 * chunk % 3] = one.astype(BF16)
        gmix_ref[(2 * chunk + 1) // 3, (2 * chunk + 1) % 3] = two.astype(BF16)
    def lay(ref, lanes, value):
        for owner in range(32):
            ref[owner % 2, owner // 8, owner // 2 % 4, :, lanes] = value[24 * owner : 24 * owner + 24].astype(BF16)

    for chunk in range(768 // step):
        lanes = slice(step * chunk, step * chunk + step)
        lay(go_ref, lanes, mm_tn(attn_ref[...], grad_attn[:, lanes]))
    for chunk in range(2 * ff // step):
        lanes = slice(step * chunk, step * chunk + step)
        lay(gi_ref, lanes, mm_tn(x_ref[...], gp_ref[:, lanes]))
    for chunk in range(ff // step):
        lanes = slice(step * chunk, step * chunk + step)
        wide_ref[lanes, :] = mm_tn(act_ref[:, lanes], branch)
    for owner in range(32):
        gd_ref[owner % 2, owner // 8, owner // 2 % 4] = wide_ref[part * owner : part * owner + part, :].astype(BF16)


class Reduce:
    def __init__(self, part, bufs, send, recv, index, first):
        _, _, self.z, self.y, core = places()
        self.core_recv, self.acc, self.recv1, self.acc1, self.recv2 = bufs
        self.send, self.recv, self.index, self.first = send, recv, index, first
        self.second = "z" if first == "y" else "y"
        self.local = pltpu.make_async_copy(part.at[core], self.acc, send.at[index, 7])
        self.hops = [[(part.at[1 - core], self.core_recv, "c", 1)], [], []]
        for step in (1, 2, 3):
            one = (self.y + step) % 4
            two = (self.z + step) % 4
            if first == "y":
                lines, rest = self.acc.at[:, one], two
            else:
                lines, rest = self.acc.at[two], one
            self.hops[1].append((lines, self.recv1.at[step - 1], first, step))
            self.hops[2].append((self.acc1.at[rest], self.recv2.at[step - 1], self.second, step))

    def copies(self, hop):
        base = (0, 1, 4)[hop]
        return [
            remote(src, dst, self.send.at[self.index, base + n], self.recv.at[self.index, base + n], peer(axis, step))
            for n, (src, dst, axis, step) in enumerate(self.hops[hop])
        ]

    def start(self, hop):
        if hop == 0:
            self.local.start()
        for copy in self.copies(hop):
            copy.start()

    def arrive(self, hop):
        if hop == 0:
            self.local.wait()
        for copy in self.copies(hop):
            copy.wait_recv()
        if hop == 0:

            @pl.loop(0, 16)
            def _(index):
                z, y = index // 4, index % 4
                total = self.acc[z, y].astype(F32) + self.core_recv[z, y].astype(F32)
                self.acc[z, y] = total.astype(BF16)

        elif hop == 1:

            @pl.loop(0, 4)
            def _(index):
                own = self.acc[index, self.y] if self.first == "y" else self.acc[self.z, index]
                total = own.astype(F32)
                for step in range(3):
                    total += self.recv1[step, index].astype(F32)
                self.acc1[index] = total.astype(BF16)

        else:
            total = self.acc1[self.z if self.first == "y" else self.y].astype(F32)
            for step in range(3):
                total += self.recv2[step].astype(F32)
            return total

    def finish(self):
        for hop in range(3):
            for copy in self.copies(hop):
                copy.wait_send()


def reduce_scratch(rows, width):
    return [
        pltpu.VMEM((4, 4, rows, width), BF16),
        pltpu.VMEM((4, 4, rows, width), BF16),
        pltpu.VMEM((3, 4, rows, width), BF16),
        pltpu.VMEM((4, rows, width), BF16),
        pltpu.VMEM((3, rows, width), BF16),
    ]


class Cross:
    def __init__(self, sources, targets, send, recv, index):
        self.list = [
            remote(src, dst, send.at[index, n], recv.at[index, n], peer("x", n + 1))
            for n, (src, dst) in enumerate(zip(sources, targets))
        ]

    def start(self):
        for copy in self.list:
            copy.start()

    def arrive(self):
        for copy in self.list:
            copy.wait_recv()

    def finish(self):
        for copy in self.list:
            copy.wait_send()


def column_block(value, start, width):
    total = value.shape[1]
    if start:
        value = roll(value, total - start)
    return value[:, :width]


def backward_kernel(
    len_ref, gmix_ref, q_ref, k_ref, v_ref, o_ref, xt_ref, cos_ref, sin_ref, hid_ref, gres_ref,
    wi_ref, wq_ref, gain1_ref, gain2_ref, one_in, gi_ref, go_ref, gd_ref,
    in_ref, gq_out, go_out, gi_out, gd_out, gain1_out, gain2_out,
    g_ref, d_ref, dq_ref, dk_ref, dv_ref, acc_ref, stage_ref, got_ref, gq_ref, full_ref,
    one_full, w_ref, m_ref, xi_ref, xo_ref, xd_ref, xg_ref, xm_ref, ri_ref, ro_ref, rd_ref, rg_ref, rm_ref,
    one_sem, red_send, red_recv, x_send, x_recv,
    *bufs,
):
    seq, _, _, _, _ = places()
    bounds = doc_bounds(len_ref)
    greet()

    def by_rank(ref):
        return [ref.at[(seq + step) % SEQ] for step in (1, 2, 3)]

    def by_step(ref):
        return [ref.at[step] for step in range(3)]

    gmix = Cross(by_rank(gmix_ref), [g_ref.at[seq]] * 3, x_send, x_recv, 0)
    gmix.start()
    red_in = Reduce(gi_ref, bufs[0:5], red_send, red_recv, 0, "y")
    red_out = Reduce(go_ref, bufs[5:10], red_send, red_recv, 1, "z")
    red_down = Reduce(gd_ref, bufs[10:15], red_send, red_recv, 2, "z")
    red_own = Reduce(m_ref, bufs[15:20], red_send, red_recv, 3, "y")
    early = (red_in, red_out, red_down)
    for red in early:
        red.start(0)
    one = pltpu.make_async_copy(one_in, one_full, one_sem.at[0])
    one.start()
    g_ref[seq] = gmix_ref[seq]
    order = edge_order(bounds[3], False)
    back = edge_order(bounds[3], True)
    low = low_lanes(HALF)
    gmix.arrive()
    for head in range(LOCAL):
        for source in range(SEQ):
            packed = g_ref[source, head].astype(F32)
            d_ref[head, TOK * source : TOK * source + HALF, :] = jnp.where(low, packed, 0.0).astype(BF16)
            d_ref[head, TOK * source + HALF : TOK * source + TOK, :] = jnp.where(
                low, roll(packed, 64), 0.0
            ).astype(BF16)
        short, long = permute_edge(order, d_ref, head)
        d_ref[head, 0:HALF, :] = short
        d_ref[head, PACK - HALF : PACK, :] = long

    @pl.loop(0, PACK // HALF)
    def _(block):
        rows = pl.ds(pl.multiple_of(block * HALF, HALF), HALF)
        for head in range(LOCAL):
            grad = d_ref[head, rows, :].astype(F32)
            inner = jnp.sum(grad * o_ref[head, rows, :].astype(F32), axis=1, keepdims=True)
            d_ref[head, rows, :] = extra_lanes(grad, inner).astype(BF16)

    mask = short_mask(bounds)
    step_rows = 224

    def attend_back(head):
        acc_ref[0:HALF, :] = backward_rows(
            head, pl.ds(0, HALF), pl.ds(0, HALF), mask, q_ref, k_ref, v_ref, d_ref, dk_ref, dv_ref
        )
        acc_ref[HALF:PACK, :] = jnp.zeros((LONGEST, 128), F32)

        @pl.loop(0, LONGEST // (2 * step_rows))
        def _(block):
            terms = []
            for part in range(2):
                start = HALF + block * (2 * step_rows) + part * step_rows
                rows = pl.ds(pl.multiple_of(start, 32), step_rows)
                terms.append(
                    backward_rows(
                        head, rows, pl.ds(HALF, LONGEST), None, q_ref, k_ref, v_ref, d_ref, dk_ref, dv_ref
                    )
                )
            acc_ref[HALF:PACK, :] += terms[0] + terms[1]

        dq_ref[head] = (acc_ref[...] * 0.125).astype(BF16)
        for ref in (dq_ref, dk_ref, dv_ref):
            top, bottom = permute_edge(back, ref, head)
            ref[head, 0:HALF, :] = top
            ref[head, PACK - HALF : PACK, :] = bottom

        @pl.loop(0, SEQ)
        def _(dest):
            top = pl.ds(pl.multiple_of(dest * TOK, TOK), HALF)
            bottom = pl.ds(pl.multiple_of(dest * TOK + HALF, HALF), HALF)
            cosine = pack_halves(cos_ref[top, :], cos_ref[bottom, :])
            sine = pack_halves(sin_ref[top, :], sin_ref[bottom, :])
            for kind, ref in enumerate((dq_ref, dk_ref, dv_ref)):
                packed = pack_halves(ref[head, top, :].astype(F32), ref[head, bottom, :].astype(F32))
                if kind < 2:
                    packed = packed * cosine - turned(packed) * sine
                stage_ref[dest, head, kind] = packed.astype(BF16)

        got_ref[seq, head] = stage_ref[seq, head]
        sources = [stage_ref.at[(seq + step) % SEQ, head] for step in (1, 2, 3)]
        cross = Cross(sources, [got_ref.at[seq, head]] * 3, x_send, x_recv, 1 + head)
        cross.start()
        return cross

    for red in early:
        red.arrive(0)
        red.start(1)
    crosses = [attend_back(0)]
    crosses.append(attend_back(1))
    for red in early:
        red.arrive(1)
        red.start(2)
    crosses.append(attend_back(2))
    for dest in range(SEQ):
        top = slice(TOK * dest, TOK * dest + HALF)
        bottom = slice(TOK * dest + HALF, TOK * dest + TOK)
        for chunk in range(5):
            lanes = slice(128 * chunk, 128 * chunk + 128)
            index = 2 * chunk
            first = stage_ref[dest, index % 3, index // 3].astype(F32)
            index = min(index + 1, 8)
            second = stage_ref[dest, index % 3, index // 3].astype(F32)
            gq_ref[top, lanes] = pack_halves(first, second).astype(BF16)
            gq_ref[bottom, lanes] = jnp.where(low, roll(first, 64), second).astype(BF16)
    total = mm(xt_ref[0], gq_ref[0:TOK, :])
    for block in range(1, SEQ):
        total += mm(xt_ref[block], gq_ref[TOK * block : TOK * block + TOK, :])
    for owner in range(32):
        m_ref[owner % 2, owner // 8, owner // 2 % 4] = total[24 * owner : 24 * owner + 24, :576].astype(BF16)
    red_own.start(0)

    ff = wi_ref.shape[1] // 2
    rows_in = red_in.arrive(2)
    rows_out = red_out.arrive(2)
    rows_down = red_down.arrive(2)

    def share(value, ref, width):
        for dest in range(SEQ):
            ref[dest] = column_block(value, width * dest, width).astype(BF16)

    share(rows_in, xi_ref, ff // 2)
    share(rows_out, xo_ref, HALF)
    share(rows_down, xd_ref, HALF)
    gain = jnp.sum(rows_in * wi_ref[...].astype(F32), axis=1, keepdims=True)
    xg_ref[0] = jnp.broadcast_to(gain, (24, 128))
    late = [
        Cross(by_rank(xi_ref), by_step(ri_ref), x_send, x_recv, 4),
        Cross(by_rank(xo_ref), by_step(ro_ref), x_send, x_recv, 5),
        Cross(by_rank(xd_ref), by_step(rd_ref), x_send, x_recv, 6),
        Cross([xg_ref.at[0]] * 3, by_step(rg_ref.at[0]), x_send, x_recv, 7),
    ]
    for cross in late:
        cross.start()

    one.wait()
    for pair in range(16):
        z, y = pair // 4, pair % 4
        rows = jnp.concatenate([one_full[z, y, 0].astype(F32), one_full[z, y, 1].astype(F32)], axis=0)
        w_ref[48 * pair : 48 * pair + 48, :] = rows.astype(BF16)
    red_own.arrive(0)
    red_own.start(1)

    for cross in late:
        cross.arrive()

    def collect(own, ref):
        return own.astype(F32) + ref[0].astype(F32) + ref[1].astype(F32) + ref[2].astype(F32)

    gi_out[...] = collect(xi_ref[seq], ri_ref) * gain2_ref[...]
    go_out[...] = collect(xo_ref[seq], ro_ref)
    gd_out[...] = collect(xd_ref[seq], rd_ref)
    gain2_out[...] = collect(xg_ref[0], rg_ref.at[0])

    for cross in crosses:
        cross.arrive()
    red_own.arrive(1)
    red_own.start(2)
    for chunk in range(18):
        pair = []
        for index in (2 * chunk, 2 * chunk + 1):
            kind, head = index // HEADS, index % HEADS
            pair.append(got_ref[head // 3, head % 3, kind].astype(F32))
        first, second = pair
        lanes = slice(128 * chunk, 128 * chunk + 128)
        full_ref[0:HALF, lanes] = pack_halves(first, second).astype(BF16)
        full_ref[HALF:TOK, lanes] = jnp.where(low, roll(first, 64), second).astype(BF16)
    rows_own = red_own.arrive(2)
    gain = jnp.sum(rows_own * wq_ref[...].astype(F32), axis=1, keepdims=True)
    xg_ref[1] = jnp.broadcast_to(gain, (24, 128))
    wide = jnp.concatenate([rows_own, jnp.zeros((24, 64), F32)], axis=1)
    for kind in range(3):
        xm_ref[kind] = column_block(wide, HALF * kind, HALF).astype(BF16)
    rm_ref[seq] = xm_ref[...]
    last = [
        Cross([xm_ref] * 3, [rm_ref.at[seq]] * 3, x_send, x_recv, 8),
        Cross([xg_ref.at[1]] * 3, by_step(rg_ref.at[1]), x_send, x_recv, 9),
    ]
    for cross in last:
        cross.start()
    grad = mm_nt(full_ref[...], w_ref[...])
    xhat, scale = norm_parts(hid_ref[...].astype(F32))
    grad = scale * (
        grad
        - jnp.mean(grad, axis=-1, keepdims=True)
        - xhat * jnp.mean(grad * xhat, axis=-1, keepdims=True)
    )
    in_ref[...] = gres_ref[...] + grad
    for cross in last:
        cross.arrive()
    for place in range(3):
        index = 3 * seq + place
        gq_out[place] = rm_ref[index % 4, index // 4].astype(F32) * gain1_ref[...]
    gain1_out[...] = collect(xg_ref[1], rg_ref.at[1])
    for item in (*early, red_own, gmix, *crosses, *late, *last):
        item.finish()


SMEM = pl.BlockSpec(memory_space=pltpu.SMEM)
VMEM = pl.BlockSpec(memory_space=pltpu.VMEM)
ANY = pl.BlockSpec(memory_space=pl.ANY)


def shape(*dims, dtype=BF16):
    return jax.ShapeDtypeStruct(dims, dtype)


def call(kernel, args, outs, scratch=(), arg_specs=None, out_specs=None, collective=None):
    return pl.pallas_call(
        kernel,
        out_shape=outs,
        in_specs=arg_specs or [VMEM] * len(args),
        out_specs=out_specs or jax.tree.map(lambda _: VMEM, outs),
        scratch_shapes=list(scratch),
        compiler_params=pltpu.CompilerParams(
            vmem_limit_bytes=VMEM_LIMIT,
            collective_id=collective,
            has_side_effects=collective is not None,
        ),
    )(*args)


def body(hidden, lengths, attn_gain, w_qkv, w_attn_out, mlp_gain, w_in, w_mlp_out, cotangent):
    rank = lax.axis_index("seq")
    lengths = lengths[0]
    gain_one = attn_gain.astype(F32)[:, None]
    gain_two = mlp_gain.astype(F32)[:, None]
    w_one = (w_qkv.astype(F32) * gain_one).astype(BF16)
    w_two = (w_in.astype(F32) * gain_two).astype(BF16)
    own = lax.dynamic_index_in_dim(w_one.reshape(-1, 3, SEQ, 192), rank, 2, keepdims=False).reshape(-1, 576)

    inverse = 160000.0 ** (np.arange(128) % 32 * (-2.0 / HEAD_DIM))
    angles = np.arange(PACK)[:, None] * inverse[None, :]
    cosine, sine = np.cos(angles).astype(np.float32), np.sin(angles).astype(np.float32)
    inverse = np.broadcast_to(inverse, (8, 128)).astype(np.float32)
    head_shape = shape(LOCAL, PACK, 128)
    ff = w_mlp_out.shape[0] * 32

    def spread(x):
        return shape(4, 4, 2, *x.shape)

    q, k, v, o, mix, xt, cosine, sine, two_full, out_full, down_full, one_full = call(
        forward_kernel,
        (lengths, inverse, cosine, sine, own, hidden[0], w_two, w_attn_out, w_mlp_out, w_one),
        (
            head_shape, head_shape, head_shape, head_shape,
            shape(SEQ, LOCAL, HALF, 128), shape(SEQ, 768, TOK),
            shape(PACK, 128, dtype=F32), shape(PACK, 128, dtype=F32),
            spread(w_two), spread(w_attn_out), spread(w_mlp_out), spread(w_one),
        ),
        (
            pltpu.VMEM((SEQ, TOK, 768), BF16),
            pltpu.VMEM((4, 4, 2, 24, 576), BF16),
            pltpu.VMEM((768, 576), BF16),
            pltpu.VMEM((SEQ, LOCAL, HALF, 128), BF16),
            pltpu.SemaphoreType.DMA((5, 9)),
            pltpu.SemaphoreType.DMA((5, 8)),
            pltpu.SemaphoreType.DMA((4,)),
            pltpu.SemaphoreType.DMA((4,)),
            pltpu.SemaphoreType.DMA((4,)),
            pltpu.SemaphoreType.DMA((4,)),
            pltpu.SemaphoreType.DMA((2,)),
        ),
        [SMEM, VMEM, ANY, ANY, VMEM, VMEM] + [ANY] * 4,
        (VMEM,) * 8 + (ANY,) * 4,
        collective=1,
    )
    two_full, out_full = (x.reshape(-1, x.shape[-1]) for x in (two_full, out_full))
    output, grad_res, grad_mix, grad_out, grad_in, grad_down = call(
        middle_kernel,
        (hidden[0], mix, out_full, two_full, down_full, cotangent[0]),
        (
            shape(TOK, 768),
            shape(TOK, 768, dtype=F32),
            shape(SEQ, LOCAL, HALF, 128),
            shape(2, 4, 4, 24, 768),
            shape(2, 4, 4, 24, 2 * ff),
            shape(2, 4, 4, ff // 32, 768),
        ),
        (
            pltpu.VMEM((TOK, 768), BF16),
            pltpu.VMEM((TOK, 768), BF16),
            pltpu.VMEM((TOK, 2 * ff), F32),
            pltpu.VMEM((TOK, ff), BF16),
            pltpu.VMEM((TOK, 2 * ff), BF16),
            pltpu.VMEM((ff, 768), F32),
            pltpu.VMEM((ff, 768), BF16),
        ),
    )
    heads = pltpu.VMEM((LOCAL, PACK, 128), BF16)
    stage = pltpu.VMEM((SEQ, LOCAL, 3, HALF, 128), BF16)
    own_raw = lax.dynamic_index_in_dim(w_qkv.reshape(-1, 3, SEQ, 192), rank, 2, keepdims=False).reshape(-1, 576)
    input_grad, grad_qkv, grad_out, grad_in, grad_down, grad_gain_one, grad_gain_two = call(
        backward_kernel,
        (
            lengths, grad_mix, q, k, v, o, xt, cosine, sine, hidden[0], grad_res,
            w_in, own_raw, gain_one, gain_two, one_full, grad_in, grad_out, grad_down,
        ),
        (
            shape(TOK, 768, dtype=F32),
            shape(3, 24, 192, dtype=F32),
            shape(24, 192, dtype=F32),
            shape(24, ff // 2, dtype=F32),
            shape(ff // 32, 192, dtype=F32),
            shape(24, 128, dtype=F32),
            shape(24, 128, dtype=F32),
        ),
        (
            pltpu.VMEM((SEQ, LOCAL, HALF, 128), BF16),
            heads, heads, heads, heads,
            pltpu.VMEM((PACK, 128), F32),
            stage, stage,
            pltpu.VMEM((PACK, 640), BF16),
            pltpu.VMEM((TOK, 2304), BF16),
            pltpu.VMEM((4, 4, 2, 24, 2304), BF16),
            pltpu.VMEM((768, 2304), BF16),
            pltpu.VMEM((2, 4, 4, 24, 576), BF16),
            pltpu.VMEM((SEQ, 24, ff // 2), BF16),
            pltpu.VMEM((SEQ, 24, HALF), BF16),
            pltpu.VMEM((SEQ, ff // 32, HALF), BF16),
            pltpu.VMEM((2, 24, 128), F32),
            pltpu.VMEM((3, 24, HALF), BF16),
            pltpu.VMEM((3, 24, ff // 2), BF16),
            pltpu.VMEM((3, 24, HALF), BF16),
            pltpu.VMEM((3, ff // 32, HALF), BF16),
            pltpu.VMEM((2, 3, 24, 128), F32),
            pltpu.VMEM((SEQ, 3, 24, HALF), BF16),
            pltpu.SemaphoreType.DMA((1,)),
            pltpu.SemaphoreType.DMA((4, 8)),
            pltpu.SemaphoreType.DMA((4, 8)),
            pltpu.SemaphoreType.DMA((10, 3)),
            pltpu.SemaphoreType.DMA((10, 3)),
            *reduce_scratch(24, 2 * ff),
            *reduce_scratch(24, 768),
            *reduce_scratch(ff // 32, 768),
            *reduce_scratch(24, 576),
        ),
        [SMEM] + [VMEM] * 14 + [ANY] * 4,
        collective=2,
    )
    return (
        output[None],
        input_grad[None],
        grad_gain_one[:, 0],
        grad_qkv.transpose(1, 0, 2).reshape(-1, 576),
        grad_out,
        grad_gain_two[:, 0],
        grad_in,
        grad_down,
    )


def solution(mesh):
    in_specs = (
        P("fsdp", "seq", None),
        P("fsdp", None),
        P("fsdp"),
        P("fsdp", None),
        P("fsdp", None),
        P("fsdp"),
        P("fsdp", None),
        P("fsdp", None),
        P("fsdp", "seq", None),
    )
    out_specs = (
        P("fsdp", "seq", None),
        P("fsdp", "seq", None),
        P("fsdp"),
        P("fsdp", "seq"),
        P("fsdp", "seq"),
        P("fsdp"),
        P("fsdp", "seq"),
        P("fsdp", "seq"),
    )
    return jax.shard_map(body, mesh=mesh, in_specs=in_specs, out_specs=out_specs, check_vma=False)
```

```python
import math

import jax
import jax.numpy as jnp
import numpy as np
from jax import lax
from jax.experimental import pallas as pl
from jax.experimental.pallas import tpu as pltpu
from jax.sharding import PartitionSpec as P

HEADS = 12
HEAD_DIM = 64
LONGEST = 1344
SEQ = 4
LOCAL = 3
TOK = 384
HALF = 192
PACK = 1536
F32 = jnp.float32
BF16 = jnp.bfloat16
VMEM_LIMIT = 63 * 1024 * 1024


def mm(left, right):
    return jnp.dot(left, right, preferred_element_type=F32)


def mm_nt(left, right):
    return lax.dot_general(left, right, (((1,), (1,)), ((), ())), preferred_element_type=F32)


def mm_tn(left, right):
    return lax.dot_general(left, right, (((0,), (0,)), ((), ())), preferred_element_type=F32)


def iota(shape, dim):
    return lax.broadcasted_iota(jnp.int32, shape, dim)


def roll(x, shift):
    return pltpu.roll(x, shift, 1)


def low_lanes(rows):
    return iota((rows, 128), 1) < 64


def turned(x):
    lane = iota(x.shape, 1)
    first = (lane & 32) == 0
    return jnp.where(first, roll(x, 96), roll(x, 32))


def norm_parts(values):
    average = jnp.mean(values, axis=-1, keepdims=True)
    centred = values - average
    variance = jnp.mean(centred * centred, axis=-1, keepdims=True)
    scale = lax.rsqrt(variance + 1e-05)
    return centred * scale, scale


def doc_bounds(len_ref):
    first = len_ref[0]
    second = first + len_ref[1]
    third = second + len_ref[2]
    start = jnp.where(
        len_ref[0] == LONGEST,
        0,
        jnp.where(len_ref[1] == LONGEST, first, jnp.where(len_ref[2] == LONGEST, second, third)),
    )
    return first, second, third, start


def edge_order(start, transposed):
    stored = iota((2 * HALF, 2 * HALF), 1 if transposed else 0)
    edge = iota((2 * HALF, 2 * HALF), 0 if transposed else 1)
    source = stored + (HALF + start)
    source = jnp.where(source >= 2 * HALF, source - 2 * HALF, source)
    return jnp.where(edge == source, 1.0, 0.0).astype(BF16)


def short_mask(bounds):
    first, second, third, start = bounds

    def numbers(dim):
        row = iota((HALF, HALF), dim) + (HALF + start)
        row = jnp.where(row >= 2 * HALF, row - 2 * HALF, row)
        place = jnp.where(row >= HALF, row + (PACK - 2 * HALF), row)
        return (
            jnp.where(place >= first, 1, 0)
            + jnp.where(place >= second, 1, 0)
            + jnp.where(place >= third, 1, 0)
        )

    return numbers(0) == numbers(1)


def extra_lanes(base, column):
    lane = iota(base.shape, 1)
    rest = -column
    top = rest.astype(BF16).astype(F32)
    rest = rest - top
    middle = rest.astype(BF16).astype(F32)
    rest = rest - middle
    return jnp.where(
        lane < 64,
        base,
        jnp.where(lane == 64, top, jnp.where(lane == 65, middle, jnp.where(lane == 66, rest, 0.0))),
    )


def permute_edge(order, ref, head):
    edge = jnp.concatenate([ref[head, 0:HALF, :], ref[head, PACK - HALF : PACK, :]], axis=0)
    moved = mm(order, edge).astype(BF16)
    return moved[0:HALF], moved[HALF : 2 * HALF]


def pack_halves(top, bottom):
    return jnp.where(low_lanes(top.shape[0]), top, roll(bottom, 64))


def rope_rows(len_ref, inv_ref, block, cos_ref, sin_ref):
    rows = pl.ds(pl.multiple_of(block * TOK, TOK), TOK)
    place = iota((TOK, 128), 0) + block * TOK
    first = len_ref[0]
    second = first + len_ref[1]
    third = second + len_ref[2]
    starts = (
        jnp.where(iota((8, 128), 0) == 1, first, 0)
        + jnp.where(iota((8, 128), 0) == 2, second, 0)
        + jnp.where(iota((8, 128), 0) == 3, third, 0)
    )
    shift = starts.astype(F32) * inv_ref[...]
    shift_cos, shift_sin = jnp.cos(shift), jnp.sin(shift)

    def pick(table):
        return jnp.where(
            place >= third,
            table[3:4],
            jnp.where(place >= second, table[2:3], jnp.where(place >= first, table[1:2], table[0:1])),
        )

    back_cos, back_sin = pick(shift_cos), pick(shift_sin)
    cosine, sine = cos_ref[rows, :], sin_ref[rows, :]
    cos_ref[rows, :] = cosine * back_cos + sine * back_sin
    sine = sine * back_cos - cosine * back_sin
    sin_ref[rows, :] = jnp.where((iota((TOK, 128), 1) & 32) == 0, -sine, sine)


def project_block(block, hid_ref, w_ref, cos_ref, sin_ref, q_ref, k_ref, v_ref, xt_ref):
    rows = pl.ds(pl.multiple_of(block * TOK, TOK), TOK)
    xhat = norm_parts(hid_ref[block].astype(F32))[0].astype(BF16)
    xt_ref[block] = jnp.transpose(xhat)
    qkv = mm(xhat, w_ref[...])
    cosine, sine = cos_ref[rows, :], sin_ref[rows, :]
    lane = iota((TOK, 128), 1)
    low = lane < 64
    ones = jnp.where(lane < 67, 1.0, 0.0)
    for chunk in range(5):
        part = qkv[:, 128 * chunk : min(128 * chunk + 128, 576)]
        if chunk == 4:
            part = jnp.concatenate([part, part], axis=1)
        if chunk < 3:
            part = part * cosine + turned(part) * sine
        for odd in range(2):
            index = 2 * chunk + odd
            if index == 9:
                continue
            piece = roll(part, 64) if odd else part
            kind, head = index // 3, index % 3
            if kind == 0:
                q_ref[head, rows, :] = (jnp.where(low, piece, 0.0).astype(BF16).astype(F32) * 0.125).astype(BF16)
            elif kind == 1:
                k_ref[head, rows, :] = jnp.where(low, piece, ones).astype(BF16)
            else:
                v_ref[head, rows, :] = jnp.where(low, piece, ones).astype(BF16)


def attend_rows(head, rows, keys, mask, q_ref, k_ref, v_ref, o_ref):
    query = q_ref[head, rows, :]
    scores = mm_nt(query, k_ref[head, keys, :])
    if mask is not None:
        scores = jnp.where(mask, scores, -1e9)
    highest = jnp.max(scores, axis=1, keepdims=True)
    weights = jnp.exp(scores - highest).astype(BF16)
    mixed = mm(weights, v_ref[head, keys, :])
    total = mixed[:, 64:65]
    lane = iota(mixed.shape, 1)
    o_ref[head, rows, :] = jnp.where(lane < 64, mixed * (1.0 / total), 0.0).astype(BF16)
    q_ref[head, rows, :] = extra_lanes(query.astype(F32), highest + jnp.log(total)).astype(BF16)


def places():
    seq, fsdp = lax.axis_index("seq"), lax.axis_index("fsdp")
    return seq, fsdp, fsdp // 8, (fsdp // 2) % 4, fsdp % 2


def peer(axis, step):
    seq, fsdp, z, y, core = places()
    if axis == "x":
        return ((seq + step) % SEQ, fsdp)
    if axis == "y":
        return (seq, z * 8 + ((y + step) % 4) * 2 + core)
    if axis == "z":
        return (seq, ((z + step) % 4) * 8 + y * 2 + core)
    return (seq, fsdp + 1 - 2 * core)


def remote(source, target, send_sem, recv_sem, device):
    return pltpu.make_async_remote_copy(
        src_ref=source,
        dst_ref=target,
        send_sem=send_sem,
        recv_sem=recv_sem,
        device_id=device,
        device_id_type=pl.DeviceIdType.MESH,
    )


ALL_PEERS = [(axis, step) for axis in "xyz" for step in (1, 2, 3)] + [("c", 1)]


def greet():
    barrier = pltpu.get_barrier_semaphore()
    for axis, step in ALL_PEERS:
        pl.semaphore_signal(barrier, inc=1, device_id=peer(axis, step), device_id_type=pl.DeviceIdType.MESH)
    pl.semaphore_wait(barrier, len(ALL_PEERS))


class Gather:
    def __init__(self, shard, full, send, recv, index, first):
        _, _, z, y, core = places()
        self.send, self.recv, self.index = send, recv, index
        mine = full.at[z, y, core]
        if first == "y":
            second, at = "z", z

            def line(k, half):
                return full.at[k % 4, half, core]

        else:
            second, at = "y", y

            def line(k, half):
                return full.at[half, k % 4, core]

        whole, low, high = pl.ds(0, 4), pl.ds(0, 2), pl.ds(2, 2)

        def both(block, axis, step):
            return (block, block, axis, step)

        self.hops = (
            [(shard, mine, first, step) for step in (1, 2, 3)],
            [both(line(at, whole), second, step) for step in (1, 3)] + [both(line(at, whole), "c", 1)],
            [
                both(line(at + 3, low), second, 1),
                both(line(at + 1, high), second, 3),
                both(line(at + 3, whole), "c", 1),
                both(line(at + 1, whole), "c", 1),
            ],
            [both(line(at + 2, whole), "c", 1)],
        )
        self.local = pltpu.make_async_copy(shard, mine, send.at[index, 11])

    def copies(self, hop):
        base = (0, 3, 6, 10)[hop]
        return [
            remote(src, dst, self.send.at[self.index, base + n], self.recv.at[self.index, base + n], peer(axis, step))
            for n, (src, dst, axis, step) in enumerate(self.hops[hop])
        ]

    def start(self, hop):
        if hop == 0:
            self.local.start()
        for copy in self.copies(hop):
            copy.start()

    def arrive(self, hop):
        if hop == 0:
            self.local.wait()
        for copy in self.copies(hop):
            copy.wait_recv()

    def advance(self, hop):
        self.arrive(hop)
        self.start(hop + 1)

    def finish(self):
        for hop in range(4):
            for copy in self.copies(hop):
                copy.wait_send()


def backward_rows(head, rows, queries, mask, q_ref, k_ref, v_ref, d_ref, dk_ref, dv_ref):
    query, grad = q_ref[head, queries, :], d_ref[head, queries, :]
    key = k_ref[head, rows, :]
    shares = jnp.exp(mm_nt(key, query))
    if mask is not None:
        shares = jnp.where(mask, shares, 0.0)
    grad_scores = (shares * mm_nt(v_ref[head, rows, :], grad)).astype(BF16)
    dv_ref[head, rows, :] = mm(shares.astype(BF16), grad).astype(BF16)
    dk_ref[head, rows, :] = mm(grad_scores, query).astype(BF16)
    return mm_tn(grad_scores, key)


class Reduce:
    def __init__(self, part, bufs, send, recv, index, first):
        _, _, self.z, self.y, self.core = places()
        self.part = part
        self.acc, self.recv1, self.acc1, self.recv2 = bufs
        self.send, self.recv, self.index, self.first = send, recv, index, first
        second = "z" if first == "y" else "y"
        self.hops = [[(part.at[:, :, 1 - self.core], self.acc, "c", 1)], [], []]
        for step in (1, 2, 3):
            one = (self.y + step) % 4
            two = (self.z + step) % 4
            if first == "y":
                lines, rest = self.acc.at[:, one], two
            else:
                lines, rest = self.acc.at[two], one
            self.hops[1].append((lines, self.recv1.at[step - 1], first, step))
            self.hops[2].append((self.acc1.at[rest], self.recv2.at[step - 1], second, step))

    def copies(self, hop):
        base = (0, 1, 4)[hop]
        return [
            remote(src, dst, self.send.at[self.index, base + n], self.recv.at[self.index, base + n], peer(axis, step))
            for n, (src, dst, axis, step) in enumerate(self.hops[hop])
        ]

    def start(self, hop):
        for copy in self.copies(hop):
            copy.start()

    def arrive(self, hop):
        for copy in self.copies(hop):
            copy.wait_recv()
        if hop == 0:

            @pl.loop(0, 16)
            def _(index):
                z, y = index // 4, index % 4
                total = self.acc[z, y].astype(F32) + self.part[z, y, self.core].astype(F32)
                self.acc[z, y] = total.astype(BF16)

        elif hop == 1:

            @pl.loop(0, 4)
            def _(index):
                own = self.acc[index, self.y] if self.first == "y" else self.acc[self.z, index]
                total = own.astype(F32)
                for step in range(3):
                    total += self.recv1[step, index].astype(F32)
                self.acc1[index] = total.astype(BF16)

        else:
            total = self.acc1[self.z if self.first == "y" else self.y].astype(F32)
            for step in range(3):
                total += self.recv2[step].astype(F32)
            return total

    def advance(self, hop):
        self.arrive(hop)
        self.start(hop + 1)

    def finish(self, first=0):
        for hop in range(first, 3):
            self.sent(hop)

    def sent(self, hop):
        for copy in self.copies(hop):
            copy.wait_send()


def reduce_scratch(rows, width):
    return [
        pltpu.VMEM((4, 4, rows, width), BF16),
        pltpu.VMEM((3, 4, rows, width), BF16),
        pltpu.VMEM((4, rows, width), BF16),
        pltpu.VMEM((3, rows, width), BF16),
    ]


class Cross:
    def __init__(self, sources, targets, send, recv, index):
        self.list = [
            remote(src, dst, send.at[index, n], recv.at[index, n], peer("x", n + 1))
            for n, (src, dst) in enumerate(zip(sources, targets))
        ]

    def start(self):
        for copy in self.list:
            copy.start()

    def arrive(self):
        for copy in self.list:
            copy.wait_recv()

    def finish(self):
        for copy in self.list:
            copy.wait_send()


def column_block(value, start, width):
    total = value.shape[1]
    if start:
        value = roll(value, total - start)
    return value[:, :width]


def own_columns(value, rank):
    total = value.shape[1]
    lane = iota((value.shape[0], 640), 1)
    result = jnp.zeros((value.shape[0], 640), F32)
    for kind in range(3):
        shift = (total - 768 * kind - HALF * rank + HALF * kind) % total
        moved = roll(value, shift) if shift else value
        result = jnp.where((lane >= HALF * kind) & (lane < HALF * kind + HALF), moved[:, :640], result)
    return result[:, :576]


def to_column(row):
    count = row.shape[1]
    diagonal = iota((count, count), 0) == iota((count, count), 1)
    return jnp.sum(jnp.where(diagonal, jnp.broadcast_to(row, (count, count)), 0.0), axis=1, keepdims=True)


def to_row(column):
    count = column.shape[0]
    diagonal = iota((count, count), 0) == iota((count, count), 1)
    return jnp.sum(jnp.where(diagonal, jnp.broadcast_to(column, (count, count)), 0.0), axis=0, keepdims=True)


def lay_pairs(full, target):
    for pair in range(16):
        z, y = pair // 4, pair % 4
        rows = jnp.concatenate([full[z, y, 0].astype(F32), full[z, y, 1].astype(F32)], axis=0)
        target[48 * pair : 48 * pair + 48, :] = rows.astype(BF16)


def layer_kernel(
    len_ref, inv_ref, cos_in, sin_in, hid_in, cot_ref, gain1_ref, gain2_ref, wq_ref, wi_ref, out_ref, down_ref,
    res_ref, in_ref, gq_out, go_out, gi_out, gd_out, gain1_out, gain2_out, one_full,
    oraw_ref, own_ref, two_ref, one_ref, cos_ref, sin_ref, hid_ref, own_full, w_ref, xt_ref,
    q_ref, k_ref, v_ref, o_ref, stage_ref, mix_ref,
    two_full, out_full, down_full, wi_full, wo_full, wd_full,
    attn_ref, x_ref, act_ref, gp_ref, wide_ref,
    g_ref, d_ref, dq_ref, dk_ref, dv_ref, acc_ref, gstage_ref, got_ref, m_ref,
    xi_ref, xo_ref, xd_ref, xg_ref, xm_ref, ri_ref, ro_ref, rd_ref, rg_ref, rm_ref,
    gather_send, gather_recv, hid_send, hid_recv, mix_send, mix_recv, local_sem,
    red_send, red_recv, x_send, x_recv,
    *bufs,
):
    seq, fsdp, _, _, _ = places()
    bounds = doc_bounds(len_ref)
    right, left = (seq + 1) % SEQ, (seq + 3) % SEQ
    ff = wi_ref.shape[1] // 2
    low = low_lanes(HALF)
    tables = (
        pltpu.make_async_copy(cos_in, cos_ref, local_sem.at[0]),
        pltpu.make_async_copy(sin_in, sin_ref, local_sem.at[1]),
    )
    for copy in tables:
        copy.start()
    gain1 = to_column(gain1_ref[...].astype(F32))
    gain2 = to_column(gain2_ref[...].astype(F32))
    raw = wq_ref[...].astype(F32)
    for rank in range(SEQ):

        @pl.when(seq == rank)
        def _(rank=rank):
            oraw_ref[...] = own_columns(raw, rank)

    own_ref[...] = (oraw_ref[...] * gain1).astype(BF16)
    one_ref[...] = (raw * gain1).astype(BF16)
    two_ref[...] = (wi_ref[...].astype(F32) * gain2).astype(BF16)
    greet()
    own = Gather(own_ref, own_full, gather_send, gather_recv, 0, "y")
    two = Gather(two_ref, two_full, gather_send, gather_recv, 1, "y")
    out = Gather(out_ref, out_full, gather_send, gather_recv, 2, "y")
    down = Gather(down_ref, down_full, gather_send, gather_recv, 3, "z")
    one = Gather(one_ref, one_full, gather_send, gather_recv, 4, "z")
    weights = (out, two, down, one)
    own.start(0)
    to_right = remote(hid_in, hid_ref.at[seq], hid_send.at[0], hid_recv.at[0], peer("x", 1))
    to_left = remote(hid_in, hid_ref.at[seq], hid_send.at[1], hid_recv.at[1], peer("x", 3))
    to_right.start()
    to_left.start()
    hid_ref[seq] = hid_in[...]
    for weight in weights:
        weight.start(0)
    for copy in tables:
        copy.wait()
    own.advance(0)
    for block in range(SEQ):
        rope_rows(len_ref, inv_ref, block, cos_ref, sin_ref)
    own.advance(1)
    for weight in weights:
        weight.advance(0)
    own.advance(2)
    own.arrive(3)
    lay_pairs(own_full, w_ref)

    def project(block):
        project_block(block, hid_ref, w_ref, cos_ref, sin_ref, q_ref, k_ref, v_ref, xt_ref)

    project(seq)
    to_right.wait_recv()
    on_right = remote(
        hid_ref.at[left, pl.ds(0, HALF)], hid_ref.at[left, pl.ds(0, HALF)],
        hid_send.at[2], hid_recv.at[2], peer("x", 1),
    )
    on_right.start()
    to_left.wait_recv()
    on_left = remote(
        hid_ref.at[right, pl.ds(HALF, HALF)], hid_ref.at[right, pl.ds(HALF, HALF)],
        hid_send.at[3], hid_recv.at[3], peer("x", 3),
    )
    on_left.start()
    project(left)
    project(right)
    on_right.wait_recv()
    on_left.wait_recv()
    project((seq + 2) % SEQ)

    order = edge_order(bounds[3], False)
    back = edge_order(bounds[3], True)
    for ref in (q_ref, k_ref, v_ref):
        for head in range(LOCAL):
            short, long = permute_edge(order, ref, head)
            ref[head, 0:HALF, :] = short
            ref[head, PACK - HALF : PACK, :] = long

    def attend(block):
        rows = pl.ds(pl.multiple_of(block * HALF, HALF), HALF)
        for head in range(LOCAL):
            attend_rows(head, rows, pl.ds(HALF, PACK - HALF), None, q_ref, k_ref, v_ref, o_ref)

    def mix_copy(dest):
        return remote(stage_ref.at[dest], mix_ref.at[seq], mix_send.at[dest], mix_recv.at[seq], (dest, fsdp))

    def give(dest, head, top, bottom):
        stage_ref[dest, head] = pack_halves(top.astype(F32), bottom.astype(F32)).astype(BF16)

    def hand_over(dest):
        @pl.when(seq != dest)
        def _():
            mix_copy(dest).start()

    def inner_dest(dest):
        pl.loop(2 * dest, 2 * dest + 2)(attend)
        for head in range(LOCAL):
            first = TOK * dest
            give(dest, head, o_ref[head, first : first + HALF, :], o_ref[head, first + HALF : first + TOK, :])
        hand_over(dest)

    inner_dest(1)
    out.advance(1)
    inner_dest(2)
    out.advance(2)
    two.advance(1)
    down.advance(1)
    mask = short_mask(bounds)
    for head in range(LOCAL):
        attend_rows(head, pl.ds(0, HALF), pl.ds(0, HALF), mask, q_ref, k_ref, v_ref, o_ref)

    @pl.loop(0, 3)
    def _(index):
        attend(1 + 5 * jnp.minimum(index, 1) + jnp.maximum(index - 1, 0))

    for head in range(LOCAL):
        top, bottom = permute_edge(back, o_ref, head)
        give(0, head, top, o_ref[head, HALF:TOK, :])
        give(3, head, o_ref[head, 3 * TOK : 3 * TOK + HALF, :], bottom)
    hand_over(0)
    hand_over(3)
    mix_ref[seq] = stage_ref[seq]
    one.advance(1)
    two.advance(2)
    down.advance(2)
    out.arrive(3)
    lay_pairs(out_full, wo_full)
    for step in (1, 2, 3):
        source = (seq + step) % SEQ
        remote(stage_ref.at[0], mix_ref.at[source], mix_send.at[0], mix_recv.at[source], peer("x", step)).wait_recv()
    for dest in range(SEQ):
        @pl.when(seq != dest)
        def _(dest=dest):
            mix_copy(dest).wait_send()

    for chunk in range(6):
        pair = []
        for index in (2 * chunk, 2 * chunk + 1):
            pair.append(mix_ref[index // 3, index % 3].astype(F32))
        first, second = pair
        lanes = slice(128 * chunk, 128 * chunk + 128)
        attn_ref[0:HALF, lanes] = pack_halves(first, second).astype(BF16)
        attn_ref[HALF:TOK, lanes] = jnp.where(low, roll(first, 64), second).astype(BF16)
    residual = hid_in[...].astype(F32) + mm(attn_ref[...], wo_full[...])
    xhat, scale = norm_parts(residual)
    x_ref[...] = xhat.astype(BF16)
    two.arrive(3)
    lay_pairs(two_full, wi_full)
    down.arrive(3)
    part = down_full.shape[3]
    for group in range(8):
        shards = [down_full[k // 8, k // 2 % 4, k % 2].astype(F32) for k in range(4 * group, 4 * group + 4)]
        wd_full[4 * part * group : 4 * part * (group + 1), :] = jnp.concatenate(shards, axis=0).astype(BF16)
    one.advance(2)
    step = 384
    output = residual
    branch = cot_ref[...]
    for chunk in range(ff // step):
        lanes = slice(step * chunk, step * chunk + step)
        upper = slice(ff + step * chunk, ff + step * chunk + step)
        inner = mm(x_ref[...], wi_full[:, lanes])
        gate = mm(x_ref[...], wi_full[:, upper])
        phi = 0.5 * (1.0 + lax.erf(inner * math.sqrt(0.5)))
        gelu = inner * phi
        act = (gelu * gate).astype(BF16)
        act_ref[:, lanes] = act
        output = output + mm(act, wd_full[lanes, :])
        grad_act = mm_nt(branch, wd_full[lanes, :])
        density = jnp.exp(inner * inner * -0.5) * (1.0 / math.sqrt(2.0 * math.pi))
        gp_ref[:, lanes] = (grad_act * gate * (phi + inner * density)).astype(BF16)
        gp_ref[:, upper] = (grad_act * gelu).astype(BF16)
    res_ref[...] = output.astype(BF16)
    grad = mm_nt(gp_ref[...], wi_full[...])
    grad = scale * (
        grad
        - jnp.mean(grad, axis=-1, keepdims=True)
        - xhat * jnp.mean(grad * xhat, axis=-1, keepdims=True)
    )
    grad_res = branch.astype(F32) + grad
    in_ref[...] = grad_res
    grad_attn = grad_res.astype(BF16)
    grad_mix = mm_nt(grad_attn, wo_full[...]).astype(BF16).astype(F32)
    for chunk in range(6):
        lanes = slice(128 * chunk, 128 * chunk + 128)
        top, bottom = grad_mix[0:HALF, lanes], grad_mix[HALF:TOK, lanes]
        first = pack_halves(top, bottom)
        second = jnp.where(low, roll(top, 64), bottom)
        stage_ref[2 * chunk // 3, 2 * chunk % 3] = first.astype(BF16)
        stage_ref[(2 * chunk + 1) // 3, (2 * chunk + 1) % 3] = second.astype(BF16)

    def by_rank(ref):
        return [ref.at[(seq + step) % SEQ] for step in (1, 2, 3)]

    def by_step(ref):
        return [ref.at[step] for step in range(3)]

    gmix = Cross(by_rank(stage_ref), [g_ref.at[seq]] * 3, x_send, x_recv, 0)
    gmix.start()
    g_ref[seq] = stage_ref[seq]

    for weight in (own, out, two, down):
        weight.finish()
    red_in = Reduce(two_full, bufs[0:4], red_send, red_recv, 0, "y")
    red_out = Reduce(out_full, bufs[4:8], red_send, red_recv, 1, "z")
    red_down = Reduce(down_full, bufs[8:12], red_send, red_recv, 2, "z")
    red_own = Reduce(m_ref, bufs[12:16], red_send, red_recv, 3, "y")
    early = (red_down, red_in, red_out)

    def lay(ref, lanes, value):
        for owner in range(32):
            ref[owner // 8, owner // 2 % 4, owner % 2, :, lanes] = value[24 * owner : 24 * owner + 24].astype(BF16)

    for column in range(2):
        lanes = slice(step * column, step * column + step)
        for chunk in range(ff // step):
            rows = slice(step * chunk, step * chunk + step)
            wide_ref[rows, :] = mm_tn(act_ref[:, rows], branch[:, lanes])
        for owner in range(32):
            down_full[owner // 8, owner // 2 % 4, owner % 2, :, lanes] = wide_ref[
                part * owner : part * owner + part, :
            ].astype(BF16)
    red_down.start(0)
    for chunk in range(2 * ff // step):
        lanes = slice(step * chunk, step * chunk + step)
        lay(two_full, lanes, mm_tn(x_ref[...], gp_ref[:, lanes]))
    red_in.start(0)
    for chunk in range(768 // step):
        lanes = slice(step * chunk, step * chunk + step)
        lay(out_full, lanes, mm_tn(attn_ref[...], grad_attn[:, lanes]))
    red_out.start(0)
    for copy in (to_right, to_left, on_right, on_left):
        copy.wait_send()

    gmix.arrive()
    for head in range(LOCAL):
        for source in range(SEQ):
            packed = g_ref[source, head].astype(F32)
            d_ref[head, TOK * source : TOK * source + HALF, :] = jnp.where(low, packed, 0.0).astype(BF16)
            d_ref[head, TOK * source + HALF : TOK * source + TOK, :] = jnp.where(
                low, roll(packed, 64), 0.0
            ).astype(BF16)
        short, long = permute_edge(order, d_ref, head)
        d_ref[head, 0:HALF, :] = short
        d_ref[head, PACK - HALF : PACK, :] = long

    @pl.loop(0, PACK // HALF)
    def _(block):
        rows = pl.ds(pl.multiple_of(block * HALF, HALF), HALF)
        for head in range(LOCAL):
            grad = d_ref[head, rows, :].astype(F32)
            inner = jnp.sum(grad * o_ref[head, rows, :].astype(F32), axis=1, keepdims=True)
            d_ref[head, rows, :] = extra_lanes(grad, inner).astype(BF16)

    mask = short_mask(bounds)
    step_rows = 224

    def attend_back(head):
        acc_ref[0:HALF, :] = backward_rows(
            head, pl.ds(0, HALF), pl.ds(0, HALF), mask, q_ref, k_ref, v_ref, d_ref, dk_ref, dv_ref
        )
        acc_ref[HALF:PACK, :] = jnp.zeros((LONGEST, 128), F32)

        @pl.loop(0, LONGEST // (2 * step_rows))
        def _(block):
            terms = []
            for part in range(2):
                start = HALF + block * (2 * step_rows) + part * step_rows
                rows = pl.ds(pl.multiple_of(start, 32), step_rows)
                terms.append(
                    backward_rows(
                        head, rows, pl.ds(HALF, LONGEST), None, q_ref, k_ref, v_ref, d_ref, dk_ref, dv_ref
                    )
                )
            acc_ref[HALF:PACK, :] += terms[0] + terms[1]

        dq_ref[head] = (acc_ref[...] * 0.125).astype(BF16)
        for ref in (dq_ref, dk_ref, dv_ref):
            top, bottom = permute_edge(back, ref, head)
            ref[head, 0:HALF, :] = top
            ref[head, PACK - HALF : PACK, :] = bottom

        @pl.loop(0, SEQ)
        def _(dest):
            top = pl.ds(pl.multiple_of(dest * TOK, TOK), HALF)
            bottom = pl.ds(pl.multiple_of(dest * TOK + HALF, HALF), HALF)
            cosine = pack_halves(cos_ref[top, :], cos_ref[bottom, :])
            sine = pack_halves(sin_ref[top, :], sin_ref[bottom, :])
            for kind, ref in enumerate((dq_ref, dk_ref, dv_ref)):
                packed = pack_halves(ref[head, top, :].astype(F32), ref[head, bottom, :].astype(F32))
                if kind < 2:
                    packed = packed * cosine - turned(packed) * sine
                gstage_ref[dest, head, kind] = packed.astype(BF16)

        got_ref[seq, head] = gstage_ref[seq, head]
        sources = [gstage_ref.at[(seq + step) % SEQ, head] for step in (1, 2, 3)]
        cross = Cross(sources, [got_ref.at[seq, head]] * 3, x_send, x_recv, 1 + head)
        cross.start()
        return cross

    for red in early:
        red.advance(0)
    one.arrive(3)
    one.finish()
    red_in.sent(0)
    one_copy = pltpu.make_async_copy(one_full, two_full, local_sem.at[2])
    one_copy.start()
    crosses = [attend_back(0)]
    crosses.append(attend_back(1))
    for red in early:
        red.advance(1)
    crosses.append(attend_back(2))
    for dest in range(SEQ):
        for chunk in range(5):
            lanes = slice(128 * chunk, 128 * chunk + 128)
            index = 2 * chunk
            first = gstage_ref[dest, index % 3, index // 3].astype(F32)
            index = min(index + 1, 8)
            second = gstage_ref[dest, index % 3, index // 3].astype(F32)
            hid_ref[dest, 0:HALF, lanes] = pack_halves(first, second).astype(BF16)
            hid_ref[dest, HALF:TOK, lanes] = jnp.where(low, roll(first, 64), second).astype(BF16)
    total = mm(xt_ref[0], hid_ref[0, :, 0:640])
    for block in range(1, SEQ):
        total += mm(xt_ref[block], hid_ref[block, :, 0:640])
    for owner in range(32):
        m_ref[owner // 8, owner // 2 % 4, owner % 2] = total[24 * owner : 24 * owner + 24, :576].astype(BF16)
    red_own.start(0)

    rows_in = red_in.arrive(2)
    rows_out = red_out.arrive(2)
    rows_down = red_down.arrive(2)

    def share(value, ref, width):
        for dest in range(SEQ):
            ref[dest] = column_block(value, width * dest, width).astype(BF16)

    share(rows_in, xi_ref, ff // 2)
    share(rows_out, xo_ref, HALF)
    share(rows_down, xd_ref, HALF)
    gain = jnp.sum(rows_in * wi_ref[...].astype(F32), axis=1, keepdims=True)
    xg_ref[0] = jnp.broadcast_to(gain, (24, 128))
    late = [
        Cross(by_rank(xi_ref), by_step(ri_ref), x_send, x_recv, 4),
        Cross(by_rank(xo_ref), by_step(ro_ref), x_send, x_recv, 5),
        Cross(by_rank(xd_ref), by_step(rd_ref), x_send, x_recv, 6),
        Cross([xg_ref.at[0]] * 3, by_step(rg_ref.at[0]), x_send, x_recv, 7),
    ]
    for cross in late:
        cross.start()

    one_copy.wait()
    lay_pairs(two_full, wi_full)
    red_own.advance(0)

    for cross in late:
        cross.arrive()

    def collect(own, ref):
        return own.astype(F32) + ref[0].astype(F32) + ref[1].astype(F32) + ref[2].astype(F32)

    gi_out[...] = collect(xi_ref[seq], ri_ref) * gain2
    go_out[...] = collect(xo_ref[seq], ro_ref)
    gd_out[...] = collect(xd_ref[seq], rd_ref)
    gain2_out[...] = to_row(collect(xg_ref[0], rg_ref.at[0])[:, 0:1])

    for cross in crosses:
        cross.arrive()
    red_own.advance(1)
    for chunk in range(18):
        pair = []
        for index in (2 * chunk, 2 * chunk + 1):
            kind, head = index // HEADS, index % HEADS
            pair.append(got_ref[head // 3, head % 3, kind].astype(F32))
        first, second = pair
        lanes = slice(128 * chunk, 128 * chunk + 128)
        gp_ref[0:HALF, lanes] = pack_halves(first, second).astype(BF16)
        gp_ref[HALF:TOK, lanes] = jnp.where(low, roll(first, 64), second).astype(BF16)
    rows_own = red_own.arrive(2)
    gain = jnp.sum(rows_own * oraw_ref[...], axis=1, keepdims=True)
    xg_ref[1] = jnp.broadcast_to(gain, (24, 128))
    wide = jnp.concatenate([rows_own, jnp.zeros((24, 64), F32)], axis=1)
    for kind in range(3):
        moved = column_block(wide, HALF * kind, 256)
        xm_ref[kind] = jnp.where(iota((24, 256), 1) < HALF, moved, 0.0).astype(BF16)
    rm_ref[seq] = xm_ref[...]
    last = [
        Cross([xm_ref] * 3, [rm_ref.at[seq]] * 3, x_send, x_recv, 8),
        Cross([xg_ref.at[1]] * 3, by_step(rg_ref.at[1]), x_send, x_recv, 9),
    ]
    for cross in last:
        cross.start()
    grad = mm_nt(gp_ref[...], wi_full[...])
    xhat, scale = norm_parts(hid_in[...].astype(F32))
    grad = scale * (
        grad
        - jnp.mean(grad, axis=-1, keepdims=True)
        - xhat * jnp.mean(grad * xhat, axis=-1, keepdims=True)
    )
    in_ref[...] += grad
    for cross in last:
        cross.arrive()
    spread = jnp.zeros((24, 640), F32)
    for place in range(3):
        index = 3 * seq + place
        piece = rm_ref[index % 4, index // 4].astype(F32) * gain1
        piece = jnp.concatenate([piece, jnp.zeros((24, 384), F32)], axis=1)
        spread += roll(piece, HALF * place) if place else piece
    gq_out[...] = spread[:, :576]
    gain1_out[...] = to_row(collect(xg_ref[1], rg_ref.at[1])[:, 0:1])
    red_in.finish(1)
    for item in (red_down, red_out, red_own, gmix, *crosses, *late, *last):
        item.finish()


SMEM = pl.BlockSpec(memory_space=pltpu.SMEM)
VMEM = pl.BlockSpec(memory_space=pltpu.VMEM)
ANY = pl.BlockSpec(memory_space=pl.ANY)


def shape(*dims, dtype=BF16):
    return jax.ShapeDtypeStruct(dims, dtype)


def body(hidden, lengths, attn_gain, w_qkv, w_attn_out, mlp_gain, w_in, w_mlp_out, cotangent):
    inverse = 160000.0 ** (np.arange(128) % 32 * (-2.0 / HEAD_DIM))
    angles = np.arange(PACK)[:, None] * inverse[None, :]
    cosine, sine = np.cos(angles).astype(np.float32), np.sin(angles).astype(np.float32)
    inverse = np.broadcast_to(inverse, (8, 128)).astype(np.float32)
    part = w_mlp_out.shape[0]
    ff = part * 32

    def low(*dims):
        return pltpu.VMEM(dims, BF16)

    def wide(*dims):
        return pltpu.VMEM(dims, F32)

    def dma(*dims):
        return pltpu.SemaphoreType.DMA(dims)

    heads = low(LOCAL, PACK, 128)
    packed = low(SEQ, LOCAL, HALF, 128)
    grads = low(SEQ, LOCAL, 3, HALF, 128)
    output, input_grad, grad_qkv, grad_out, grad_in, grad_down, gain_one, gain_two, _ = pl.pallas_call(
        layer_kernel,
        out_shape=(
            shape(TOK, 768),
            shape(TOK, 768, dtype=F32),
            shape(24, 576, dtype=F32),
            shape(24, HALF, dtype=F32),
            shape(24, ff // 2, dtype=F32),
            shape(part, HALF, dtype=F32),
            shape(1, 24, dtype=F32),
            shape(1, 24, dtype=F32),
            shape(4, 4, 2, 24, 2304),
        ),
        in_specs=[SMEM, VMEM, ANY, ANY] + [VMEM] * 6 + [ANY] * 2,
        out_specs=(VMEM,) * 8 + (ANY,),
        scratch_shapes=[
            wide(24, 576), low(24, 576), low(24, 2 * ff), low(24, 2304),
            wide(PACK, 128), wide(PACK, 128),
            low(SEQ, TOK, 768), low(4, 4, 2, 24, 576), low(768, 576), low(SEQ, 768, TOK),
            heads, heads, heads, heads, packed, packed,
            low(4, 4, 2, 24, 2 * ff), low(4, 4, 2, 24, 768), low(4, 4, 2, part, 768),
            low(768, 2 * ff), low(768, 768), low(ff, 768),
            low(TOK, 768), low(TOK, 768), low(TOK, ff), low(TOK, 2 * ff), wide(ff, 384),
            packed, heads, heads, heads, heads, wide(PACK, 128), grads, grads, low(4, 4, 2, 24, 576),
            low(SEQ, 24, ff // 2), low(SEQ, 24, HALF), low(SEQ, part, HALF), wide(2, 24, 128), low(3, 24, 256),
            low(3, 24, ff // 2), low(3, 24, HALF), low(3, part, HALF), wide(2, 3, 24, 128), low(SEQ, 3, 24, 256),
            dma(5, 12), dma(5, 11), dma(4), dma(4), dma(4), dma(4), dma(3),
            dma(4, 7), dma(4, 7), dma(10, 3), dma(10, 3),
            *reduce_scratch(24, 2 * ff),
            *reduce_scratch(24, 768),
            *reduce_scratch(part, 768),
            *reduce_scratch(24, 576),
        ],
        compiler_params=pltpu.CompilerParams(
            vmem_limit_bytes=VMEM_LIMIT, collective_id=1, has_side_effects=True
        ),
        name="layer",
    )(
        lengths[0], inverse, cosine, sine, hidden[0], cotangent[0],
        attn_gain[None], mlp_gain[None], w_qkv, w_in, w_attn_out, w_mlp_out,
    )
    return (
        output[None],
        input_grad[None],
        gain_one[0],
        grad_qkv,
        grad_out,
        gain_two[0],
        grad_in,
        grad_down,
    )


def solution(mesh):
    in_specs = (
        P("fsdp", "seq", None),
        P("fsdp", None),
        P("fsdp"),
        P("fsdp", None),
        P("fsdp", None),
        P("fsdp"),
        P("fsdp", None),
        P("fsdp", None),
        P("fsdp", "seq", None),
    )
    out_specs = (
        P("fsdp", "seq", None),
        P("fsdp", "seq", None),
        P("fsdp"),
        P("fsdp", "seq"),
        P("fsdp", "seq"),
        P("fsdp"),
        P("fsdp", "seq"),
        P("fsdp", "seq"),
    )
    return jax.shard_map(body, mesh=mesh, in_specs=in_specs, out_specs=out_specs, check_vma=False)
```

```python
import math

import jax
import jax.numpy as jnp
import numpy as np
from jax import lax
from jax.experimental import pallas as pl
from jax.experimental.pallas import tpu as pltpu
from jax.sharding import PartitionSpec as P

HEADS = 12
HEAD_DIM = 64
LONGEST = 1344
SEQ = 4
LOCAL = 3
TOK = 384
HALF = 192
PACK = 1536
F32 = jnp.float32
BF16 = jnp.bfloat16
VMEM_LIMIT = 63 * 1024 * 1024


def mm(left, right):
    return jnp.dot(left, right, preferred_element_type=F32)


def mm_nt(left, right):
    return lax.dot_general(left, right, (((1,), (1,)), ((), ())), preferred_element_type=F32)


def mm_tn(left, right):
    return lax.dot_general(left, right, (((0,), (0,)), ((), ())), preferred_element_type=F32)


def iota(shape, dim):
    return lax.broadcasted_iota(jnp.int32, shape, dim)


def roll(x, shift):
    return pltpu.roll(x, shift, 1)


def low_lanes(rows):
    return iota((rows, 128), 1) < 64


def turned(x):
    lane = iota(x.shape, 1)
    first = (lane & 32) == 0
    return jnp.where(first, roll(x, 96), roll(x, 32))


def norm_parts(values):
    average = jnp.mean(values, axis=-1, keepdims=True)
    centred = values - average
    variance = jnp.mean(centred * centred, axis=-1, keepdims=True)
    scale = lax.rsqrt(variance + 1e-05)
    return centred * scale, scale


def doc_bounds(len_ref):
    first = len_ref[0]
    second = first + len_ref[1]
    third = second + len_ref[2]
    start = jnp.where(
        len_ref[0] == LONGEST,
        0,
        jnp.where(len_ref[1] == LONGEST, first, jnp.where(len_ref[2] == LONGEST, second, third)),
    )
    return first, second, third, start


def edge_order(start, transposed):
    stored = iota((2 * HALF, 2 * HALF), 1 if transposed else 0)
    edge = iota((2 * HALF, 2 * HALF), 0 if transposed else 1)
    source = stored + (HALF + start)
    source = jnp.where(source >= 2 * HALF, source - 2 * HALF, source)
    return jnp.where(edge == source, 1.0, 0.0).astype(BF16)


def short_mask(bounds):
    first, second, third, start = bounds

    def numbers(dim):
        row = iota((HALF, HALF), dim) + (HALF + start)
        row = jnp.where(row >= 2 * HALF, row - 2 * HALF, row)
        place = jnp.where(row >= HALF, row + (PACK - 2 * HALF), row)
        return (
            jnp.where(place >= first, 1, 0)
            + jnp.where(place >= second, 1, 0)
            + jnp.where(place >= third, 1, 0)
        )

    return numbers(0) == numbers(1)


def extra_lanes(base, column):
    lane = iota(base.shape, 1)
    rest = -column
    top = rest.astype(BF16).astype(F32)
    rest = rest - top
    middle = rest.astype(BF16).astype(F32)
    rest = rest - middle
    return jnp.where(
        lane < 64,
        base,
        jnp.where(lane == 64, top, jnp.where(lane == 65, middle, jnp.where(lane == 66, rest, 0.0))),
    )


def permute_edge(order, ref, head):
    edge = jnp.concatenate([ref[head, 0:HALF, :], ref[head, PACK - HALF : PACK, :]], axis=0)
    moved = mm(order, edge).astype(BF16)
    return moved[0:HALF], moved[HALF : 2 * HALF]


def pack_halves(top, bottom):
    return jnp.where(low_lanes(top.shape[0]), top, roll(bottom, 64))


def rope_rows(len_ref, inv_ref, block, cos_ref, sin_ref):
    rows = pl.ds(pl.multiple_of(block * TOK, TOK), TOK)
    place = iota((TOK, 128), 0) + block * TOK
    first = len_ref[0]
    second = first + len_ref[1]
    third = second + len_ref[2]
    starts = (
        jnp.where(iota((8, 128), 0) == 1, first, 0)
        + jnp.where(iota((8, 128), 0) == 2, second, 0)
        + jnp.where(iota((8, 128), 0) == 3, third, 0)
    )
    shift = starts.astype(F32) * inv_ref[...]
    shift_cos, shift_sin = jnp.cos(shift), jnp.sin(shift)

    def pick(table):
        return jnp.where(
            place >= third,
            table[3:4],
            jnp.where(place >= second, table[2:3], jnp.where(place >= first, table[1:2], table[0:1])),
        )

    back_cos, back_sin = pick(shift_cos), pick(shift_sin)
    cosine, sine = cos_ref[rows, :], sin_ref[rows, :]
    cos_ref[rows, :] = cosine * back_cos + sine * back_sin
    sine = sine * back_cos - cosine * back_sin
    sin_ref[rows, :] = jnp.where((iota((TOK, 128), 1) & 32) == 0, -sine, sine)


def project_block(block, hid_ref, w_ref, cos_ref, sin_ref, q_ref, k_ref, v_ref, xt_ref):
    rows = pl.ds(pl.multiple_of(block * TOK, TOK), TOK)
    xhat = norm_parts(hid_ref[block].astype(F32))[0].astype(BF16)
    xt_ref[block] = jnp.transpose(xhat)
    qkv = mm(xhat, w_ref[...])
    cosine, sine = cos_ref[rows, :], sin_ref[rows, :]
    lane = iota((TOK, 128), 1)
    low = lane < 64
    ones = jnp.where(lane < 67, 1.0, 0.0)
    for chunk in range(5):
        part = qkv[:, 128 * chunk : min(128 * chunk + 128, 576)]
        if chunk == 4:
            part = jnp.concatenate([part, part], axis=1)
        if chunk < 3:
            part = part * cosine + turned(part) * sine
        for odd in range(2):
            index = 2 * chunk + odd
            if index == 9:
                continue
            piece = roll(part, 64) if odd else part
            kind, head = index // 3, index % 3
            if kind == 0:
                q_ref[head, rows, :] = (jnp.where(low, piece, 0.0).astype(BF16).astype(F32) * 0.125).astype(BF16)
            elif kind == 1:
                k_ref[head, rows, :] = jnp.where(low, piece, ones).astype(BF16)
            else:
                v_ref[head, rows, :] = jnp.where(low, piece, ones).astype(BF16)


def attend_rows(head, rows, keys, mask, q_ref, k_ref, v_ref, o_ref):
    query = q_ref[head, rows, :]
    scores = mm_nt(query, k_ref[head, keys, :])
    if mask is not None:
        scores = jnp.where(mask, scores, -1e9)
    highest = jnp.max(scores, axis=1, keepdims=True)
    weights = jnp.exp(scores - highest).astype(BF16)
    mixed = mm(weights, v_ref[head, keys, :])
    total = mixed[:, 64:65]
    lane = iota(mixed.shape, 1)
    o_ref[head, rows, :] = jnp.where(lane < 64, mixed * (1.0 / total), 0.0).astype(BF16)
    q_ref[head, rows, :] = extra_lanes(query.astype(F32), highest + jnp.log(total)).astype(BF16)


def places():
    seq, fsdp = lax.axis_index("seq"), lax.axis_index("fsdp")
    return seq, fsdp, fsdp // 8, (fsdp // 2) % 4, fsdp % 2


def peer(axis, step):
    seq, fsdp, z, y, core = places()
    if axis == "x":
        return ((seq + step) % SEQ, fsdp)
    if axis == "y":
        return (seq, z * 8 + ((y + step) % 4) * 2 + core)
    if axis == "z":
        return (seq, ((z + step) % 4) * 8 + y * 2 + core)
    return (seq, fsdp + 1 - 2 * core)


def remote(source, target, send_sem, recv_sem, device):
    return pltpu.make_async_remote_copy(
        src_ref=source,
        dst_ref=target,
        send_sem=send_sem,
        recv_sem=recv_sem,
        device_id=device,
        device_id_type=pl.DeviceIdType.MESH,
    )


ALL_PEERS = [(axis, step) for axis in "xyz" for step in (1, 2, 3)] + [("c", 1)]


def greet():
    barrier = pltpu.get_barrier_semaphore()
    for axis, step in ALL_PEERS:
        pl.semaphore_signal(barrier, inc=1, device_id=peer(axis, step), device_id_type=pl.DeviceIdType.MESH)
    pl.semaphore_wait(barrier, len(ALL_PEERS))


class Gather:
    def __init__(self, shard, full, send, recv, index, first):
        _, _, z, y, core = places()
        self.send, self.recv, self.index = send, recv, index
        mine = full.at[z, y, core]
        if first == "y":
            second, at = "z", z

            def line(k, half):
                return full.at[k % 4, half, core]

        else:
            second, at = "y", y

            def line(k, half):
                return full.at[half, k % 4, core]

        whole, low, high = pl.ds(0, 4), pl.ds(0, 2), pl.ds(2, 2)

        def both(block, axis, step):
            return (block, block, axis, step)

        self.hops = (
            [(shard, mine, first, step) for step in (1, 2, 3)],
            [both(line(at, whole), second, step) for step in (1, 3)] + [both(line(at, whole), "c", 1)],
            [
                both(line(at + 3, low), second, 1),
                both(line(at + 1, high), second, 3),
                both(line(at + 3, whole), "c", 1),
                both(line(at + 1, whole), "c", 1),
            ],
            [both(line(at + 2, whole), "c", 1)],
        )
        self.local = pltpu.make_async_copy(shard, mine, send.at[index, 11])

    def copies(self, hop):
        base = (0, 3, 6, 10)[hop]
        return [
            remote(src, dst, self.send.at[self.index, base + n], self.recv.at[self.index, base + n], peer(axis, step))
            for n, (src, dst, axis, step) in enumerate(self.hops[hop])
        ]

    def start(self, hop):
        if hop == 0:
            self.local.start()
        for copy in self.copies(hop):
            copy.start()

    def arrive(self, hop):
        if hop == 0:
            self.local.wait()
        for copy in self.copies(hop):
            copy.wait_recv()

    def advance(self, hop):
        self.arrive(hop)
        self.start(hop + 1)

    def finish(self):
        for hop in range(4):
            for copy in self.copies(hop):
                copy.wait_send()


def backward_rows(head, rows, queries, mask, q_ref, k_ref, v_ref, d_ref, dk_ref, dv_ref):
    query, grad = q_ref[head, queries, :], d_ref[head, queries, :]
    key = k_ref[head, rows, :]
    shares = jnp.exp(mm_nt(key, query))
    if mask is not None:
        shares = jnp.where(mask, shares, 0.0)
    grad_scores = (shares * mm_nt(v_ref[head, rows, :], grad)).astype(BF16)
    dv_ref[head, rows, :] = mm(shares.astype(BF16), grad).astype(BF16)
    dk_ref[head, rows, :] = mm(grad_scores, query).astype(BF16)
    return mm_tn(grad_scores, key)


class Reduce:
    def __init__(self, part, bufs, send, recv, index, first):
        _, _, self.z, self.y, self.core = places()
        self.part = part
        self.acc, self.recv1, self.acc1, self.recv2 = bufs
        self.send, self.recv, self.index, self.first = send, recv, index, first
        second = "z" if first == "y" else "y"
        self.hops = [[(part.at[:, :, 1 - self.core], self.acc, "c", 1)], [], []]
        for step in (1, 2, 3):
            one = (self.y + step) % 4
            two = (self.z + step) % 4
            if first == "y":
                lines, rest = self.acc.at[:, one], two
            else:
                lines, rest = self.acc.at[two], one
            self.hops[1].append((lines, self.recv1.at[step - 1], first, step))
            self.hops[2].append((self.acc1.at[rest], self.recv2.at[step - 1], second, step))

    def copies(self, hop):
        base = (0, 1, 4)[hop]
        return [
            remote(src, dst, self.send.at[self.index, base + n], self.recv.at[self.index, base + n], peer(axis, step))
            for n, (src, dst, axis, step) in enumerate(self.hops[hop])
        ]

    def start(self, hop):
        for copy in self.copies(hop):
            copy.start()

    def arrive(self, hop):
        for copy in self.copies(hop):
            copy.wait_recv()
        if hop == 0:

            @pl.loop(0, 16)
            def _(index):
                z, y = index // 4, index % 4
                total = self.acc[z, y].astype(F32) + self.part[z, y, self.core].astype(F32)
                self.acc[z, y] = total.astype(BF16)

        elif hop == 1:

            @pl.loop(0, 4)
            def _(index):
                own = self.acc[index, self.y] if self.first == "y" else self.acc[self.z, index]
                total = own.astype(F32)
                for step in range(3):
                    total += self.recv1[step, index].astype(F32)
                self.acc1[index] = total.astype(BF16)

        else:
            total = self.acc1[self.z if self.first == "y" else self.y].astype(F32)
            for step in range(3):
                total += self.recv2[step].astype(F32)
            return total

    def advance(self, hop):
        self.arrive(hop)
        self.start(hop + 1)

    def finish(self, first=0):
        for hop in range(first, 3):
            self.sent(hop)

    def sent(self, hop):
        for copy in self.copies(hop):
            copy.wait_send()


def reduce_scratch(rows, width):
    return [
        pltpu.VMEM((4, 4, rows, width), BF16),
        pltpu.VMEM((3, 4, rows, width), BF16),
        pltpu.VMEM((4, rows, width), BF16),
        pltpu.VMEM((3, rows, width), BF16),
    ]


class Cross:
    def __init__(self, sources, targets, send, recv, index):
        self.list = [
            remote(src, dst, send.at[index, n], recv.at[index, n], peer("x", n + 1))
            for n, (src, dst) in enumerate(zip(sources, targets))
        ]

    def start(self):
        for copy in self.list:
            copy.start()

    def arrive(self):
        for copy in self.list:
            copy.wait_recv()

    def finish(self):
        for copy in self.list:
            copy.wait_send()


def column_block(value, start, width):
    total = value.shape[1]
    if start:
        value = roll(value, total - start)
    return value[:, :width]


def own_columns(value, rank):
    total = value.shape[1]
    lane = iota((value.shape[0], 640), 1)
    result = jnp.zeros((value.shape[0], 640), F32)
    for kind in range(3):
        shift = (total - 768 * kind - HALF * rank + HALF * kind) % total
        moved = roll(value, shift) if shift else value
        result = jnp.where((lane >= HALF * kind) & (lane < HALF * kind + HALF), moved[:, :640], result)
    return result[:, :576]


def to_column(row):
    count = row.shape[1]
    diagonal = iota((count, count), 0) == iota((count, count), 1)
    return jnp.sum(jnp.where(diagonal, jnp.broadcast_to(row, (count, count)), 0.0), axis=1, keepdims=True)


def to_row(column):
    count = column.shape[0]
    diagonal = iota((count, count), 0) == iota((count, count), 1)
    return jnp.sum(jnp.where(diagonal, jnp.broadcast_to(column, (count, count)), 0.0), axis=0, keepdims=True)


def lay_pairs(full, target):
    for pair in range(16):
        z, y = pair // 4, pair % 4
        rows = jnp.concatenate([full[z, y, 0].astype(F32), full[z, y, 1].astype(F32)], axis=0)
        target[48 * pair : 48 * pair + 48, :] = rows.astype(BF16)


def layer_kernel(
    len_ref, inv_ref, cos_in, sin_in, hid_in, cot_ref, gain1_ref, gain2_ref, wq_ref, wi_ref, out_ref, down_ref,
    res_ref, in_ref, gq_out, go_out, gi_out, gd_out, gain1_out, gain2_out, one_full,
    oraw_ref, own_ref, two_ref, one_ref, cos_ref, sin_ref, hid_ref, own_full, w_ref, xt_ref,
    q_ref, k_ref, v_ref, o_ref, stage_ref, mix_ref,
    two_full, out_full, down_full, wi_full, wo_full, wd_full,
    attn_ref, x_ref, act_ref, gp_ref, wide_ref,
    g_ref, d_ref, dq_ref, dk_ref, dv_ref, acc_ref, gstage_ref, got_ref, m_ref,
    xi_ref, xo_ref, xd_ref, xg_ref, xm_ref, ri_ref, ro_ref, rd_ref, rg_ref, rm_ref,
    gather_send, gather_recv, hid_send, hid_recv, mix_send, mix_recv, local_sem,
    red_send, red_recv, x_send, x_recv,
    *bufs,
):
    seq, fsdp, _, _, _ = places()
    bounds = doc_bounds(len_ref)
    right, left = (seq + 1) % SEQ, (seq + 3) % SEQ
    ff = wi_ref.shape[1] // 2
    low = low_lanes(HALF)
    tables = (
        pltpu.make_async_copy(cos_in, cos_ref, local_sem.at[0]),
        pltpu.make_async_copy(sin_in, sin_ref, local_sem.at[1]),
    )
    for copy in tables:
        copy.start()
    gain1 = to_column(gain1_ref[...].astype(F32))
    gain2 = to_column(gain2_ref[...].astype(F32))
    raw = wq_ref[...].astype(F32)
    for rank in range(SEQ):

        @pl.when(seq == rank)
        def _(rank=rank):
            oraw_ref[...] = own_columns(raw, rank)

    own_ref[...] = (oraw_ref[...] * gain1).astype(BF16)
    one_ref[...] = (raw * gain1).astype(BF16)
    two_ref[...] = (wi_ref[...].astype(F32) * gain2).astype(BF16)
    greet()
    own = Gather(own_ref, own_full, gather_send, gather_recv, 0, "y")
    def half(shard, full, column, index, first):
        lanes = pl.ds(1152 * column, 1152)
        return Gather(
            shard.at[:, lanes], full.at[:, :, :, :, lanes], gather_send, gather_recv, index, first
        )

    two, two_more = half(two_ref, two_full, 0, 1, "y"), half(two_ref, two_full, 1, 5, "z")
    out = Gather(out_ref, out_full, gather_send, gather_recv, 2, "y")
    down = Gather(down_ref, down_full, gather_send, gather_recv, 3, "z")
    ones = (half(one_ref, one_full, 0, 4, "y"), half(one_ref, one_full, 1, 6, "z"))
    early_weights = (out, two, two_more, down)
    own.start(0)
    to_right = remote(hid_in, hid_ref.at[seq], hid_send.at[0], hid_recv.at[0], peer("x", 1))
    to_left = remote(hid_in, hid_ref.at[seq], hid_send.at[1], hid_recv.at[1], peer("x", 3))
    to_right.start()
    to_left.start()
    hid_ref[seq] = hid_in[...]
    for weight in early_weights:
        weight.start(0)
    for copy in tables:
        copy.wait()
    own.advance(0)
    for block in range(SEQ):
        rope_rows(len_ref, inv_ref, block, cos_ref, sin_ref)
    own.advance(1)
    for weight in early_weights:
        weight.advance(0)
    own.advance(2)
    own.arrive(3)
    lay_pairs(own_full, w_ref)

    def project(block):
        project_block(block, hid_ref, w_ref, cos_ref, sin_ref, q_ref, k_ref, v_ref, xt_ref)

    project(seq)
    to_right.wait_recv()
    on_right = remote(
        hid_ref.at[left, pl.ds(0, HALF)], hid_ref.at[left, pl.ds(0, HALF)],
        hid_send.at[2], hid_recv.at[2], peer("x", 1),
    )
    on_right.start()
    to_left.wait_recv()
    on_left = remote(
        hid_ref.at[right, pl.ds(HALF, HALF)], hid_ref.at[right, pl.ds(HALF, HALF)],
        hid_send.at[3], hid_recv.at[3], peer("x", 3),
    )
    on_left.start()
    project(left)
    project(right)
    on_right.wait_recv()
    on_left.wait_recv()
    project((seq + 2) % SEQ)

    order = edge_order(bounds[3], False)
    back = edge_order(bounds[3], True)
    for ref in (q_ref, k_ref, v_ref):
        for head in range(LOCAL):
            short, long = permute_edge(order, ref, head)
            ref[head, 0:HALF, :] = short
            ref[head, PACK - HALF : PACK, :] = long

    def attend(block):
        rows = pl.ds(pl.multiple_of(block * HALF, HALF), HALF)
        for head in range(LOCAL):
            attend_rows(head, rows, pl.ds(HALF, PACK - HALF), None, q_ref, k_ref, v_ref, o_ref)

    def mix_copy(dest):
        return remote(stage_ref.at[dest], mix_ref.at[seq], mix_send.at[dest], mix_recv.at[seq], (dest, fsdp))

    def give(dest, head, top, bottom):
        stage_ref[dest, head] = pack_halves(top.astype(F32), bottom.astype(F32)).astype(BF16)

    def hand_over(dest):
        @pl.when(seq != dest)
        def _():
            mix_copy(dest).start()

    def inner_dest(dest):
        pl.loop(2 * dest, 2 * dest + 2)(attend)
        for head in range(LOCAL):
            first = TOK * dest
            give(dest, head, o_ref[head, first : first + HALF, :], o_ref[head, first + HALF : first + TOK, :])
        hand_over(dest)

    inner_dest(1)
    for weight in early_weights:
        weight.advance(1)
    inner_dest(2)
    for weight in early_weights:
        weight.advance(2)
    for one in ones:
        one.start(0)
    mask = short_mask(bounds)
    for head in range(LOCAL):
        attend_rows(head, pl.ds(0, HALF), pl.ds(0, HALF), mask, q_ref, k_ref, v_ref, o_ref)

    @pl.loop(0, 3)
    def _(index):
        attend(1 + 5 * jnp.minimum(index, 1) + jnp.maximum(index - 1, 0))

    for head in range(LOCAL):
        top, bottom = permute_edge(back, o_ref, head)
        give(0, head, top, o_ref[head, HALF:TOK, :])
        give(3, head, o_ref[head, 3 * TOK : 3 * TOK + HALF, :], bottom)
    hand_over(0)
    hand_over(3)
    mix_ref[seq] = stage_ref[seq]
    for one in ones:
        one.advance(0)
    out.arrive(3)
    lay_pairs(out_full, wo_full)
    two.arrive(3)
    two_more.arrive(3)
    lay_pairs(two_full, wi_full)
    for step in (1, 2, 3):
        source = (seq + step) % SEQ
        remote(stage_ref.at[0], mix_ref.at[source], mix_send.at[0], mix_recv.at[source], peer("x", step)).wait_recv()
    for dest in range(SEQ):
        @pl.when(seq != dest)
        def _(dest=dest):
            mix_copy(dest).wait_send()

    for chunk in range(6):
        pair = []
        for index in (2 * chunk, 2 * chunk + 1):
            pair.append(mix_ref[index // 3, index % 3].astype(F32))
        first, second = pair
        lanes = slice(128 * chunk, 128 * chunk + 128)
        attn_ref[0:HALF, lanes] = pack_halves(first, second).astype(BF16)
        attn_ref[HALF:TOK, lanes] = jnp.where(low, roll(first, 64), second).astype(BF16)
    residual = hid_in[...].astype(F32) + mm(attn_ref[...], wo_full[...])
    xhat, scale = norm_parts(residual)
    x_ref[...] = xhat.astype(BF16)
    down.arrive(3)
    part = down_full.shape[3]
    for group in range(8):
        shards = [down_full[k // 8, k // 2 % 4, k % 2].astype(F32) for k in range(4 * group, 4 * group + 4)]
        wd_full[4 * part * group : 4 * part * (group + 1), :] = jnp.concatenate(shards, axis=0).astype(BF16)
    step = 384
    output = residual
    branch = cot_ref[...]
    for chunk in range(ff // step):
        lanes = slice(step * chunk, step * chunk + step)
        upper = slice(ff + step * chunk, ff + step * chunk + step)
        inner = mm(x_ref[...], wi_full[:, lanes])
        gate = mm(x_ref[...], wi_full[:, upper])
        phi = 0.5 * (1.0 + lax.erf(inner * math.sqrt(0.5)))
        gelu = inner * phi
        act = (gelu * gate).astype(BF16)
        act_ref[:, lanes] = act
        output = output + mm(act, wd_full[lanes, :])
        grad_act = mm_nt(branch, wd_full[lanes, :])
        density = jnp.exp(inner * inner * -0.5) * (1.0 / math.sqrt(2.0 * math.pi))
        gp_ref[:, lanes] = (grad_act * gate * (phi + inner * density)).astype(BF16)
        gp_ref[:, upper] = (grad_act * gelu).astype(BF16)
    res_ref[...] = output.astype(BF16)
    for one in ones:
        one.advance(1)
    for item in (own, *early_weights):
        item.finish()
    red_in = Reduce(two_full, bufs[0:4], red_send, red_recv, 0, "y")
    red_out = Reduce(out_full, bufs[4:8], red_send, red_recv, 1, "z")
    red_down = Reduce(down_full, bufs[8:12], red_send, red_recv, 2, "z")
    red_own = Reduce(m_ref, bufs[12:16], red_send, red_recv, 3, "y")
    early = (red_down, red_in, red_out)
    for column in range(2):
        lanes = slice(step * column, step * column + step)
        for chunk in range(ff // step):
            rows = slice(step * chunk, step * chunk + step)
            wide_ref[rows, :] = mm_tn(act_ref[:, rows], branch[:, lanes])
        for owner in range(32):
            down_full[owner // 8, owner // 2 % 4, owner % 2, :, lanes] = wide_ref[
                part * owner : part * owner + part, :
            ].astype(BF16)
    red_down.start(0)
    grad = mm_nt(gp_ref[...], wi_full[...])
    grad = scale * (
        grad
        - jnp.mean(grad, axis=-1, keepdims=True)
        - xhat * jnp.mean(grad * xhat, axis=-1, keepdims=True)
    )
    grad_res = branch.astype(F32) + grad
    in_ref[...] = grad_res
    grad_attn = grad_res.astype(BF16)
    grad_mix = mm_nt(grad_attn, wo_full[...]).astype(BF16).astype(F32)
    for chunk in range(6):
        lanes = slice(128 * chunk, 128 * chunk + 128)
        top, bottom = grad_mix[0:HALF, lanes], grad_mix[HALF:TOK, lanes]
        first = pack_halves(top, bottom)
        second = jnp.where(low, roll(top, 64), bottom)
        stage_ref[2 * chunk // 3, 2 * chunk % 3] = first.astype(BF16)
        stage_ref[(2 * chunk + 1) // 3, (2 * chunk + 1) % 3] = second.astype(BF16)

    def by_rank(ref):
        return [ref.at[(seq + step) % SEQ] for step in (1, 2, 3)]

    def by_step(ref):
        return [ref.at[step] for step in range(3)]

    gmixes = []
    for head in range(LOCAL):
        sources = [stage_ref.at[(seq + hop) % SEQ, head] for hop in (1, 2, 3)]
        gmixes.append(Cross(sources, [g_ref.at[seq, head]] * 3, x_send, x_recv, (0, 10, 11)[head]))
        gmixes[head].start()
    g_ref[seq] = stage_ref[seq]

    def lay(ref, lanes, value):
        for owner in range(32):
            ref[owner // 8, owner // 2 % 4, owner % 2, :, lanes] = value[24 * owner : 24 * owner + 24].astype(BF16)

    for chunk in range(2 * ff // step):
        lanes = slice(step * chunk, step * chunk + step)
        lay(two_full, lanes, mm_tn(x_ref[...], gp_ref[:, lanes]))
    red_in.start(0)
    for chunk in range(768 // step):
        lanes = slice(step * chunk, step * chunk + step)
        lay(out_full, lanes, mm_tn(attn_ref[...], grad_attn[:, lanes]))
    red_out.start(0)
    for copy in (to_right, to_left, on_right, on_left):
        copy.wait_send()

    def prepare(head):
        gmixes[head].arrive()
        for source in range(SEQ):
            packed = g_ref[source, head].astype(F32)
            d_ref[head, TOK * source : TOK * source + HALF, :] = jnp.where(low, packed, 0.0).astype(BF16)
            d_ref[head, TOK * source + HALF : TOK * source + TOK, :] = jnp.where(
                low, roll(packed, 64), 0.0
            ).astype(BF16)
        short, long = permute_edge(order, d_ref, head)
        d_ref[head, 0:HALF, :] = short
        d_ref[head, PACK - HALF : PACK, :] = long

        @pl.loop(0, SEQ)
        def _(block):
            rows = pl.ds(pl.multiple_of(block * TOK, TOK), TOK)
            grad = d_ref[head, rows, :].astype(F32)
            inner = jnp.sum(grad * o_ref[head, rows, :].astype(F32), axis=1, keepdims=True)
            d_ref[head, rows, :] = extra_lanes(grad, inner).astype(BF16)

    step_rows = 224

    def attend_back(head):
        acc_ref[0:HALF, :] = backward_rows(
            head, pl.ds(0, HALF), pl.ds(0, HALF), mask, q_ref, k_ref, v_ref, d_ref, dk_ref, dv_ref
        )
        acc_ref[HALF:PACK, :] = jnp.zeros((LONGEST, 128), F32)

        @pl.loop(0, LONGEST // (2 * step_rows))
        def _(block):
            terms = []
            for part in range(2):
                start = HALF + block * (2 * step_rows) + part * step_rows
                rows = pl.ds(pl.multiple_of(start, 32), step_rows)
                terms.append(
                    backward_rows(
                        head, rows, pl.ds(HALF, LONGEST), None, q_ref, k_ref, v_ref, d_ref, dk_ref, dv_ref
                    )
                )
            acc_ref[HALF:PACK, :] += terms[0] + terms[1]

        dq_ref[head] = (acc_ref[...] * 0.125).astype(BF16)
        for ref in (dq_ref, dk_ref, dv_ref):
            top, bottom = permute_edge(back, ref, head)
            ref[head, 0:HALF, :] = top
            ref[head, PACK - HALF : PACK, :] = bottom

        @pl.loop(0, SEQ)
        def _(dest):
            top = pl.ds(pl.multiple_of(dest * TOK, TOK), HALF)
            bottom = pl.ds(pl.multiple_of(dest * TOK + HALF, HALF), HALF)
            cosine = pack_halves(cos_ref[top, :], cos_ref[bottom, :])
            sine = pack_halves(sin_ref[top, :], sin_ref[bottom, :])
            for kind, ref in enumerate((dq_ref, dk_ref, dv_ref)):
                packed = pack_halves(ref[head, top, :].astype(F32), ref[head, bottom, :].astype(F32))
                if kind < 2:
                    packed = packed * cosine - turned(packed) * sine
                gstage_ref[dest, head, kind] = packed.astype(BF16)

        got_ref[seq, head] = gstage_ref[seq, head]
        sources = [gstage_ref.at[(seq + step) % SEQ, head] for step in (1, 2, 3)]
        cross = Cross(sources, [got_ref.at[seq, head]] * 3, x_send, x_recv, 1 + head)
        cross.start()
        return cross

    prepare(0)
    for red in early:
        red.advance(0)
    crosses = [attend_back(0)]
    for one in ones:
        one.advance(2)
    prepare(1)
    crosses.append(attend_back(1))
    for one in ones:
        one.arrive(3)
        one.finish()
    red_in.sent(0)
    one_copy = pltpu.make_async_copy(one_full, two_full, local_sem.at[2])
    one_copy.start()
    for red in early:
        red.advance(1)
    prepare(2)
    crosses.append(attend_back(2))
    for dest in range(SEQ):
        for chunk in range(5):
            lanes = slice(128 * chunk, 128 * chunk + 128)
            index = 2 * chunk
            first = gstage_ref[dest, index % 3, index // 3].astype(F32)
            index = min(index + 1, 8)
            second = gstage_ref[dest, index % 3, index // 3].astype(F32)
            hid_ref[dest, 0:HALF, lanes] = pack_halves(first, second).astype(BF16)
            hid_ref[dest, HALF:TOK, lanes] = jnp.where(low, roll(first, 64), second).astype(BF16)
    total = mm(xt_ref[0], hid_ref[0, :, 0:640])
    for block in range(1, SEQ):
        total += mm(xt_ref[block], hid_ref[block, :, 0:640])
    for owner in range(32):
        m_ref[owner // 8, owner // 2 % 4, owner % 2] = total[24 * owner : 24 * owner + 24, :576].astype(BF16)
    red_own.start(0)

    rows_in = red_in.arrive(2)
    rows_out = red_out.arrive(2)
    rows_down = red_down.arrive(2)

    def share(value, ref, width):
        for dest in range(SEQ):
            ref[dest] = column_block(value, width * dest, width).astype(BF16)

    share(rows_in, xi_ref, ff // 2)
    share(rows_out, xo_ref, HALF)
    share(rows_down, xd_ref, HALF)
    gain = jnp.sum(rows_in * wi_ref[...].astype(F32), axis=1, keepdims=True)
    xg_ref[0] = jnp.broadcast_to(gain, (24, 128))
    late = [
        Cross(by_rank(xi_ref), by_step(ri_ref), x_send, x_recv, 4),
        Cross(by_rank(xo_ref), by_step(ro_ref), x_send, x_recv, 5),
        Cross(by_rank(xd_ref), by_step(rd_ref), x_send, x_recv, 6),
        Cross([xg_ref.at[0]] * 3, by_step(rg_ref.at[0]), x_send, x_recv, 7),
    ]
    for cross in late:
        cross.start()

    one_copy.wait()
    lay_pairs(two_full, wi_full)
    red_own.advance(0)

    for cross in late:
        cross.arrive()

    def collect(own, ref):
        return own.astype(F32) + ref[0].astype(F32) + ref[1].astype(F32) + ref[2].astype(F32)

    gi_out[...] = collect(xi_ref[seq], ri_ref) * gain2
    go_out[...] = collect(xo_ref[seq], ro_ref)
    gd_out[...] = collect(xd_ref[seq], rd_ref)
    gain2_out[...] = to_row(collect(xg_ref[0], rg_ref.at[0])[:, 0:1])

    for cross in crosses:
        cross.arrive()
    red_own.advance(1)
    for chunk in range(18):
        pair = []
        for index in (2 * chunk, 2 * chunk + 1):
            kind, head = index // HEADS, index % HEADS
            pair.append(got_ref[head // 3, head % 3, kind].astype(F32))
        first, second = pair
        lanes = slice(128 * chunk, 128 * chunk + 128)
        gp_ref[0:HALF, lanes] = pack_halves(first, second).astype(BF16)
        gp_ref[HALF:TOK, lanes] = jnp.where(low, roll(first, 64), second).astype(BF16)
    rows_own = red_own.arrive(2)
    gain = jnp.sum(rows_own * oraw_ref[...], axis=1, keepdims=True)
    xg_ref[1] = jnp.broadcast_to(gain, (24, 128))
    wide = jnp.concatenate([rows_own, jnp.zeros((24, 64), F32)], axis=1)
    for kind in range(3):
        moved = column_block(wide, HALF * kind, 256)
        xm_ref[kind] = jnp.where(iota((24, 256), 1) < HALF, moved, 0.0).astype(BF16)
    rm_ref[seq] = xm_ref[...]
    last = [
        Cross([xm_ref] * 3, [rm_ref.at[seq]] * 3, x_send, x_recv, 8),
        Cross([xg_ref.at[1]] * 3, by_step(rg_ref.at[1]), x_send, x_recv, 9),
    ]
    for cross in last:
        cross.start()
    grad = mm_nt(gp_ref[...], wi_full[...])
    xhat, scale = norm_parts(hid_in[...].astype(F32))
    grad = scale * (
        grad
        - jnp.mean(grad, axis=-1, keepdims=True)
        - xhat * jnp.mean(grad * xhat, axis=-1, keepdims=True)
    )
    in_ref[...] += grad
    for cross in last:
        cross.arrive()
    spread = jnp.zeros((24, 640), F32)
    for place in range(3):
        index = 3 * seq + place
        piece = rm_ref[index % 4, index // 4].astype(F32) * gain1
        piece = jnp.concatenate([piece, jnp.zeros((24, 384), F32)], axis=1)
        spread += roll(piece, HALF * place) if place else piece
    gq_out[...] = spread[:, :576]
    gain1_out[...] = to_row(collect(xg_ref[1], rg_ref.at[1])[:, 0:1])
    red_in.finish(1)
    for item in (red_down, red_out, red_own, *gmixes, *crosses, *late, *last):
        item.finish()


SMEM = pl.BlockSpec(memory_space=pltpu.SMEM)
VMEM = pl.BlockSpec(memory_space=pltpu.VMEM)
ANY = pl.BlockSpec(memory_space=pl.ANY)


def shape(*dims, dtype=BF16):
    return jax.ShapeDtypeStruct(dims, dtype)


def body(hidden, lengths, attn_gain, w_qkv, w_attn_out, mlp_gain, w_in, w_mlp_out, cotangent):
    inverse = 160000.0 ** (np.arange(128) % 32 * (-2.0 / HEAD_DIM))
    angles = np.arange(PACK)[:, None] * inverse[None, :]
    cosine, sine = np.cos(angles).astype(np.float32), np.sin(angles).astype(np.float32)
    inverse = np.broadcast_to(inverse, (8, 128)).astype(np.float32)
    part = w_mlp_out.shape[0]
    ff = part * 32

    def low(*dims):
        return pltpu.VMEM(dims, BF16)

    def wide(*dims):
        return pltpu.VMEM(dims, F32)

    def dma(*dims):
        return pltpu.SemaphoreType.DMA(dims)

    heads = low(LOCAL, PACK, 128)
    packed = low(SEQ, LOCAL, HALF, 128)
    grads = low(SEQ, LOCAL, 3, HALF, 128)
    output, input_grad, grad_qkv, grad_out, grad_in, grad_down, gain_one, gain_two, _ = pl.pallas_call(
        layer_kernel,
        out_shape=(
            shape(TOK, 768),
            shape(TOK, 768, dtype=F32),
            shape(24, 576, dtype=F32),
            shape(24, HALF, dtype=F32),
            shape(24, ff // 2, dtype=F32),
            shape(part, HALF, dtype=F32),
            shape(1, 24, dtype=F32),
            shape(1, 24, dtype=F32),
            shape(4, 4, 2, 24, 2304),
        ),
        in_specs=[SMEM, VMEM, ANY, ANY] + [VMEM] * 6 + [ANY] * 2,
        out_specs=(VMEM,) * 8 + (ANY,),
        scratch_shapes=[
            wide(24, 576), low(24, 576), low(24, 2 * ff), low(24, 2304),
            wide(PACK, 128), wide(PACK, 128),
            low(SEQ, TOK, 768), low(4, 4, 2, 24, 576), low(768, 576), low(SEQ, 768, TOK),
            heads, heads, heads, heads, packed, packed,
            low(4, 4, 2, 24, 2 * ff), low(4, 4, 2, 24, 768), low(4, 4, 2, part, 768),
            low(768, 2 * ff), low(768, 768), low(ff, 768),
            low(TOK, 768), low(TOK, 768), low(TOK, ff), low(TOK, 2 * ff), wide(ff, 384),
            packed, heads, heads, heads, heads, wide(PACK, 128), grads, grads, low(4, 4, 2, 24, 576),
            low(SEQ, 24, ff // 2), low(SEQ, 24, HALF), low(SEQ, part, HALF), wide(2, 24, 128), low(3, 24, 256),
            low(3, 24, ff // 2), low(3, 24, HALF), low(3, part, HALF), wide(2, 3, 24, 128), low(SEQ, 3, 24, 256),
            dma(7, 12), dma(7, 11), dma(4), dma(4), dma(4), dma(4), dma(3),
            dma(4, 7), dma(4, 7), dma(12, 3), dma(12, 3),
            *reduce_scratch(24, 2 * ff),
            *reduce_scratch(24, 768),
            *reduce_scratch(part, 768),
            *reduce_scratch(24, 576),
        ],
        compiler_params=pltpu.CompilerParams(
            vmem_limit_bytes=VMEM_LIMIT, collective_id=1, has_side_effects=True
        ),
        name="layer",
    )(
        lengths[0], inverse, cosine, sine, hidden[0], cotangent[0],
        attn_gain[None], mlp_gain[None], w_qkv, w_in, w_attn_out, w_mlp_out,
    )
    return (
        output[None],
        input_grad[None],
        gain_one[0],
        grad_qkv,
        grad_out,
        gain_two[0],
        grad_in,
        grad_down,
    )


def solution(mesh):
    in_specs = (
        P("fsdp", "seq", None),
        P("fsdp", None),
        P("fsdp"),
        P("fsdp", None),
        P("fsdp", None),
        P("fsdp"),
        P("fsdp", None),
        P("fsdp", None),
        P("fsdp", "seq", None),
    )
    out_specs = (
        P("fsdp", "seq", None),
        P("fsdp", "seq", None),
        P("fsdp"),
        P("fsdp", "seq"),
        P("fsdp", "seq"),
        P("fsdp"),
        P("fsdp", "seq"),
        P("fsdp", "seq"),
    )
    return jax.shard_map(body, mesh=mesh, in_specs=in_specs, out_specs=out_specs, check_vma=False)
```
